32 devices in a mesh: dp: 4 (over y, core), rep: 4 (over z), head: 2 (over x).
Axes of the slice: x: 2, y: 2, z: 4, core: 2. Of those that a mesh axis runs over, the one named last changes fastest.
Arguments:
- hidden: bfloat16 [16384, 768], P(('dp', 'rep')), may hold values from -6 to 6
- source_index: int32 [16, 1024], P(('dp', 'rep')), may hold values from 0 to 1023, each once within a row
- crop_lengths: int32 [16, 5], P(('dp', 'rep')), may hold values from 1 to 256, 1024 in all within a row
- deleted: int32 [16, 1024], P(('dp', 'rep')), may hold values 0 or 1
- qkv_weight: bfloat16 [768, 2304], P(None, 'head'), may hold values from -0.21875 to 0.21875
- qv_bias: float32 [2, 768], P('head'), may hold values from -3 to 3
- out_weight: bfloat16 [768, 768], P('head'), may hold values from -0.875 to 0.875
- out_bias: float32 [768], replicated, may hold values from -3 to 3
- attn_gain: float32 [768], replicated, may hold values from 0.25 to 1.75
- attn_shift: float32 [768], replicated, may hold values from -3 to 3
- up_weight: bfloat16 [768, 3072], P(None, 'head'), may hold values from -0.21875 to 0.21875
- up_bias: float32 [2, 1536], P('head'), may hold values from -3 to 3
- down_weight: bfloat16 [3072, 768], P('head'), may hold values from -0.109375 to 0.109375
- down_bias: float32 [768], replicated, may hold values from -3 to 3
- ffn_gain: float32 [768], replicated, may hold values from 0.25 to 1.75
- ffn_shift: float32 [768], replicated, may hold values from -3 to 3
- cotangent: bfloat16 [16384, 768], P(('dp', 'rep', 'head')), may hold values from -6 to 6
Outputs:
- output: bfloat16 [16384, 768], P(('dp', 'rep', 'head'))
- pooled: float32 [80, 768], P(('dp', 'rep'))
- grad_hidden: float32 [16384, 768], P(('dp', 'rep', 'head'))
- grad_qkv_weight: float32 [768, 2304], P(('dp', 'rep'), 'head')
- grad_qv_bias: float32 [2, 768], P('head', ('dp', 'rep'))
- grad_out_weight: float32 [768, 768], P('head', ('dp', 'rep'))
- grad_out_bias: float32 [768], P(('dp', 'rep', 'head'))
- grad_attn_gain: float32 [768], P(('dp', 'rep', 'head'))
- grad_attn_shift: float32 [768], P(('dp', 'rep', 'head'))
- grad_up_weight: float32 [768, 3072], P(('dp', 'rep'), 'head')
- grad_up_bias: float32 [2, 1536], P('head', ('dp', 'rep'))
- grad_down_weight: float32 [3072, 768], P('head', ('dp', 'rep'))
- grad_down_bias: float32 [768], P(('dp', 'rep', 'head'))
- grad_ffn_gain: float32 [768], P(('dp', 'rep', 'head'))
- grad_ffn_shift: float32 [768], P(('dp', 'rep', 'head'))
The draws below stay inside these ranges and needn't reach their ends.
Inputs may be any that keep to these rules, and one draw needn't show every extreme that they name: Each packed row of source_index names every position of 0 to 1023 once. `crop_lengths`: the lengths of one packed row sum to 1024.
All inputs are finite; a program needn't handle non-finite values. No bound on the sum of `deleted` on one device may be relied on, other than what follows from the above.
Results may differ from the reference program's by a relative error of at most 0.018.
Values may be sent and summed in bfloat16 or wider, within the bound.
No kernel may reach another device: no remote copies, remote signals or barrier semaphores. Data moves between devices by JAX's collectives and lax.ppermute only.
A program may use at most 192 MiB of HBM per device.

```python
import math
import jax
import jax.numpy as jnp
import numpy as np
from jax import lax

D = 768
FF = 3072
HEADS = 12
HEAD_DIM = 64
ROW_LEN = 1024
CROP_MAX = 256
CROPS = 5
GROUP_W = 384
FF_DEV = 1536
ROWS = 16
TOKENS = 16384
CROPS_ALL = 80
N_HEAD = 2


def place_ends(array, rng, smallest, top_value):
    longest = array.shape.index(max(array.shape))
    spots = []
    for shift in (0, 1):
        where = [jax.random.randint(jax.random.fold_in(rng, axis), (), 0, length) for axis, length in enumerate(array.shape)]
        where[longest] = (where[longest] + shift) % array.shape[longest]
        spots.append(tuple(where))
    return array.at[spots[0]].set(smallest).at[spots[1]].set(top_value)


def shard_levels(rng, shape, pieces, low, largest):
    factor_of, own = 1.0, jax.random.fold_in(rng, 6)
    for position, shards_of in pieces:
        steps = jnp.exp(jax.random.uniform(jax.random.fold_in(own, position), (shards_of,), jnp.float32, low / len(pieces), largest / len(pieces)))
        factor_of = factor_of * jnp.repeat(steps, shape[position] // shards_of).reshape([-1 if axis == position else 1 for axis in range(len(shape))])
    return factor_of


def split_up(number_of, total, reach, lean):
    portions = [(1 << 20) // math.isqrt(standing ** lean) + 1 for standing in range(2, number_of + 1)]
    surplus, holding = total - reach - (number_of - 1), [1] * (number_of - 1)
    while surplus > 0:
        candidates = [i for i in range(number_of - 1) if holding[i] < reach]
        whole, remaining = sum([portions[i] for i in candidates]), surplus
        for i in candidates:
            more = min(reach - holding[i], max(1, remaining * portions[i] // whole), surplus)
            holding[i] = holding[i] + more
            surplus = surplus - more
    return np.array([reach] + holding)


def ragged_sizes(key, count, total, reach, slope):
    if count == 2:
        one = jax.random.randint(key, (), max(1, total - reach), min(reach, total - 1) + 1)
        return jnp.stack([one, total - one])
    tallies = jnp.asarray(split_up(count, total, reach, slope), jnp.int32)
    couples = (count - 1) // 2
    source_of, taker = tallies[1:1 + 2 * couples:2], tallies[2:2 + 2 * couples:2]
    room = jnp.minimum(source_of - 1, reach - taker)
    moved = jax.random.randint(jax.random.fold_in(key, 1), (couples,), 0, 1 << 20) % (room + 1)
    tallies = tallies.at[1:1 + 2 * couples:2].set(source_of - moved).at[2:2 + 2 * couples:2].set(taker + moved)
    return tallies[jax.random.permutation(jax.random.fold_in(key, 2), count)]


def normal_values(stream_key, extent, width, most, cuts=(), kind=jnp.bfloat16):
    loudness = shard_levels(stream_key, extent, cuts, -0.22, 0.18) if cuts else 1.0
    entries = jax.random.normal(stream_key, extent, jnp.float32) * width * loudness
    return jnp.minimum(jnp.maximum(entries, -most), most).astype(kind)


def setup_inputs(seed: int = 0) -> dict:
    key_of = jax.random.split(jax.random.key(seed), 18)
    return {
        "hidden": normal_values(key_of[0], (TOKENS, D), 1.0, 6.0, ((0, 16),)),
        "source_index": jax.vmap(lambda own: jax.random.permutation(own, ROW_LEN))(jax.random.split(key_of[1], ROWS)).reshape((ROWS, ROW_LEN)).astype(jnp.int32),
        "crop_lengths": jax.vmap(lambda own: ragged_sizes(own, CROPS, ROW_LEN, CROP_MAX, 1))(jax.random.split(key_of[2], ROWS)).reshape((ROWS, CROPS)).astype(jnp.int32),
        "deleted": place_ends((jax.random.randint(key_of[3], (ROWS, ROW_LEN), 0, 10) < 1).astype(jnp.int32), jax.random.fold_in(key_of[3], 1), 0, 1),
        "qkv_weight": normal_values(key_of[4], (D, 3 * D), D ** -0.5, 0.21875, ((1, 2),)),
        "qv_bias": normal_values(key_of[5], (N_HEAD, 2 * GROUP_W), 0.5, 3.0, ((0, 2),), jnp.float32),
        "out_weight": normal_values(key_of[6], (D, D), (D // 16) ** -0.5, 0.875, ((0, 2),)),
        "out_bias": normal_values(key_of[7], (D,), 0.5, 3.0, (), jnp.float32),
        "attn_gain": jnp.clip(1.0 + 0.15 * jax.random.normal(key_of[8], (D,), jnp.float32), 0.25, 1.75),
        "attn_shift": normal_values(key_of[9], (D,), 0.5, 3.0, (), jnp.float32),
        "up_weight": normal_values(key_of[10], (D, FF), D ** -0.5, 0.21875, ((1, 2),)),
        "up_bias": normal_values(key_of[11], (N_HEAD, FF_DEV), 0.5, 3.0, ((0, 2),), jnp.float32),
        "down_weight": normal_values(key_of[12], (FF, D), FF ** -0.5, 0.109375, ((0, 2),)),
        "down_bias": normal_values(key_of[13], (D,), 0.5, 3.0, (), jnp.float32),
        "ffn_gain": jnp.clip(1.0 + 0.15 * jax.random.normal(key_of[14], (D,), jnp.float32), 0.25, 1.75),
        "ffn_shift": normal_values(key_of[15], (D,), 0.5, 3.0, (), jnp.float32),
        "cotangent": normal_values(key_of[16], (TOKENS, D), 1.0, 6.0, ((0, 32),)),
    }


EPS = 1e-12
MASKED = -1e+30
PRECISE = lax.Precision.HIGHEST

@jax.custom_vjp
def low(v):
    return lax.optimization_barrier(v.astype(jnp.bfloat16)).astype(jnp.float32)

@jax.custom_vjp
def low_back(v):
    return v

def low_keep(v):
    return (low(v), None)

def low_pass(kept, grad):
    return (grad,)

def back_keep(v):
    return (v, None)

def back_low(kept, grad):
    return (low(grad),)
low.defvjp(low_keep, low_pass)
low_back.defvjp(back_keep, back_low)

def rounded(values):
    return low(low_back(values))

def layer_norm(values, gain, shift):
    center = values - lax.optimization_barrier(jnp.mean(values, axis=-1, keepdims=True))
    scaled = center * lax.rsqrt(lax.optimization_barrier(jnp.mean(center * center, axis=-1, keepdims=True)) + EPS)
    return scaled * gain + shift

def crop_numbers(lengths):
    ends = jnp.cumsum(lengths, axis=-1)
    places = jnp.arange(ROW_LEN, dtype=jnp.int32)
    return lax.optimization_barrier(jnp.sum((places[:, None] >= ends[None, :]).astype(jnp.int32), axis=-1))

def row_forward(params, source_rows, order, segment, kept, lengths):
    qkv_weight, qv_bias, out_weight, out_bias, attn_gain, attn_shift, up_weight, up_bias, down_weight, down_bias, ffn_gain, ffn_shift = params
    group_width = D // N_HEAD
    group_heads = HEADS // N_HEAD
    ff_group = FF // N_HEAD
    packed = source_rows[order]
    projected = jnp.dot(packed, qkv_weight, precision=PRECISE).reshape(ROW_LEN, N_HEAD, 3, group_width)
    biases = qv_bias.reshape(N_HEAD, 2, group_width)
    biases = jnp.stack([biases[:, 0], jnp.zeros_like(biases[:, 0]), biases[:, 1]], axis=1)
    projected = rounded(projected + biases[None])
    projected = projected.reshape(ROW_LEN, N_HEAD, 3, group_heads, HEAD_DIM)
    query = projected[:, :, 0]
    keys = projected[:, :, 1]
    values = projected[:, :, 2]
    logits = jnp.einsum('qgha,kgha->ghqk', query, keys, precision=PRECISE) * HEAD_DIM ** (-0.5)
    logits = low_back(logits)
    places = jnp.arange(ROW_LEN, dtype=jnp.int32)
    allowed = (segment[:, None] == segment[None, :]) & (kept[None, :] | (places[:, None] == places[None, :]))
    logits = jnp.where(allowed, logits, MASKED)
    peak = lax.optimization_barrier(jnp.max(logits, axis=-1, keepdims=True))
    scaled = jnp.exp(logits - peak)
    prob = low(scaled / lax.optimization_barrier(jnp.sum(scaled, axis=-1, keepdims=True)))
    mixed = jnp.einsum('ghqk,kgha->qgha', prob, values, precision=PRECISE)
    mixed = rounded(mixed.reshape(ROW_LEN, N_HEAD, group_width))
    parts = jnp.einsum('lgc,gcd->lgd', mixed, out_weight.reshape(N_HEAD, group_width, D), precision=PRECISE)
    attn_out = low_back(lax.optimization_barrier(jnp.sum(low(parts), axis=1)))
    normed1 = layer_norm(packed + attn_out + out_bias, attn_gain, attn_shift)
    normed_low = low(normed1)
    up_pre = jnp.dot(normed_low, up_weight, precision=PRECISE) + up_bias.reshape(FF)
    up_pre = low_back(up_pre)
    act = low(jax.nn.gelu(up_pre, approximate=False))
    parts = jnp.einsum('lgf,gfd->lgd', act.reshape(ROW_LEN, N_HEAD, ff_group), down_weight.reshape(N_HEAD, ff_group, D), precision=PRECISE)
    ffn_out = low_back(lax.optimization_barrier(jnp.sum(low(parts), axis=1)))
    result = layer_norm(normed1 + ffn_out + down_bias, ffn_gain, ffn_shift)
    member = (jnp.arange(CROPS, dtype=jnp.int32)[:, None] == segment[None, :]) & kept[None, :]
    crop_sums = jnp.dot(member.astype(jnp.float32), result, precision=PRECISE)
    pooled_row = crop_sums / lengths.astype(jnp.float32)[:, None]
    return (result, pooled_row)

def reference(hidden, source_index, crop_lengths, deleted, qkv_weight, qv_bias, out_weight, out_bias, attn_gain, attn_shift, up_weight, up_bias, down_weight, down_bias, ffn_gain, ffn_shift, cotangent):
    params = tuple((tensor.astype(jnp.float32) for tensor in (qkv_weight, qv_bias, out_weight, out_bias, attn_gain, attn_shift, up_weight, up_bias, down_weight, down_bias, ffn_gain, ffn_shift)))
    source = hidden.astype(jnp.float32).reshape(ROWS, ROW_LEN, D)
    upstream = cotangent.astype(jnp.float32).reshape(ROWS, ROW_LEN, D)

    def one_row(totals, items):
        source_rows, order, lengths, dropped, grad_rows = items
        segment = crop_numbers(lengths)
        kept = dropped == 0

        def forward(weights_all, rows_in):
            return row_forward(weights_all, rows_in, order, segment, kept, lengths)
        (result, pooled_row), pull = jax.vjp(forward, params, source_rows)
        grad_params, grad_source = pull((grad_rows, jnp.zeros((CROPS, D), jnp.float32)))
        totals = jax.tree.map(jnp.add, totals, grad_params)
        return (totals, (result.astype(jnp.bfloat16), pooled_row, grad_source))
    zeros = tuple((jnp.zeros_like(tensor) for tensor in params))
    totals, (outputs, pooled, grad_source) = lax.scan(one_row, zeros, (source, source_index, crop_lengths, deleted, upstream))
    return (outputs.reshape(TOKENS, D), pooled.reshape(CROPS_ALL, D), grad_source.reshape(TOKENS, D), totals[0], totals[1], totals[2], totals[3], totals[4], totals[5], totals[6], totals[7], totals[8], totals[9], totals[10], totals[11])
```

```python
import functools
import math

import jax
import jax.numpy as jnp
import numpy as np
from jax import lax
from jax.experimental import pallas as pl
from jax.experimental.pallas import tpu as pltpu
from jax.sharding import PartitionSpec as P

HEAD_DIM = 64
CROP_MAX = 256
EPS = 1e-12
MASKED = -1e30
NN = ((1,), (0,))
NT = ((1,), (1,))
f32 = jnp.float32
bf16 = jnp.bfloat16
i32 = jnp.int32
VMEM_LIMIT = 60 * 1024 * 1024
QB = 256


def dot(left, right, how):
    return lax.dot_general(left, right, (how, ((), ())), preferred_element_type=f32)


def params(**kw):
    return pltpu.CompilerParams(vmem_limit_bytes=VMEM_LIMIT, **kw)


def cost(flops, moved):
    return pl.CostEstimate(flops=int(flops), bytes_accessed=int(moved), transcendentals=0)


def full(shape):
    return pl.BlockSpec(shape, lambda *_: (0,) * len(shape))


def gelu_pair(u):
    t = 1.0 / (1.0 + (0.3275911 / math.sqrt(2.0)) * jnp.abs(u))
    bell = jnp.exp(-0.5 * (u * u))
    poly = t * (
        0.127414796 + t * (-0.142248368 + t * (0.7107068705 + t * (-0.7265760135 + t * 0.5307027145)))
    )
    tail = poly * bell
    phi = jnp.where(u < 0, tail, 1.0 - tail)
    return u * phi, phi + u * bell * (1.0 / math.sqrt(2.0 * math.pi))


def prep_kernel(
    lens, hidden, idx, dele, w, bias, packed, q, k, v, kt, vt, segrow, code, pool
):
    length, width = hidden.shape
    group = q.shape[1]
    crops = lens.shape[1]
    idx_col = jnp.transpose(jnp.broadcast_to(idx[...].astype(f32), (8, length)))[:, :1]
    lane = lax.broadcasted_iota(i32, (8, length), 1)
    seg = jnp.zeros((8, length), f32)
    end = jnp.int32(0)
    for c in range(crops):
        end = end + lens[0, c]
        seg = seg + jnp.where(lane >= end, 1.0, 0.0)
    segrow[...] = seg
    kept = jnp.broadcast_to(dele[...], (8, length)) == 0
    code_row = jnp.where(kept, seg, -1.0)
    code[...] = jnp.broadcast_to(jnp.transpose(code_row)[:, :1], code.shape)
    crop_row = lax.broadcasted_iota(i32, pool.shape, 0).astype(f32)
    pool[...] = jnp.where(
        crop_row == jnp.broadcast_to(code_row[:1], pool.shape), 1.0, 0.0
    ).astype(bf16)
    for i in range(length // QB):
        rows = slice(i * QB, (i + 1) * QB)
        place = lax.broadcasted_iota(i32, (QB, length), 1).astype(f32)
        onehot = jnp.where(idx_col[rows] == place, 1.0, 0.0).astype(bf16)
        pk = dot(onehot, hidden[...], NN).astype(bf16)
        packed[rows, :] = pk
        out = (dot(pk, w[...], NN) + bias[...]).astype(bf16)
        q[rows, :] = out[:, :group] * jnp.asarray(HEAD_DIM**-0.5, bf16)
        k[rows, :] = out[:, group : 2 * group]
        v[rows, :] = out[:, 2 * group :]
        kt[:, rows] = jnp.transpose(out[:, group : 2 * group])
        vt[:, rows] = jnp.transpose(out[:, 2 * group :])


def prepare(lens, hidden, idx, dele, w, bias):
    length, width = hidden.shape
    group = w.shape[1] // 3
    shape = jax.ShapeDtypeStruct
    vm = pl.BlockSpec(memory_space=pltpu.VMEM)
    return pl.pallas_call(
        prep_kernel,
        in_specs=[pl.BlockSpec(memory_space=pltpu.SMEM)] + [vm] * 5,
        out_specs=[vm] * 9,
        out_shape=[
            shape((length, width), bf16),
            shape((length, group), bf16),
            shape((length, group), bf16),
            shape((length, group), bf16),
            shape((group, length), bf16),
            shape((group, length), bf16),
            shape((8, length), f32),
            shape((length, 128), f32),
            shape((16, length), bf16),
        ],
        compiler_params=params(),
        cost_estimate=cost(2 * length * width * (length + 3 * group), 9e6),
        name="prepare",
    )(lens, hidden, idx, dele, w, bias)


def half_blocks(p):
    half = 2 * QB
    return (
        (pl.multiple_of(QB * p, QB), pl.multiple_of(half * p, QB), 2 * QB, 0, pl.multiple_of(QB * p, QB)),
        (pl.multiple_of(QB - QB * p, QB), pl.multiple_of(QB * p, QB), 3 * QB, 2 * QB, 0),
    )


def attend_kernel(own, sc, q, k, vt, segrow, code, e, mixed, recip, cap):
    p = sc[0] if own else sc[1]
    blocks = half_blocks(p)

    @pl.when(pl.program_id(0) == 0)
    def _():
        for qs, ks, count, off, _ in blocks:
            first = pl.multiple_of(2 * QB * p + qs, QB)
            keys = code[pl.ds(ks, count), :]
            keys = jnp.concatenate([keys] * (QB // 128), axis=1)
            ask = segrow[0:1, pl.ds(first, QB)]
            shift = lax.broadcasted_iota(i32, (count, QB), 0) - lax.broadcasted_iota(
                i32, (count, QB), 1
            )
            allowed = (keys == ask) | (shift == first - ks)
            cap[off : off + count, :] = jnp.where(allowed, 3e38, MASKED)

    lane = lax.broadcasted_iota(i32, (QB, 128), 1)
    for qs, ks, count, off, _ in blocks:
        q_blk = q[pl.ds(qs, QB), :]
        k_win = k[pl.ds(ks, count), :]
        outs, recips = [], []
        for a in range(2):
            q_one = jnp.where((lane < HEAD_DIM) == (a == 0), q_blk, jnp.zeros_like(q_blk))
            s = jnp.minimum(dot(k_win, q_one, NT), cap[off : off + count, :])
            peak = jnp.max(s, axis=0, keepdims=True)
            weights = jnp.exp(s - peak).astype(bf16)
            e[0, a, off : off + count, :] = weights
            v_one = vt[a * HEAD_DIM : (a + 1) * HEAD_DIM, pl.ds(ks, count)]
            v_aug = jnp.concatenate([v_one, jnp.ones((16, count), bf16)], axis=0)
            o = dot(v_aug, weights, NN)
            inv = 1.0 / o[HEAD_DIM : HEAD_DIM + 1]
            outs.append(o[:HEAD_DIM] * inv)
            recips.append(jnp.broadcast_to(inv, (HEAD_DIM, QB)))
        mixed[pl.ds(qs, QB), :] = jnp.transpose(jnp.concatenate(outs, axis=0)).astype(bf16)
        recip[pl.ds(qs, QB), :] = jnp.transpose(jnp.concatenate(recips, axis=0))


def attend(own, sc, q, k, vt, segrow, code):
    length, group = q.shape
    half = length // 2
    pairs = group // 128
    side = 0 if own else 1
    shape = jax.ShapeDtypeStruct
    return pl.pallas_call(
        functools.partial(attend_kernel, own),
        grid_spec=pltpu.PrefetchScalarGridSpec(
            num_scalar_prefetch=1,
            grid=(pairs,),
            in_specs=[
                pl.BlockSpec((half, 128), lambda t, s: (s[side], t)),
                pl.BlockSpec((length, 128), lambda t, s: (0, t)),
                pl.BlockSpec((128, length), lambda t, s: (t, 0)),
                full((8, length)),
                full((length, 128)),
            ],
            out_specs=[
                pl.BlockSpec((1, 2, 5 * QB, QB), lambda t, s: (t, 0, 0, 0)),
                pl.BlockSpec((half, 128), lambda t, s: (0, t)),
                pl.BlockSpec((half, 128), lambda t, s: (0, t)),
            ],
            scratch_shapes=[pltpu.VMEM((5 * QB, QB), f32)],
        ),
        out_shape=[
            shape((pairs, 2, 5 * QB, QB), bf16),
            shape((half, group), bf16),
            shape((half, group), f32),
        ],
        compiler_params=params(),
        cost_estimate=cost(4e9, 6e6),
        name="attend_own" if own else "attend_other",
    )(sc, q, k, vt, segrow, code)


def attend_back_kernel(own, sc, g, o, recip, q, v, kt, e, dq, dk, dv):
    p = sc[0] if own else sc[1]
    lane = lax.broadcasted_iota(i32, (QB, 128), 1)
    pick = jnp.where(
        lax.broadcasted_iota(i32, (16, 128), 0)
        == lax.broadcasted_iota(i32, (16, 128), 1) // HEAD_DIM,
        1.0,
        0.0,
    ).astype(bf16)
    outer, inner = half_blocks(p)
    for number, (qs, ks, count, off, loc) in enumerate((inner, outer)):
        rows = pl.ds(qs, QB)
        grad = g[rows, :].astype(f32) * recip[rows, :]
        both = grad * o[rows, :].astype(f32)
        high = both.astype(bf16)
        rest = (both - high.astype(f32)).astype(bf16)
        delta = dot(pick, high, NT) + dot(pick, rest, NT)
        grad = grad.astype(bf16)
        q_blk = q[rows, :]
        v_win = v[pl.ds(ks, count), :]
        dk_sum = jnp.zeros((count, 128), f32)
        dv_sum = jnp.zeros((count, 128), f32)
        dqs = []
        for a in range(2):
            mine = (lane < HEAD_DIM) == (a == 0)
            g_one = jnp.where(mine, grad, jnp.zeros_like(grad))
            q_one = jnp.where(mine, q_blk, jnp.zeros_like(q_blk))
            weights = e[0, a, off : off + count, :]
            ds = (
                weights.astype(f32) * (dot(v_win, g_one, NT) - delta[a : a + 1])
            ).astype(bf16)
            dk_sum += dot(ds, q_one, NN)
            dv_sum += dot(weights, g_one, NN)
            dqs.append(dot(kt[a * HEAD_DIM : (a + 1) * HEAD_DIM, pl.ds(ks, count)], ds, NN))
        dq[rows, :] = (
            jnp.transpose(jnp.concatenate(dqs, axis=0)) * HEAD_DIM ** (-0.5)
        ).astype(bf16)
        if number == 0:
            dk[...] = dk_sum
            dv[...] = dv_sum
        else:
            dk[pl.ds(loc, count), :] += dk_sum
            dv[pl.ds(loc, count), :] += dv_sum


def attend_back(own, sc, g, o, recip, q, v, kt, e):
    length, group = q.shape
    half = length // 2
    pairs = group // 128
    side = 0 if own else 1
    shape = jax.ShapeDtypeStruct
    cols = pl.BlockSpec((half, 128), lambda t, s: (0, t))
    wide = pl.BlockSpec((3 * QB, 128), lambda t, s: (0, t))
    return pl.pallas_call(
        functools.partial(attend_back_kernel, own),
        grid_spec=pltpu.PrefetchScalarGridSpec(
            num_scalar_prefetch=1,
            grid=(pairs,),
            in_specs=[
                cols,
                cols,
                cols,
                pl.BlockSpec((half, 128), lambda t, s: (s[side], t)),
                pl.BlockSpec((length, 128), lambda t, s: (0, t)),
                pl.BlockSpec((128, length), lambda t, s: (t, 0)),
                pl.BlockSpec((1, 2, 5 * QB, QB), lambda t, s: (t, 0, 0, 0)),
            ],
            out_specs=[cols, wide, wide],
        ),
        out_shape=[
            shape((half, group), bf16),
            shape((3 * QB, group), f32),
            shape((3 * QB, group), f32),
        ],
        compiler_params=params(),
        cost_estimate=cost(8e9, 8e6),
        name="attend_back_own" if own else "attend_back_other",
    )(sc, g, o, recip, q, v, kt, e)


def middle_kernel(
    sc,
    lens,
    packed,
    mixed_own,
    mixed_other,
    cot,
    ow_own,
    out_bias,
    attn_gain,
    attn_shift,
    down_bias,
    ffn_gain,
    ffn_shift,
    up_bias,
    pool,
    up_own,
    dn_own,
    a0,
    a1,
    a2,
    a3,
    b0,
    b1,
    b2,
    b3,
    out,
    pooled,
    send,
    gm_own,
    g1b,
    g2b,
    n1b,
    smalls,
    act,
    gp,
    wup,
    wdn,
    ow_other,
    ub,
    slope,
    scaled1,
    normed1,
    sem_up,
    sem_dn,
    sem_ow,
    sem_ub,
):
    quarter = sc[2]
    blk = wup.shape[2]
    width = wup.shape[1]
    group = ow_own.shape[0]
    piece = group // 4
    parts = ((a0, b0), (a1, b1), (a2, b2), (a3, b3))
    ups, dns, ows, ubs = [], [], [], []
    for r, (a_ref, _) in enumerate(parts):
        place = quarter ^ r
        rows = pl.ds(pl.multiple_of(piece * place, 16), piece)
        for c in range(2):
            ows.append(
                pltpu.make_async_copy(
                    a_ref.at[pl.ds(width + c * piece, piece), :],
                    ow_other.at[rows, pl.ds(c * blk, blk)],
                    sem_ow.at[2 * r + c],
                )
            )
        ubs.append(
            pltpu.make_async_copy(
                a_ref.at[pl.ds(width + 2 * piece, 16), :], ub.at[place], sem_ub.at[r]
            )
        )
    for j in range(4):
        cols = pl.ds(j * blk, blk)
        ups.append(pltpu.make_async_copy(up_own.at[:, cols], wup.at[j], sem_up.at[j]))
        dns.append(pltpu.make_async_copy(dn_own.at[cols, :], wdn.at[j], sem_dn.at[j]))
    for r, (a_ref, b_ref) in enumerate(parts):
        place = 4 + (quarter ^ r)
        ups.append(
            pltpu.make_async_copy(a_ref.at[pl.ds(0, width), :], wup.at[place], sem_up.at[4 + r])
        )
        dns.append(pltpu.make_async_copy(b_ref, wdn.at[place], sem_dn.at[4 + r]))
    for copy in ows + ubs + ups + dns:
        copy.start()

    for copy in ows + ubs:
        copy.wait()
    resid = (
        packed[...].astype(f32)
        + dot(mixed_own[...], ow_own[...], NN)
        + dot(mixed_other[...], ow_other[...], NN)
        + out_bias[...]
    )
    center = resid - jnp.mean(resid, axis=-1, keepdims=True)
    inv1 = lax.rsqrt(jnp.mean(center * center, axis=-1, keepdims=True) + EPS)
    norm = center * inv1
    scaled1[...] = norm
    norm = norm * attn_gain[...] + attn_shift[...]
    normed1[...] = norm
    low = norm.astype(bf16)
    n1b[...] = low
    total = jnp.zeros(norm.shape, f32)
    for j in range(8):
        if j < 4:
            ups[j].wait()
            dns[j].wait()
        elif j == 4:
            for copy in ups[4:] + dns[4:]:
                copy.wait()
        here = (j // 4, slice(None), slice((j % 4) * blk, (j % 4 + 1) * blk))
        if j < 4:
            bias = up_bias[:, j * blk : (j + 1) * blk]
        else:
            three = ub[j - 4].astype(f32)
            bias = three[0:1] + three[1:2] + three[2:3]
        value, deriv = gelu_pair(dot(low, wup[j], NN) + bias)
        value = value.astype(bf16)
        act[here] = value
        slope[j] = deriv.astype(bf16)
        total = total + dot(value, wdn[j], NN)
    resid = normed1[...] + total + down_bias[...]
    center = resid - jnp.mean(resid, axis=-1, keepdims=True)
    inv2 = lax.rsqrt(jnp.mean(center * center, axis=-1, keepdims=True) + EPS)
    scaled2 = center * inv2
    result = scaled2 * ffn_gain[...] + ffn_shift[...]
    high = result.astype(bf16)
    out[...] = high
    rest = (result - high.astype(f32)).astype(bf16)
    sums = dot(pool[...], high, NN) + dot(pool[...], rest, NN)
    row = lax.broadcasted_iota(i32, (16, 1), 0)
    scale = jnp.zeros((16, 1), f32)
    for c in range(lens.shape[1]):
        scale = jnp.where(row == c, 1.0 / lens[0, c].astype(f32), scale)
    sums = sums * scale
    pooled[...] = sums
    tokens = n1b.shape[0]
    sums = sums.astype(bf16)
    send[tokens : tokens + 16, :] = sums[:, :group]
    send[tokens + 16 : tokens + 32, :] = sums[:, group:]

    grad = cot[...].astype(f32)
    smalls[4:5, :] = jnp.sum(grad * scaled2, axis=0, keepdims=True)
    smalls[5:6, :] = jnp.sum(grad, axis=0, keepdims=True)
    smalls[6:8, :] = jnp.zeros((2, smalls.shape[1]), f32)
    grad = grad * ffn_gain[...]
    grad_resid2 = inv2 * (
        grad
        - jnp.mean(grad, axis=-1, keepdims=True)
        - scaled2 * jnp.mean(grad * scaled2, axis=-1, keepdims=True)
    )
    smalls[3:4, :] = jnp.sum(grad_resid2, axis=0, keepdims=True)
    low = grad_resid2.astype(bf16)
    g2b[...] = low
    total = grad_resid2
    for j in range(8):
        here = (j // 4, slice(None), slice((j % 4) * blk, (j % 4 + 1) * blk))
        pre = (dot(low, wdn[j], NT) * slope[j].astype(f32)).astype(bf16)
        gp[here] = pre
        total = total + dot(pre, wup[j], NT)
    norm = scaled1[...]
    smalls[1:2, :] = jnp.sum(total * norm, axis=0, keepdims=True)
    smalls[2:3, :] = jnp.sum(total, axis=0, keepdims=True)
    grad = total * attn_gain[...]
    grad_resid1 = inv1 * (
        grad
        - jnp.mean(grad, axis=-1, keepdims=True)
        - norm * jnp.mean(grad * norm, axis=-1, keepdims=True)
    )
    smalls[0:1, :] = jnp.sum(grad_resid1, axis=0, keepdims=True)
    low = grad_resid1.astype(bf16)
    g1b[...] = low
    send[0:tokens, :] = dot(low, ow_other[...], NT).astype(bf16)
    gm_own[...] = dot(low, ow_own[...], NT).astype(bf16)


def middle(sc, lens, packed, mixed_own, mixed_other, cot, ow, vectors, up_bias, pool, up, dn, quads):
    half = packed.shape[0] // 2
    width = packed.shape[1]
    group = ow.shape[0]
    hid = up.shape[1]
    blk = hid // 4
    shape = jax.ShapeDtypeStruct
    anyspace = pl.BlockSpec(memory_space=pl.ANY)
    outs = [
        ((half, width), bf16),
        ((16, width), f32),
        ((half + 32, group), bf16),
        ((half, group), bf16),
        ((half, width), bf16),
        ((half, width), bf16),
        ((half, width), bf16),
        ((8, width), f32),
        ((2, half, hid), bf16),
        ((2, half, hid), bf16),
    ]
    return pl.pallas_call(
        middle_kernel,
        grid_spec=pltpu.PrefetchScalarGridSpec(
            num_scalar_prefetch=1,
            grid=(1,),
            in_specs=[
                pl.BlockSpec(memory_space=pltpu.SMEM),
                pl.BlockSpec((half, width), lambda t, s: (s[0], 0)),
                full((half, group)),
                full((half, group)),
                full((half, width)),
                full((group, width)),
            ]
            + [full((1, width))] * 6
            + [full((1, hid)), pl.BlockSpec((16, half), lambda t, s: (0, s[0]))]
            + [anyspace] * 10,
            out_specs=[full(s) for s, _ in outs],
            scratch_shapes=[
                pltpu.VMEM((8, width, blk), bf16),
                pltpu.VMEM((8, blk, width), bf16),
                pltpu.VMEM((group, width), bf16),
                pltpu.VMEM((4, 16, blk), bf16),
                pltpu.VMEM((8, half, blk), bf16),
                pltpu.VMEM((half, width), f32),
                pltpu.VMEM((half, width), f32),
                pltpu.SemaphoreType.DMA((8,)),
                pltpu.SemaphoreType.DMA((8,)),
                pltpu.SemaphoreType.DMA((8,)),
                pltpu.SemaphoreType.DMA((4,)),
            ],
        ),
        out_shape=[shape(s, d) for s, d in outs],
        compiler_params=params(),
        cost_estimate=cost(8 * half * width * 2 * hid + 8 * half * width * group, 25e6),
        name="middle",
    )(
        sc,
        lens,
        packed,
        mixed_own,
        mixed_other,
        cot,
        ow,
        *vectors,
        up_bias,
        pool,
        up,
        dn,
        *[a for a, _ in quads],
        *[b for _, b in quads],
    )


def order_matrix(sc, tabs, width, per):
    source = (tabs[:, 0:1] ^ sc[3]) * per + tabs[:, 1:2]
    feature = lax.broadcasted_iota(i32, (width, width), 1)
    return jnp.where(source == feature, 1.0, 0.0).astype(bf16)


def order_kernel(per, sc, tabs, packed, out):
    width = packed.shape[1]
    out[...] = dot(order_matrix(sc, tabs, width, per), packed[...], NT).astype(bf16)


def ordered(per, sc, tabs, packed):
    length, width = packed.shape
    return pl.pallas_call(
        functools.partial(order_kernel, per),
        grid_spec=pltpu.PrefetchScalarGridSpec(
            num_scalar_prefetch=1,
            grid=(1,),
            in_specs=[full(tabs.shape), full((length, width))],
            out_specs=full((width, length)),
        ),
        out_shape=jax.ShapeDtypeStruct((width, length), bf16),
        compiler_params=params(),
        cost_estimate=cost(2 * width * width * length, 3e6),
        name="ordered",
    )(sc, tabs, packed)


def down_grad_kernel(per, sc, tabs, g2b, act, keep, send, gt):
    width = g2b.shape[1]

    @pl.when((pl.program_id(0) == 0) & (pl.program_id(1) == 0))
    def _():
        gt[...] = dot(order_matrix(sc, tabs, width, per), g2b[...], NT).astype(bf16)

    grad = dot(gt[...], act[0], NN)
    keep[...] = grad[: width // 2].astype(bf16)
    send[...] = grad[width // 2 :].astype(bf16)


def down_grad(per, sc, tabs, g2b, act):
    half, width = g2b.shape
    hid = act.shape[2]
    blk = 512
    count = hid // blk
    shape = jax.ShapeDtypeStruct((width // 2, 2 * hid), bf16)
    spec = pl.BlockSpec((width // 2, blk), lambda i, j, s: (0, i * count + j))
    return pl.pallas_call(
        functools.partial(down_grad_kernel, per),
        grid_spec=pltpu.PrefetchScalarGridSpec(
            num_scalar_prefetch=1,
            grid=(2, count),
            in_specs=[
                full(tabs.shape),
                full((half, width)),
                pl.BlockSpec((1, half, blk), lambda i, j, s: (i, 0, j)),
            ],
            out_specs=[spec, spec],
            scratch_shapes=[pltpu.VMEM((width, half), bf16)],
        ),
        out_shape=[shape, shape],
        compiler_params=params(),
        cost_estimate=cost(4 * half * width * hid, 8e6),
        name="down_grad",
    )(sc, tabs, g2b, act)


def up_grad_kernel(
    per,
    pieces,
    sc,
    tabs,
    n1b,
    g1b,
    mixed_own,
    mixed_other,
    smalls,
    small_block,
    small_lane,
    bias_block,
    bias_lane,
    gp,
    keep,
    send,
    nt,
    gt,
    sums,
):
    side, step = pl.program_id(0), pl.program_id(1)
    width = n1b.shape[1]
    mid = width // 2
    blk = gp.shape[2]
    group = mixed_own.shape[1]

    @pl.when((side == 0) & (step == 0))
    def _():
        matrix = order_matrix(sc, tabs, width, per)
        nt[...] = dot(matrix, n1b[...], NT).astype(bf16)
        gt[...] = dot(matrix, g1b[...], NT).astype(bf16)

    @pl.when(step < 3)
    def _():
        grad = dot(nt[...], gp[0], NN)
        keep[0] = grad[:mid].astype(bf16)
        send[0] = grad[mid:].astype(bf16)
        sums[step] = jnp.broadcast_to(
            jnp.sum(gp[0].astype(f32), axis=0, keepdims=True), (8, blk)
        )

    @pl.when(step == 3)
    def _():
        mixed = jnp.where(side == 0, mixed_own[...], mixed_other[...])
        grad = dot(gt[...], mixed, NN).astype(bf16)
        keep[0, :, :group] = grad[:mid]
        send[0, :, :group] = grad[mid:]
        block = tabs[:, 0:1] ^ sc[3]
        off = tabs[:, 1:2]
        member = jnp.where(side == 0, sc[0], sc[1])
        pick = jnp.where(
            off == lax.broadcasted_iota(i32, (width, 8), 1), 1.0, 0.0
        ).astype(bf16)
        rows = dot(pick, smalls[...].astype(bf16), NN)
        rows = jnp.where(2 * block + member == small_block[...], rows, 0.0).astype(bf16)
        extra = dot(rows, small_lane[...], NN)
        key = jnp.where(off < pieces, pieces * block + off, -1)
        for j in range(3):
            cols = slice(j * blk, (j + 1) * blk)
            rows = jnp.where(key == bias_block[:, cols], sums[j][0:1], 0.0).astype(bf16)
            extra += dot(rows, bias_lane[cols, :], NN)
        extra = extra.astype(bf16)
        keep[0, :, group:] = extra[:mid]
        send[0, :, group:] = extra[mid:]


def up_grad(per, pieces, sc, tabs, n1b, g1b, mixed_own, mixed_other, smalls, tables, gp):
    half, width = n1b.shape
    hid = gp.shape[2]
    group = mixed_own.shape[1]
    blk = 512
    shape = jax.ShapeDtypeStruct((2, width // 2, hid + blk), bf16)
    spec = pl.BlockSpec((1, width // 2, blk), lambda i, j, s: (i, 0, j))
    return pl.pallas_call(
        functools.partial(up_grad_kernel, per, pieces),
        grid_spec=pltpu.PrefetchScalarGridSpec(
            num_scalar_prefetch=1,
            grid=(2, 4),
            in_specs=[
                full(tabs.shape),
                full((half, width)),
                full((half, width)),
                full((half, group)),
                full((half, group)),
                full((8, width)),
            ]
            + [full(t.shape) for t in tables]
            + [pl.BlockSpec((1, half, blk), lambda i, j, s: (i, 0, jnp.minimum(j, 2)))],
            out_specs=[spec, spec],
            scratch_shapes=[
                pltpu.VMEM((width, half), bf16),
                pltpu.VMEM((width, half), bf16),
                pltpu.VMEM((3, 8, blk), f32),
            ],
        ),
        out_shape=[shape, shape],
        compiler_params=params(),
        cost_estimate=cost(4 * half * width * (hid + blk), 10e6),
        name="up_grad",
    )(sc, tabs, n1b, g1b, mixed_own, mixed_other, smalls, *tables, gp)


def project_grad_kernel(
    sc, tabs, pt, dq_own, dq_other, dk_own, dk_other, dv_own, dv_other, qv_block, qv_lane,
    gq, keep, send, ksum, vsum,
):
    h = sc[0]
    width = pt.shape[0]
    mid = width // 2
    length, group = ksum.shape
    half = length // 2
    own = pl.ds(pl.multiple_of(half * h, half), half)
    other = pl.ds(pl.multiple_of(half - half * h, half), half)
    win_own = pl.ds(pl.multiple_of(QB * h, QB), 3 * QB)
    win_other = pl.ds(pl.multiple_of(QB - QB * h, QB), 3 * QB)
    gq[own, 0:group] = dq_own[...]
    gq[other, 0:group] = dq_other[...]
    for total, first, second, place in ((ksum, dk_own, dk_other, 1), (vsum, dv_own, dv_other, 2)):
        total[...] = jnp.zeros_like(total)
        total[win_own, :] = first[...]
        total[win_other, :] += second[...]
        gq[:, place * group : (place + 1) * group] = total[...].astype(bf16)
    grads = gq[...]
    grad = dot(pt[...], grads, NN).astype(bf16)
    keep[:, : 3 * group] = grad[:mid]
    send[:, : 3 * group] = grad[mid:]
    sums = jnp.sum(grads.astype(f32), axis=0, keepdims=True)
    sums = jnp.concatenate([sums[:, :group], sums[:, 2 * group :]], axis=1)
    key = jnp.where(tabs[:, 1:2] == 0, tabs[:, 0:1] ^ sc[3], -1)
    rows = jnp.where(key == qv_block[...], sums, 0.0).astype(bf16)
    extra = dot(rows, qv_lane[...], NN).astype(bf16)
    keep[:, 3 * group :] = extra[:mid]
    send[:, 3 * group :] = extra[mid:]


def project_grad(sc, tabs, pt, pieces, tables):
    width, length = pt.shape
    group = pieces[0].shape[1]
    shape = jax.ShapeDtypeStruct
    wide = (width // 2, 3 * group + 128)
    return pl.pallas_call(
        project_grad_kernel,
        grid_spec=pltpu.PrefetchScalarGridSpec(
            num_scalar_prefetch=1,
            grid=(1,),
            in_specs=[full(x.shape) for x in (tabs, pt, *pieces, *tables)],
            out_specs=[full((length, 3 * group)), full(wide), full(wide)],
            scratch_shapes=[pltpu.VMEM((length, group), f32)] * 2,
        ),
        out_shape=[shape((length, 3 * group), bf16), shape(wide, bf16), shape(wide, bf16)],
        compiler_params=params(),
        cost_estimate=cost(6 * length * width * group, 15e6),
        name="project_grad",
    )(sc, tabs, pt, *pieces, *tables)


def place_rows(idx, first, rows, grads):
    spot = lax.broadcasted_iota(i32, (rows, grads.shape[0]), 0) + first
    onehot = jnp.where(spot == idx[...], 1.0, 0.0).astype(bf16)
    return dot(onehot, grads, NN)


def input_grad_kernel(sc, idx, gq, w, g1b, terms, out):
    h = sc[0]
    half = g1b.shape[0]
    for i in range(2):
        mine = jnp.where(h == i, 1.0, 0.0)
        part = dot(gq[i * half : (i + 1) * half, :], w[...], NT)
        part = part + mine * g1b[...].astype(f32)
        terms[i * half : (i + 1) * half, :] = part.astype(bf16)
    out[...] = place_rows(idx, (1 - h) * half, half, terms[...]).astype(bf16)


def input_grad(sc, idx, gq, w, g1b):
    length = gq.shape[0]
    half, width = g1b.shape
    shape = jax.ShapeDtypeStruct
    return pl.pallas_call(
        input_grad_kernel,
        grid_spec=pltpu.PrefetchScalarGridSpec(
            num_scalar_prefetch=1,
            grid=(1,),
            in_specs=[full(x.shape) for x in (idx, gq, w, g1b)],
            out_specs=[full((length, width)), full((half, width))],
        ),
        out_shape=[shape((length, width), bf16), shape((half, width), bf16)],
        compiler_params=params(),
        cost_estimate=cost(2 * length * width * (gq.shape[1] + half), 8e6),
        name="input_grad",
    )(sc, idx, gq, w, g1b)


def own_rows_kernel(sc, idx, terms, out):
    half = out.shape[0]
    out[...] = place_rows(idx, sc[0] * half, half, terms[...])


def own_rows(sc, idx, terms):
    length, width = terms.shape
    half = length // 2
    return pl.pallas_call(
        own_rows_kernel,
        grid_spec=pltpu.PrefetchScalarGridSpec(
            num_scalar_prefetch=1,
            grid=(1,),
            in_specs=[full(idx.shape), full(terms.shape)],
            out_specs=full((half, width)),
        ),
        out_shape=jax.ShapeDtypeStruct((half, width), f32),
        compiler_params=params(),
        cost_estimate=cost(2 * length * width * half, 4e6),
        name="own_rows",
    )(sc, idx, terms)


def swap(value, axis, bit):
    count = lax.axis_size(axis)
    return lax.ppermute(value, axis, [(i, i ^ (1 << bit)) for i in range(count)])


def add_low(left, right):
    return (left.astype(f32) + right.astype(f32)).astype(bf16)


def halve(value, axis, bit):
    rows = value.shape[0] // 2
    return add_low(value[:rows], swap(value[rows:], axis, bit))


def halve_head(own, other):
    return own.astype(f32) + swap(other, "head", 0).astype(f32)


def body(
    hidden,
    source_index,
    crop_lengths,
    deleted,
    qkv_weight,
    qv_bias,
    out_weight,
    out_bias,
    attn_gain,
    attn_shift,
    up_weight,
    up_bias,
    down_weight,
    down_bias,
    ffn_gain,
    ffn_shift,
    cotangent,
):
    length, width = hidden.shape
    crops = crop_lengths.shape[1]
    group = out_weight.shape[0]
    hid = up_weight.shape[1]
    half = length // 2
    blk = hid // 4
    n_dp, n_rep = lax.axis_size("dp"), lax.axis_size("rep")
    dp_bits, rep_bits = n_dp.bit_length() - 1, n_rep.bit_length() - 1
    shards = n_dp * n_rep
    per = width // shards
    h, dp = lax.axis_index("head"), lax.axis_index("dp")
    me = dp * n_rep + lax.axis_index("rep")
    quarter = dp & 3
    sc = jnp.stack([h, 1 - h, quarter, me]).astype(i32)

    stages = [("dp", b) for b in range(dp_bits)] + [("rep", b) for b in range(rep_bits)]
    block = np.zeros(shards, np.int32)
    for number, (axis, bit) in enumerate(stages):
        value = (np.arange(shards) >> (len(stages) - 1 - number)) & 1
        block |= (value << (bit + (rep_bits if axis == "dp" else 0))).astype(np.int32)
    row = np.arange(width)
    tabs = np.zeros((width, 8), np.int32)
    tabs[:, 0] = block[row // per]
    tabs[:, 1] = row % per
    pieces = min(6, per)
    n_small = width // (2 * shards)
    n_bias = hid // (shards * pieces)
    n_qv = 2 * group // shards

    def lanes(count, each, start):
        table = np.zeros((count, 128), np.float32)
        table[np.arange(count), start + np.arange(count) % each] = 1.0
        return jnp.asarray(table, bf16)

    def blocks(count, each):
        return jnp.asarray((np.arange(count) // each)[None, :], i32)

    tabs = jnp.asarray(tabs)
    small_tables = (
        blocks(width, n_small),
        lanes(width, n_small, 0),
        blocks(hid, n_bias),
        lanes(hid, n_bias, 64),
    )
    qv_tables = (blocks(2 * group, n_qv), lanes(2 * group, n_qv, 0))

    bias_quarter = lax.dynamic_slice_in_dim(up_bias, quarter * blk, blk, 1)
    bias_high = bias_quarter.astype(bf16)
    bias_rest = bias_quarter - bias_high.astype(f32)
    bias_mid = bias_rest.astype(bf16)
    bias_low = (bias_rest - bias_mid.astype(f32)).astype(bf16)
    out_quarter = lax.dynamic_slice_in_dim(out_weight, quarter * (group // 4), group // 4, 0)
    first = jnp.concatenate(
        [
            lax.dynamic_slice_in_dim(up_weight, quarter * blk, blk, 1),
            out_quarter[:, :blk],
            out_quarter[:, blk:],
            bias_high,
            bias_mid,
            bias_low,
            jnp.zeros((13, blk), bf16),
        ],
        axis=0,
    )
    second = lax.dynamic_slice_in_dim(down_weight, quarter * blk, blk, 0)
    quads = []
    for value in (first, second):
        r0 = swap(value, "head", 0)
        r2 = swap(r0, "dp", 1)
        r1 = swap(r0, "dp", 0)
        r3 = swap(r2, "dp", 0)
        quads.append((r0, r1, r2, r3))
    quads = list(zip(*quads))

    zero_bias = jnp.zeros((1, group), f32)
    bias_row = jnp.concatenate([qv_bias[:, :group], zero_bias, qv_bias[:, group:]], axis=1)
    packed, q, k, v, kt, vt, segrow, code, pool = prepare(
        crop_lengths, hidden, source_index, deleted, qkv_weight, bias_row
    )
    e_other, o_other, recip_other = attend(False, sc, q, k, vt, segrow, code)
    mixed_recv = swap(o_other, "head", 0)
    e_own, o_own, recip_own = attend(True, sc, q, k, vt, segrow, code)
    vectors = [
        x.reshape(1, width)
        for x in (out_bias, attn_gain, attn_shift, down_bias, ffn_gain, ffn_shift)
    ]
    output, pooled, send, gm_own, g1b, g2b, n1b, smalls, act, gp = middle(
        sc, crop_lengths, packed, o_own, mixed_recv, cotangent, out_weight, vectors, up_bias, pool,
        up_weight, down_weight, quads,
    )
    recv = swap(send, "head", 0)
    dn_keep, dn_send = down_grad(per, sc, tabs, g2b, act)
    up_keep, up_send = up_grad(
        per, pieces, sc, tabs, n1b, g1b, o_own, mixed_recv, smalls, small_tables, gp
    )
    pt = ordered(per, sc, tabs, packed)
    dq_own, dk_own, dv_own = attend_back(True, sc, gm_own, o_own, recip_own, q, v, kt, e_own)
    dq_other, dk_other, dv_other = attend_back(
        False, sc, recv, o_other, recip_other, q, v, kt, e_other
    )
    gq, qkv_keep, qkv_send = project_grad(
        sc, tabs, pt, (dq_own, dq_other, dk_own, dk_other, dv_own, dv_other), qv_tables
    )
    terms, hidden_other = input_grad(sc, source_index, gq, qkv_weight, g1b)
    hidden_recv = swap(hidden_other, "head", 0)
    hidden_own = own_rows(sc, source_index, terms)
    grad_hidden = hidden_own + hidden_recv.astype(f32)

    down = add_low(dn_keep, swap(dn_send, "dp", 0))
    for axis, bit in stages[1:]:
        down = halve(down, axis, bit)
    down = halve_head(down[:, :hid], down[:, hid:])

    up = add_low(up_keep, swap(up_send, "dp", 0))
    up = halve_head(up[0], up[1]).astype(bf16)
    for axis, bit in stages[1:]:
        up = halve(up, axis, bit)
    up = up.astype(f32)

    qkv = add_low(qkv_keep, swap(qkv_send, "dp", 0))
    for axis, bit in stages[1:]:
        qkv = halve(qkv, axis, bit)
    qkv = qkv.astype(f32)

    extra = up[:, hid + group :]
    small = [extra[i, :n_small] for i in range(6)]
    pooled_other = recv[half:].astype(f32)
    pooled_other = jnp.concatenate([pooled_other[:crops], pooled_other[16 : 16 + crops]], axis=1)
    return (
        output,
        pooled[:crops] + pooled_other,
        grad_hidden,
        qkv[:, : 3 * group],
        qkv[0:1, 3 * group : 3 * group + n_qv],
        up[:, hid : hid + group].T,
        small[0],
        small[1],
        small[2],
        up[:, :hid],
        extra[:pieces, 64 : 64 + n_bias].reshape(1, pieces * n_bias),
        down.T,
        small[3],
        small[4],
        small[5],
    )


def solution(mesh):
    rows = P(("dp", "rep"), None)
    every = P(("dp", "rep", "head"), None)
    vector = P(("dp", "rep", "head"))
    return jax.shard_map(
        body,
        mesh=mesh,
        in_specs=(
            rows,
            rows,
            rows,
            rows,
            P(None, "head"),
            P("head", None),
            P("head", None),
            P(),
            P(),
            P(),
            P(None, "head"),
            P("head", None),
            P("head", None),
            P(),
            P(),
            P(),
            every,
        ),
        out_specs=(
            every,
            rows,
            every,
            P(("dp", "rep"), "head"),
            P("head", ("dp", "rep")),
            P("head", ("dp", "rep")),
            vector,
            vector,
            vector,
            P(("dp", "rep"), "head"),
            P("head", ("dp", "rep")),
            P("head", ("dp", "rep")),
            vector,
            vector,
            vector,
        ),
        check_vma=False,
    )
```

```python
import functools
import math

import jax
import jax.numpy as jnp
import numpy as np
from jax import lax
from jax.experimental import pallas as pl
from jax.experimental.pallas import tpu as pltpu
from jax.sharding import PartitionSpec as P

HEAD_DIM = 64
CROP_MAX = 256
EPS = 1e-12
MASKED = -1e30
NN = ((1,), (0,))
NT = ((1,), (1,))
TN = ((0,), (0,))
f32 = jnp.float32
bf16 = jnp.bfloat16
i32 = jnp.int32
VMEM_LIMIT = 60 * 1024 * 1024
QB = CROP_MAX
HB = 512
SCALE = 0.4
ORDERED = 30

shape = jax.ShapeDtypeStruct
ANY = pl.BlockSpec(memory_space=pl.ANY)


def dot(left, right, how):
    return lax.dot_general(left, right, (how, ((), ())), preferred_element_type=f32)


def cost(micros):
    return pl.CostEstimate(
        flops=int(SCALE * micros * 1.1e9), bytes_accessed=1024, transcendentals=0
    )


def full(dims):
    return pl.BlockSpec(dims, lambda *_: (0,) * len(dims))


def call(kernel, name, micros, sc, args, in_specs, outs, out_specs, scratch):
    return pl.pallas_call(
        kernel,
        grid_spec=pltpu.PrefetchScalarGridSpec(
            num_scalar_prefetch=1,
            grid=(1,),
            in_specs=in_specs,
            out_specs=out_specs,
            scratch_shapes=scratch,
        ),
        out_shape=[shape(s, d) for s, d in outs],
        compiler_params=pltpu.CompilerParams(vmem_limit_bytes=VMEM_LIMIT),
        cost_estimate=cost(micros),
        name=name,
    )(sc, *args)


def onehot(hit):
    return jnp.where(hit, 1.0, 0.0).astype(bf16)


def gelu_pair(u):
    t = 1.0 / (1.0 + (0.3275911 / math.sqrt(2.0)) * jnp.abs(u))
    bell = jnp.exp(-0.5 * (u * u))
    poly = t * (
        0.127414796 + t * (-0.142248368 + t * (0.7107068705 + t * (-0.7265760135 + t * 0.5307027145)))
    )
    tail = poly * bell
    phi = jnp.where(u < 0, tail, 1.0 - tail)
    return u * phi, phi + u * bell * (1.0 / math.sqrt(2.0 * math.pi))


def order_matrix(sc, tabs, width, per):
    source = (tabs[0:1, :] ^ sc[3]) * per + tabs[1:2, :]
    return onehot(source == lax.broadcasted_iota(i32, (width, width), 0))


def bundle_kernel(sc, up_bias, up, dn, ow, first, second, sems):
    quarter = sc[2]
    width, blk = up.shape[0], second.shape[0]
    piece = ow.shape[0] // 4
    cols = pl.ds(pl.multiple_of(quarter * blk, 128), blk)
    slab = pl.ds(pl.multiple_of(quarter * piece, 16), piece)
    copies = [
        pltpu.make_async_copy(up.at[:, cols], first.at[pl.ds(0, width), :], sems.at[0]),
        pltpu.make_async_copy(
            ow.at[slab, pl.ds(0, blk)], first.at[pl.ds(width, piece), :], sems.at[1]
        ),
        pltpu.make_async_copy(
            ow.at[slab, pl.ds(blk, blk)], first.at[pl.ds(width + piece, piece), :], sems.at[2]
        ),
        pltpu.make_async_copy(
            dn.at[pl.ds(pl.multiple_of(quarter * blk, 16), blk), :], second, sems.at[3]
        ),
    ]
    for copy in copies:
        copy.start()
    bias = up_bias[0:1, cols]
    high = bias.astype(bf16).astype(f32)
    mid = (bias - high).astype(bf16).astype(f32)
    low = bias - high - mid
    first[width + 2 * piece :, :] = jnp.concatenate(
        [high, mid, low, jnp.zeros((13, blk), f32)], axis=0
    ).astype(bf16)
    for copy in copies:
        copy.wait()


def bundle(sc, up_bias, up, dn, ow):
    width, hid = up.shape
    blk = hid // 4
    rows = width + ow.shape[0] // 2 + 16
    return call(
        bundle_kernel, "bundle", 2, sc, (up_bias, up, dn, ow),
        [full(up_bias.shape), ANY, ANY, ANY],
        [((rows, blk), bf16), ((blk, width), bf16)],
        [full((rows, blk)), full((blk, width))],
        [pltpu.SemaphoreType.DMA((4,))],
    )


def half_blocks(p):
    half = 2 * QB
    return (
        (pl.multiple_of(QB * p, QB), pl.multiple_of(half * p, QB), 2 * QB, 0, pl.multiple_of(QB * p, QB)),
        (pl.multiple_of(QB - QB * p, QB), pl.multiple_of(QB * p, QB), 3 * QB, 2 * QB, 0),
    )


def fill_cap(p, segrow, code, cap):
    for qs, ks, count, off, _ in half_blocks(p):
        first = pl.multiple_of(2 * QB * p + qs, QB)
        keys = code[pl.ds(ks, count), :]
        keys = jnp.concatenate([keys] * (QB // 128), axis=1)
        ask = segrow[0:1, pl.ds(first, QB)]
        shift = lax.broadcasted_iota(i32, (count, QB), 0) - lax.broadcasted_iota(
            i32, (count, QB), 1
        )
        allowed = (keys == ask) | (shift == first - ks)
        cap[off : off + count, :] = jnp.where(allowed, 3e38, MASKED)


def attend_pair(p, base, t, q, k, v, cap, e, mixed, recip):
    lane = lax.broadcasted_iota(i32, (QB, 128), 1) < HEAD_DIM
    cols = slice(t * 128, (t + 1) * 128)
    for qs, ks, count, off, _ in half_blocks(p):
        q_blk = q[pl.ds(pl.multiple_of(base + qs, QB), QB), cols]
        k_win = k[pl.ds(ks, count), cols]
        v_win = v[pl.ds(ks, count), cols]
        v_lane = lax.broadcasted_iota(i32, (count, 128), 1) < HEAD_DIM
        outs, recips = [], []
        for a in range(2):
            q_one = jnp.where(lane == (a == 0), q_blk, jnp.zeros_like(q_blk))
            s = jnp.minimum(dot(k_win, q_one, NT), cap[off : off + count, :])
            weights = jnp.exp(s - jnp.max(s, axis=0, keepdims=True)).astype(bf16)
            e[t, a, off : off + count, :] = weights
            v_one = jnp.where(v_lane == (a == 0), v_win, jnp.ones_like(v_win))
            o = dot(v_one, weights, TN)
            value, total = o[:HEAD_DIM], o[HEAD_DIM:]
            if a == 1:
                value, total = total, value
            inv = 1.0 / total
            outs.append(value * inv)
            recips.append(inv)
        mixed[pl.ds(qs, QB), cols] = jnp.transpose(jnp.concatenate(outs, axis=0)).astype(bf16)
        recip[pl.ds(qs, QB), cols] = jnp.transpose(jnp.concatenate(recips, axis=0))


def prepare_kernel(
    sc, lens, hidden, idx, dele, w, qv_bias,
    packed_hbm, q_hbm, k_hbm, v_hbm, e_hbm, mixed, recip, segrow, code, pool,
    packed, q, k, v, e, cap, sems,
):
    length, width = hidden.shape
    group = q.shape[1]
    idx_col = jnp.transpose(jnp.broadcast_to(idx[...].astype(f32), (8, length)))[:, :1]
    lane = lax.broadcasted_iota(i32, (8, length), 1)
    seg = jnp.zeros((8, length), f32)
    end = jnp.int32(0)
    for c in range(lens.shape[1]):
        end = end + lens[0, c]
        seg = seg + jnp.where(lane >= end, 1.0, 0.0)
    segrow[...] = seg
    code_row = jnp.where(jnp.broadcast_to(dele[...], (8, length)) == 0, seg, -1.0)
    code[...] = jnp.broadcast_to(jnp.transpose(code_row)[:, :1], code.shape)
    crop_row = lax.broadcasted_iota(i32, pool.shape, 0).astype(f32)
    pool[...] = onehot(crop_row == jnp.broadcast_to(code_row[:1], pool.shape))
    copies = []
    for i in range(length // QB):
        rows = slice(i * QB, (i + 1) * QB)
        place = lax.broadcasted_iota(i32, (QB, length), 1).astype(f32)
        pk = dot(onehot(idx_col[rows] == place), hidden[...], NN).astype(bf16)
        packed[rows, :] = pk
        out = dot(pk, w[...], NN)
        q[rows, :] = (out[:, :group] + qv_bias[:, :group]).astype(bf16) * jnp.asarray(
            HEAD_DIM**-0.5, bf16
        )
        k[rows, :] = out[:, group : 2 * group].astype(bf16)
        v[rows, :] = (out[:, 2 * group :] + qv_bias[:, group:]).astype(bf16)
    for number, (source, target) in enumerate(
        ((packed, packed_hbm), (q, q_hbm), (k, k_hbm), (v, v_hbm))
    ):
        copies.append(pltpu.make_async_copy(source, target, sems.at[number]))
        copies[-1].start()
    p = sc[1]
    fill_cap(p, segrow, code, cap)
    for t in range(group // 128):
        attend_pair(p, 2 * QB * p, t, q, k, v, cap, e, mixed, recip)
        copies.append(pltpu.make_async_copy(e.at[t], e_hbm.at[t], sems.at[4 + t]))
        copies[-1].start()
    for copy in copies:
        copy.wait()


def prepare(sc, lens, hidden, idx, dele, w, qv_bias):
    length, width = hidden.shape
    group = w.shape[1] // 3
    half, pairs = length // 2, group // 128
    weights = (pairs, 2, 5 * QB, QB)
    return call(
        prepare_kernel, "prepare", 15, sc, (lens, hidden, idx, dele, w, qv_bias),
        [pl.BlockSpec(memory_space=pltpu.SMEM)]
        + [full(x.shape) for x in (hidden, idx, dele, w, qv_bias)],
        [
            ((length, width), bf16),
            ((length, group), bf16),
            ((length, group), bf16),
            ((length, group), bf16),
            (weights, bf16),
            ((half, group), bf16),
            ((half, group), f32),
            ((8, length), f32),
            ((length, 128), f32),
            ((16, length), bf16),
        ],
        [ANY] * 5
        + [full((half, group)), full((half, group)), full((8, length)), full((length, 128)),
           full((16, length))],
        [
            pltpu.VMEM((length, width), bf16),
            pltpu.VMEM((length, group), bf16),
            pltpu.VMEM((length, group), bf16),
            pltpu.VMEM((length, group), bf16),
            pltpu.VMEM(weights, bf16),
            pltpu.VMEM((5 * QB, QB), f32),
            pltpu.SemaphoreType.DMA((4 + pairs,)),
        ],
    )


def attend_kernel(sc, q, k, v, segrow, code, e_hbm, mixed, recip, e, cap, sems):
    p = sc[0]
    fill_cap(p, segrow, code, cap)
    copies = []
    for t in range(q.shape[1] // 128):
        attend_pair(p, 0, t, q, k, v, cap, e, mixed, recip)
        copies.append(pltpu.make_async_copy(e.at[t], e_hbm.at[t], sems.at[t]))
        copies[-1].start()
    for copy in copies:
        copy.wait()


def attend(sc, q, k, v, segrow, code):
    length, group = q.shape
    half, pairs = length // 2, group // 128
    weights = (pairs, 2, 5 * QB, QB)
    return call(
        attend_kernel, "attend", 9, sc, (q, k, v, segrow, code),
        [pl.BlockSpec((half, group), lambda t, s: (s[0], 0))]
        + [full(x.shape) for x in (k, v, segrow, code)],
        [(weights, bf16), ((half, group), bf16), ((half, group), f32)],
        [ANY, full((half, group)), full((half, group))],
        [
            pltpu.VMEM(weights, bf16),
            pltpu.VMEM((5 * QB, QB), f32),
            pltpu.SemaphoreType.DMA((pairs,)),
        ],
    )


def back_pair(p, t, g, o, recip, q, k, v, e, put_dq, put_kv):
    lane = lax.broadcasted_iota(i32, (QB, 128), 1) < HEAD_DIM
    cols = slice(t * 128, (t + 1) * 128)
    pick = onehot(
        (lax.broadcasted_iota(i32, (16, 128), 1) < HEAD_DIM)
        == (lax.broadcasted_iota(i32, (16, 128), 0) == 0)
    )
    outer, inner = half_blocks(p)
    for number, (qs, ks, count, off, loc) in enumerate((inner, outer)):
        rows = pl.ds(qs, QB)
        grad = g[rows, cols].astype(f32) * recip[rows, cols]
        both = grad * o[rows, cols].astype(f32)
        high = both.astype(bf16)
        rest = (both - high.astype(f32)).astype(bf16)
        delta = dot(pick, high, NT) + dot(pick, rest, NT)
        grad = grad.astype(bf16)
        q_blk = q[rows, cols]
        k_win = k[pl.ds(ks, count), cols]
        v_win = v[pl.ds(ks, count), cols]
        dk = jnp.zeros((count, 128), f32)
        dv = jnp.zeros((count, 128), f32)
        dqs = []
        for a in range(2):
            g_one = jnp.where(lane == (a == 0), grad, jnp.zeros_like(grad))
            q_one = jnp.where(lane == (a == 0), q_blk, jnp.zeros_like(q_blk))
            weights = e[t, a, off : off + count, :]
            ds = (
                weights.astype(f32) * (dot(v_win, g_one, NT) - delta[a : a + 1])
            ).astype(bf16)
            dk += dot(ds, q_one, NN)
            dv += dot(weights, g_one, NN)
            dqs.append(dot(k_win, ds, TN)[a * HEAD_DIM : (a + 1) * HEAD_DIM])
        dq = jnp.transpose(jnp.concatenate(dqs, axis=0)) * HEAD_DIM ** (-0.5)
        put_dq(qs, cols, dq.astype(bf16))
        put_kv(number, loc, ks, count, cols, dk, dv)


def back_kernel(sc, g, o, recip, q, k, v, e_hbm, dq, dk, dv, e, sems):
    p = sc[0]
    pairs = q.shape[1] // 128
    loads = [pltpu.make_async_copy(e_hbm.at[t], e.at[t], sems.at[t]) for t in range(pairs)]
    for load in loads:
        load.start()

    def put_dq(qs, cols, value):
        dq[pl.ds(qs, QB), cols] = value

    def put_kv(number, loc, ks, count, cols, dk_part, dv_part):
        for ref, value in ((dk, dk_part), (dv, dv_part)):
            if number == 0:
                ref[:, cols] = value
            else:
                ref[pl.ds(loc, count), cols] += value

    for t in range(pairs):
        loads[t].wait()
        back_pair(p, t, g, o, recip, q, k, v, e, put_dq, put_kv)


def attend_back(sc, g, o, recip, q, k, v, e):
    length, group = q.shape
    half = length // 2
    return call(
        back_kernel, "attend_back", 9, sc, (g, o, recip, q, k, v, e),
        [full((half, group))] * 3
        + [pl.BlockSpec((half, group), lambda t, s: (s[0], 0)), full(k.shape), full(v.shape), ANY],
        [((half, group), bf16), ((3 * QB, group), f32), ((3 * QB, group), f32)],
        [full((half, group)), full((3 * QB, group)), full((3 * QB, group))],
        [pltpu.VMEM(e.shape, bf16), pltpu.SemaphoreType.DMA((group // 128,))],
    )


def finish_kernel(
    per, sc, tabs, idx, g, o, recip, q, k, v, dq_own, dk_own, dv_own, pt, w, g1b, e_hbm,
    keep, send, hid_other, hid_own, e, gq, ksum, vsum, terms, sems,
):
    h, p = sc[0], sc[1]
    width = pt.shape[1]
    mid = width // 2
    length, group = ksum.shape
    half = length // 2
    pairs = group // 128
    loads = [pltpu.make_async_copy(e_hbm.at[t], e.at[t], sems.at[t]) for t in range(pairs)]
    for load in loads:
        load.start()
    own = pl.ds(pl.multiple_of(half * h, half), half)
    window = pl.ds(pl.multiple_of(QB * h, QB), 3 * QB)
    gq[own, 0:group] = dq_own[...]
    for total, part in ((ksum, dk_own), (vsum, dv_own)):
        total[...] = jnp.zeros_like(total)
        total[window, :] = part[...]

    def put_dq(qs, cols, value):
        gq[pl.ds(pl.multiple_of(half * p + qs, QB), QB), cols] = value

    def put_kv(number, loc, ks, count, cols, dk_part, dv_part):
        ksum[pl.ds(ks, count), cols] += dk_part
        vsum[pl.ds(ks, count), cols] += dv_part

    for t in range(pairs):
        loads[t].wait()
        back_pair(p, t, g, o, recip, q, k, v, e, put_dq, put_kv)
    gq[:, group : 2 * group] = ksum[...].astype(bf16)
    gq[:, 2 * group :] = vsum[...].astype(bf16)
    grads = gq[...]
    grad = dot(pt[...], grads, TN).astype(bf16)
    keep[:, : 3 * group] = grad[:mid]
    send[:, : 3 * group] = grad[mid:]
    sums = jnp.sum(grads.astype(f32), axis=0, keepdims=True)
    sums = jnp.concatenate([sums[:, :group], sums[:, 2 * group :]], axis=1).astype(bf16)
    sums = jnp.broadcast_to(sums, (16, 2 * group))
    sums = dot(sums, order_matrix(sc, tabs, width, per), NN).astype(bf16)
    first = onehot(lax.broadcasted_iota(i32, (16, 128), 0) == 0)
    extra = dot(sums, first, TN).astype(bf16)
    keep[:, 3 * group :] = extra[:mid]
    send[:, 3 * group :] = extra[mid:]
    for i in range(2):
        rows = slice(i * half, (i + 1) * half)
        mine = jnp.where(h == i, 1.0, 0.0)
        part = dot(grads[rows], w[...], NT) + mine * g1b[...].astype(f32)
        terms[rows, :] = part.astype(bf16)
    spot = lax.broadcasted_iota(i32, (half, length), 0)
    hid_other[...] = dot(onehot(spot + half * p == idx[...]), terms[...], NN).astype(bf16)
    hid_own[...] = dot(onehot(spot + half * h == idx[...]), terms[...], NN).astype(bf16)


def finish(per, sc, tabs, idx, g, o, recip, q, k, v, parts, pt, w, g1b, e):
    length, group = q.shape
    half, width = g1b.shape
    wide = (width // 2, 3 * group + 128)
    args = (tabs, idx, g, o, recip, q, k, v, *parts, pt, w, g1b, e)
    specs = [full(x.shape) for x in args[:-1]] + [ANY]
    specs[2] = full((half, group))
    specs[5] = pl.BlockSpec((half, group), lambda t, s: (s[1], 0))
    return call(
        functools.partial(finish_kernel, per), "finish", 20, sc, args, specs,
        [(wide, bf16), (wide, bf16), ((half, width), bf16), ((half, width), bf16)],
        [full(wide), full(wide), full((half, width)), full((half, width))],
        [
            pltpu.VMEM(e.shape, bf16),
            pltpu.VMEM((length, 3 * group), bf16),
            pltpu.VMEM((length, group), f32),
            pltpu.VMEM((length, group), f32),
            pltpu.VMEM((length, width), bf16),
            pltpu.SemaphoreType.DMA((group // 128,)),
        ],
    )


def ordered_kernel(per, sc, tabs, packed, out):
    width = packed.shape[1]
    out[...] = dot(packed[...], order_matrix(sc, tabs, width, per), NN).astype(bf16)


def ordered(per, sc, tabs, packed):
    return call(
        functools.partial(ordered_kernel, per), "ordered", ORDERED, sc, (tabs, packed),
        [full(tabs.shape), full(packed.shape)], [(packed.shape, bf16)], [full(packed.shape)], [],
    )[0]


def middle_kernel(
    per, sc, lens, tabs, packed, mixed_own, mixed_other, cot, ow_own, vectors, up_bias, pool,
    up_own, dn_own, a0, a1, a2, a3, b0, b1, b2, b3,
    out, pooled, send, gm_own, g1b, up_keep, up_send, dn_keep, dn_send,
    wup, wdn, ow_other, ub, act, slope, scaled1, normed1, nrel, grel, upk, ups, dnk, dns,
    smalls, bias_sums, sem_up, sem_dn, sem_ow, sem_ub, sem_out,
):
    quarter = sc[2]
    width = wup.shape[1]
    mid = width // 2
    hid = wup.shape[2]
    blk = hid // 4
    steps = hid // HB
    group = ow_own.shape[0]
    tokens = packed.shape[0]
    piece = group // 4
    out_bias, attn_gain, attn_shift, down_bias, ffn_gain, ffn_shift = (
        vectors[i : i + 1, :] for i in range(6)
    )
    ups_in, dns_in, small_in = [], [], []
    for j in range(steps):
        cols = pl.ds(j * HB, HB)
        ups_in.append(pltpu.make_async_copy(up_own.at[:, cols], wup.at[0, :, cols], sem_up.at[j]))
        dns_in.append(pltpu.make_async_copy(dn_own.at[cols, :], wdn.at[0, cols, :], sem_dn.at[j]))
    for r, (a_ref, b_ref) in enumerate(((a0, b0), (a1, b1), (a2, b2), (a3, b3))):
        place = quarter ^ r
        rows = pl.ds(pl.multiple_of(piece * place, 16), piece)
        for c in range(2):
            small_in.append(
                pltpu.make_async_copy(
                    a_ref.at[pl.ds(width + c * piece, piece), :],
                    ow_other.at[rows, pl.ds(c * blk, blk)],
                    sem_ow.at[2 * r + c],
                )
            )
        small_in.append(
            pltpu.make_async_copy(
                a_ref.at[pl.ds(width + 2 * piece, 16), :],
                ub.at[:, pl.ds(pl.multiple_of(blk * place, 128), blk)],
                sem_ub.at[r],
            )
        )
        ups_in.append(
            pltpu.make_async_copy(
                a_ref.at[pl.ds(0, width), :],
                wup.at[1, :, pl.ds(pl.multiple_of(blk * place, 128), blk)],
                sem_up.at[steps + r],
            )
        )
        dns_in.append(
            pltpu.make_async_copy(
                b_ref,
                wdn.at[1, pl.ds(pl.multiple_of(blk * place, 16), blk), :],
                sem_dn.at[steps + r],
            )
        )
    for copy in small_in + ups_in + dns_in:
        copy.start()
    for copy in small_in:
        copy.wait()
    resid = (
        packed[...].astype(f32)
        + dot(mixed_own[...], ow_own[...], NN)
        + dot(mixed_other[...], ow_other[...], NN)
        + out_bias
    )
    center = resid - jnp.mean(resid, axis=-1, keepdims=True)
    inv1 = lax.rsqrt(jnp.mean(center * center, axis=-1, keepdims=True) + EPS)
    norm = center * inv1
    scaled1[...] = norm
    norm = norm * attn_gain + attn_shift
    normed1[...] = norm
    low = norm.astype(bf16)
    order = order_matrix(sc, tabs, width, per)
    nrel[...] = dot(low, order, NN).astype(bf16)
    total = jnp.zeros(norm.shape, f32)
    for j in range(2 * steps):
        side, cols = j // steps, slice((j % steps) * HB, (j % steps + 1) * HB)
        if side == 0:
            ups_in[j].wait()
            dns_in[j].wait()
            bias = up_bias[:, cols]
        else:
            if j == steps:
                for copy in ups_in[steps:] + dns_in[steps:]:
                    copy.wait()
            three = ub[:, cols].astype(f32)
            bias = three[0:1] + three[1:2] + three[2:3]
        value, deriv = gelu_pair(dot(low, wup[side, :, cols], NN) + bias)
        value = value.astype(bf16)
        act[j] = value
        slope[j] = deriv.astype(bf16)
        total = total + dot(value, wdn[side, cols, :], NN)
    resid = normed1[...] + total + down_bias
    center = resid - jnp.mean(resid, axis=-1, keepdims=True)
    inv2 = lax.rsqrt(jnp.mean(center * center, axis=-1, keepdims=True) + EPS)
    scaled2 = center * inv2
    result = scaled2 * ffn_gain + ffn_shift
    high = result.astype(bf16)
    out[...] = high
    rest = (result - high.astype(f32)).astype(bf16)
    sums = dot(pool[...], high, NN) + dot(pool[...], rest, NN)
    row = lax.broadcasted_iota(i32, (16, 1), 0)
    scale = jnp.zeros((16, 1), f32)
    for c in range(lens.shape[1]):
        scale = jnp.where(row == c, 1.0 / lens[0, c].astype(f32), scale)
    sums = sums * scale
    pooled[...] = sums
    sums = sums.astype(bf16)
    send[tokens : tokens + 16, :] = sums[:, :group]
    send[tokens + 16 : tokens + 32, :] = sums[:, group:]

    grad = cot[...].astype(f32)
    smalls[4:5, :] = jnp.sum(grad * scaled2, axis=0, keepdims=True)
    smalls[5:6, :] = jnp.sum(grad, axis=0, keepdims=True)
    smalls[6:16, :] = jnp.zeros((10, width), f32)
    grad = grad * ffn_gain
    grad_resid2 = inv2 * (
        grad
        - jnp.mean(grad, axis=-1, keepdims=True)
        - scaled2 * jnp.mean(grad * scaled2, axis=-1, keepdims=True)
    )
    smalls[3:4, :] = jnp.sum(grad_resid2, axis=0, keepdims=True)
    low = grad_resid2.astype(bf16)
    grel[...] = dot(low, order, NN).astype(bf16)
    total = grad_resid2
    bias_sums[...] = jnp.zeros_like(bias_sums)
    copies = []

    def store(pairs):
        for source, target in pairs:
            copies.append(pltpu.make_async_copy(source, target, sem_out.at[len(copies)]))
            copies[-1].start()

    for j in range(2 * steps):
        side, cols = j // steps, slice((j % steps) * HB, (j % steps + 1) * HB)
        pre = (dot(low, wdn[side, cols, :], NT) * slope[j].astype(f32)).astype(bf16)
        total = total + dot(pre, wup[side, :, cols], NT)
        bias_sums[side : side + 1, cols] = jnp.sum(pre.astype(f32), axis=0, keepdims=True)
        grad = dot(nrel[...], pre, TN).astype(bf16)
        upk[side, :, cols] = grad[:mid]
        ups[side, :, cols] = grad[mid:]
        grad = dot(grel[...], act[j], TN).astype(bf16)
        both = slice(j * HB, (j + 1) * HB)
        dnk[:, both] = grad[:mid]
        dns[:, both] = grad[mid:]
        store(
            (
                (upk.at[side, :, cols], up_keep.at[side, :, cols]),
                (ups.at[side, :, cols], up_send.at[side, :, cols]),
                (dnk.at[:, both], dn_keep.at[:, both]),
                (dns.at[:, both], dn_send.at[:, both]),
            )
        )
    norm = scaled1[...]
    smalls[1:2, :] = jnp.sum(total * norm, axis=0, keepdims=True)
    smalls[2:3, :] = jnp.sum(total, axis=0, keepdims=True)
    grad = total * attn_gain
    grad_resid1 = inv1 * (
        grad
        - jnp.mean(grad, axis=-1, keepdims=True)
        - norm * jnp.mean(grad * norm, axis=-1, keepdims=True)
    )
    smalls[0:1, :] = jnp.sum(grad_resid1, axis=0, keepdims=True)
    low = grad_resid1.astype(bf16)
    g1b[...] = low
    send[0:tokens, :] = dot(low, ow_other[...], NT).astype(bf16)
    gm_own[...] = dot(low, ow_own[...], NT).astype(bf16)

    low = dot(low, order, NN).astype(bf16)
    rows = dot(smalls[...].astype(bf16), order, NN)
    pieces = []
    source = (tabs[0:1, :] ^ sc[3]) * (2 * per) + tabs[1:2, :]
    for part in range(hid // width):
        spread = onehot(source + part * per == lax.broadcasted_iota(i32, (hid, width), 0))
        pieces.append(dot(bias_sums[...].astype(bf16), spread, NN))
    eye = onehot(
        lax.broadcasted_iota(i32, (16, 128), 0) == lax.broadcasted_iota(i32, (16, 128), 1)
    )
    tail = slice(hid, hid + HB)
    for side in range(2):
        mixed = (mixed_own, mixed_other)[side]
        grad = dot(low, mixed[...], TN).astype(bf16)
        lines = jnp.concatenate(
            [rows[:8]] + [x[side : side + 1] for x in pieces] + [rows[8 + len(pieces) :]], axis=0
        ).astype(bf16)
        extra = dot(lines, eye, TN).astype(bf16)
        for ref, part in ((upk, slice(0, mid)), (ups, slice(mid, width))):
            ref[side, :, hid : hid + group] = grad[part]
            ref[side, :, hid + group :] = extra[part]
        store(
            (
                (upk.at[side, :, tail], up_keep.at[side, :, tail]),
                (ups.at[side, :, tail], up_send.at[side, :, tail]),
            )
        )
    for copy in copies:
        copy.wait()


def middle(per, sc, lens, tabs, packed, mixed_own, mixed_other, cot, ow, vectors, up_bias, pool, up, dn, quads):
    half = packed.shape[0] // 2
    width, hid = up.shape
    group = ow.shape[0]
    blk, steps = hid // 4, hid // HB
    mid = width // 2
    wide = (2, mid, hid + HB)
    outs = [
        ((half, width), bf16),
        ((16, width), f32),
        ((half + 32, group), bf16),
        ((half, group), bf16),
        ((half, width), bf16),
        (wide, bf16),
        (wide, bf16),
        ((mid, 2 * hid), bf16),
        ((mid, 2 * hid), bf16),
    ]
    args = (
        lens, tabs, packed, mixed_own, mixed_other, cot, ow, vectors, up_bias, pool, up, dn,
        *[a for a, _ in quads], *[b for _, b in quads],
    )
    return call(
        functools.partial(middle_kernel, per), "middle", 35, sc, args,
        [
            pl.BlockSpec(memory_space=pltpu.SMEM),
            full(tabs.shape),
            pl.BlockSpec((half, width), lambda t, s: (s[0], 0)),
            full((half, group)),
            full((half, group)),
            full((half, width)),
            full((group, width)),
            full(vectors.shape),
            full((1, hid)),
            pl.BlockSpec((16, half), lambda t, s: (0, s[0])),
        ]
        + [ANY] * 10,
        outs,
        [full(s) for s, _ in outs[:5]] + [ANY] * 4,
        [
            pltpu.VMEM((2, width, hid), bf16),
            pltpu.VMEM((2, hid, width), bf16),
            pltpu.VMEM((group, width), bf16),
            pltpu.VMEM((16, hid), bf16),
            pltpu.VMEM((2 * steps, half, HB), bf16),
            pltpu.VMEM((2 * steps, half, HB), bf16),
            pltpu.VMEM((half, width), f32),
            pltpu.VMEM((half, width), f32),
            pltpu.VMEM((half, width), bf16),
            pltpu.VMEM((half, width), bf16),
            pltpu.VMEM(wide, bf16),
            pltpu.VMEM(wide, bf16),
            pltpu.VMEM((mid, 2 * hid), bf16),
            pltpu.VMEM((mid, 2 * hid), bf16),
            pltpu.VMEM((16, width), f32),
            pltpu.VMEM((16, hid), f32),
            pltpu.SemaphoreType.DMA((steps + 4,)),
            pltpu.SemaphoreType.DMA((steps + 4,)),
            pltpu.SemaphoreType.DMA((8,)),
            pltpu.SemaphoreType.DMA((4,)),
            pltpu.SemaphoreType.DMA((8 * steps + 4,)),
        ],
    )


def swap(value, axis, bit):
    count = lax.axis_size(axis)
    return lax.ppermute(value, axis, [(i, i ^ (1 << bit)) for i in range(count)])


def pin(*values):
    return lax.optimization_barrier(values)


def add_low(left, right):
    return (left.astype(f32) + right.astype(f32)).astype(bf16)


def body(
    hidden,
    source_index,
    crop_lengths,
    deleted,
    qkv_weight,
    qv_bias,
    out_weight,
    out_bias,
    attn_gain,
    attn_shift,
    up_weight,
    up_bias,
    down_weight,
    down_bias,
    ffn_gain,
    ffn_shift,
    cotangent,
):
    length, width = hidden.shape
    crops = crop_lengths.shape[1]
    group = out_weight.shape[0]
    hid = up_weight.shape[1]
    half = length // 2
    n_dp, n_rep = lax.axis_size("dp"), lax.axis_size("rep")
    dp_bits, rep_bits = n_dp.bit_length() - 1, n_rep.bit_length() - 1
    shards = n_dp * n_rep
    per = width // shards
    h, dp = lax.axis_index("head"), lax.axis_index("dp")
    me = dp * n_rep + lax.axis_index("rep")
    sc = jnp.stack([h, 1 - h, dp & 3, me]).astype(i32)

    stages = [("dp", b) for b in range(dp_bits)] + [("rep", b) for b in range(rep_bits)]
    block = np.zeros(shards, np.int32)
    for number, (axis, bit) in enumerate(stages):
        value = (np.arange(shards) >> (len(stages) - 1 - number)) & 1
        block |= (value << (bit + (rep_bits if axis == "dp" else 0))).astype(np.int32)
    row = np.arange(width)
    tabs = np.zeros((8, width), np.int32)
    tabs[0] = block[row // per]
    tabs[1] = row % per
    tabs = jnp.asarray(tabs)

    first, second = bundle(sc, up_bias, up_weight, down_weight, out_weight)
    first = swap(first, "head", 0)
    second = swap(second, "head", 0)
    packed, q, k, v, e_other, o_other, recip_other, segrow, code, pool = prepare(
        sc, crop_lengths, hidden, source_index, deleted, qkv_weight, qv_bias
    )
    mixed_recv = swap(o_other, "head", 0)
    first, o_other = pin(first, o_other)
    first_y = swap(first, "dp", 1)
    q_late, first = pin(q, first)
    e_own, o_own, recip_own = attend(sc, q_late, k, v, segrow, code)
    second, o_own = pin(second, o_own)
    second_y = swap(second, "dp", 1)
    packed_late, mixed_recv, second = pin(packed, mixed_recv, second)
    pt = ordered(per, sc, tabs, packed_late)
    first, first_y, second_y, pt = pin(first, first_y, second_y, pt)
    first_c, first_cy = swap(first, "dp", 0), swap(first_y, "dp", 0)
    second_c, second_cy = swap(second, "dp", 0), swap(second_y, "dp", 0)
    quads = [(first, second), (first_c, second_c), (first_y, second_y), (first_cy, second_cy)]
    vectors = jnp.stack(
        [out_bias, attn_gain, attn_shift, down_bias, ffn_gain, ffn_shift, ffn_shift, ffn_shift]
    )
    output, pooled, send, gm_own, g1b, up_keep, up_send, dn_keep, dn_send = middle(
        per, sc, crop_lengths, tabs, packed, o_own, mixed_recv, cotangent, out_weight, vectors,
        up_bias, pool, up_weight, down_weight, quads,
    )
    recv = swap(send, "head", 0)
    dq_own, dk_own, dv_own = attend_back(sc, gm_own, o_own, recip_own, q, k, v, e_own)
    up_recv = pin(swap(up_send, "dp", 0), dq_own)[0]
    up_next = add_low(up_keep[1, :, :hid], up_recv[1, :, :hid])
    rest = add_low(up_keep[:, :, hid:], up_recv[:, :, hid:])
    rest = rest.reshape(2, n_dp // 2, n_rep, per, HB)
    dn_recv = pin(swap(dn_send, "dp", 0), up_next, rest)[0]
    part = width // 4
    dn_next = add_low(dn_keep[part:], dn_recv[part:])
    recv, dn_next, up_next, rest, dq_own = pin(recv, dn_next, up_next, rest, dq_own)
    qkv_keep, qkv_send, hidden_other, hidden_own = finish(
        per, sc, tabs, source_index, recv, o_other, recip_other, q, k, v,
        (dq_own, dk_own, dv_own), pt, qkv_weight, g1b, e_other,
    )
    hidden_recv = swap(hidden_other, "head", 0)

    last = [hidden_own]

    def arrive(value):
        return pin(value, last[0])[0].astype(f32)

    def keep_low(value):
        last[0] = value.astype(bf16)
        return last[0]

    def low_half(value, axis, bit):
        rows = value.shape[0] // 2
        return keep_low(value[:rows].astype(f32) + arrive(swap(value[rows:], axis, bit)))

    def low_rest(value, axis, bit, dim):
        count = value.shape[dim] // 2
        keep, out = jnp.split(value, 2, axis=dim)
        return keep_low(keep.astype(f32) + arrive(swap(out, axis, bit)))

    later = stages[1:]
    dp_later = [x for x in later if x[0] == "dp"]
    rep_all = [x for x in later if x[0] == "rep"]
    up_swap = swap(up_next, "head", 0)
    dn_swap = swap(dn_next, *later[0])
    qkv_swap = swap(qkv_send, "dp", 0)

    rest = low_rest(rest, *rep_all[0], 2)
    down = keep_low(
        dn_keep[:part].astype(f32) + dn_recv[:part].astype(f32) + arrive(dn_swap)
    )
    up = keep_low(
        up_keep[0, :, :hid].astype(f32) + up_recv[0, :, :hid].astype(f32) + arrive(up_swap)
    )
    qkv = keep_low(qkv_keep.astype(f32) + arrive(qkv_swap))
    rest_later = [(x, 2) for x in rep_all[1:]] + [(x, 1) for x in dp_later]
    for number, (axis, bit) in enumerate(later[1:]):
        (rest_axis, rest_bit), dim = rest_later[number]
        rest = low_rest(rest, rest_axis, rest_bit, dim)
        down = low_half(down, axis, bit)
        up = low_half(up, *later[number])
        qkv = low_half(qkv, *later[number])
        if number == 0:
            grad_hidden = hidden_own.astype(f32) + arrive(hidden_recv)
            last[0] = grad_hidden
    axis, bit = later[-1]
    rows = up.shape[0] // 2
    rest = rest[0].astype(f32) + arrive(swap(rest[1], "head", 0))
    last[0] = rest
    down = down[:, :hid].astype(f32) + arrive(swap(down[:, hid:], "head", 0))
    last[0] = down
    up = up[:rows].astype(f32) + arrive(swap(up[rows:], axis, bit))
    last[0] = up
    qkv = qkv[:rows].astype(f32) + arrive(swap(qkv[rows:], axis, bit))
    rest = rest.reshape(per, HB)

    extra = rest[:, group:].T
    small = lax.dynamic_slice_in_dim(extra[:6], h * (per // 2), per // 2, 1)
    pooled_other = recv[half:].astype(f32)
    pooled_other = jnp.concatenate([pooled_other[:crops], pooled_other[16 : 16 + crops]], axis=1)
    return (
        output,
        pooled[:crops] + pooled_other,
        grad_hidden,
        qkv[:, : 3 * group],
        qkv[:, 3 * group].reshape(1, per),
        rest[:, :group].T,
        small[0],
        small[1],
        small[2],
        up,
        extra[8 : 8 + hid // width].reshape(1, hid // shards),
        down.T,
        small[3],
        small[4],
        small[5],
    )


def solution(mesh):
    rows = P(("dp", "rep"), None)
    every = P(("dp", "rep", "head"), None)
    vector = P(("dp", "rep", "head"))
    return jax.shard_map(
        body,
        mesh=mesh,
        in_specs=(
            rows,
            rows,
            rows,
            rows,
            P(None, "head"),
            P("head", None),
            P("head", None),
            P(),
            P(),
            P(),
            P(None, "head"),
            P("head", None),
            P("head", None),
            P(),
            P(),
            P(),
            every,
        ),
        out_specs=(
            every,
            rows,
            every,
            P(("dp", "rep"), "head"),
            P("head", ("dp", "rep")),
            P("head", ("dp", "rep")),
            vector,
            vector,
            vector,
            P(("dp", "rep"), "head"),
            P("head", ("dp", "rep")),
            P("head", ("dp", "rep")),
            vector,
            vector,
            vector,
        ),
        check_vma=False,
    )
```

```python
import functools
import math

import jax
import jax.numpy as jnp
import numpy as np
from jax import lax
from jax.experimental import pallas as pl
from jax.experimental.pallas import tpu as pltpu
from jax.sharding import PartitionSpec as P

HEAD_DIM = 64
CROP_MAX = 256
EPS = 1e-12
MASKED = -1e30
NN = ((1,), (0,))
NT = ((1,), (1,))
TN = ((0,), (0,))
f32 = jnp.float32
bf16 = jnp.bfloat16
i32 = jnp.int32
NEEDS = {
    "bundle": 60,
    "prepare": 26,
    "attend": 18,
    "ordered": 14,
    "forward": 60,
    "backward": 60,
    "attend_back": 24,
    "finish": 40,
    "input_grad": 24,
    "down_sums": 8,
    "up_sums": 10,
}
QB = CROP_MAX
HB = 512
SCALE = 0.4
ORDERED = 60

shape = jax.ShapeDtypeStruct
ANY = pl.BlockSpec(memory_space=pl.ANY)


def dot(left, right, how):
    return lax.dot_general(left, right, (how, ((), ())), preferred_element_type=f32)


def cost(micros):
    return pl.CostEstimate(
        flops=int(SCALE * micros * 1.1e9), bytes_accessed=1024, transcendentals=0
    )


def full(dims):
    return pl.BlockSpec(dims, lambda *_: (0,) * len(dims))


def call(kernel, name, micros, sc, args, in_specs, outs, out_specs, scratch):
    return pl.pallas_call(
        kernel,
        grid_spec=pltpu.PrefetchScalarGridSpec(
            num_scalar_prefetch=1,
            grid=(1,),
            in_specs=in_specs,
            out_specs=out_specs,
            scratch_shapes=scratch,
        ),
        out_shape=[shape(s, d) for s, d in outs],
        compiler_params=pltpu.CompilerParams(vmem_limit_bytes=NEEDS[name] * 1024 * 1024),
        cost_estimate=cost(micros),
        name=name,
    )(sc, *args)


def onehot(hit):
    return jnp.where(hit, 1.0, 0.0).astype(bf16)


def gelu_pair(u):
    t = 1.0 / (1.0 + (0.3275911 / math.sqrt(2.0)) * jnp.abs(u))
    bell = jnp.exp(-0.5 * (u * u))
    poly = t * (
        0.127414796 + t * (-0.142248368 + t * (0.7107068705 + t * (-0.7265760135 + t * 0.5307027145)))
    )
    tail = poly * bell
    phi = jnp.where(u < 0, tail, 1.0 - tail)
    return u * phi, phi + u * bell * (1.0 / math.sqrt(2.0 * math.pi))


def order_matrix(sc, tabs, width, per):
    source = (tabs[0:1, :] ^ sc[3]) * per + tabs[1:2, :]
    return onehot(source == lax.broadcasted_iota(i32, (width, width), 0))


def bundle_kernel(sc, up_bias, up, dn, ow, first, second, sems):
    quarter = sc[2]
    width, blk = up.shape[0], second.shape[0]
    piece = ow.shape[0] // 4
    cols = pl.ds(pl.multiple_of(quarter * blk, 128), blk)
    slab = pl.ds(pl.multiple_of(quarter * piece, 16), piece)
    copies = [
        pltpu.make_async_copy(up.at[:, cols], first.at[pl.ds(0, width), :], sems.at[0]),
        pltpu.make_async_copy(
            ow.at[slab, pl.ds(0, blk)], first.at[pl.ds(width, piece), :], sems.at[1]
        ),
        pltpu.make_async_copy(
            ow.at[slab, pl.ds(blk, blk)], first.at[pl.ds(width + piece, piece), :], sems.at[2]
        ),
        pltpu.make_async_copy(
            dn.at[pl.ds(pl.multiple_of(sc[4] * blk, 16), blk), :], second, sems.at[3]
        ),
    ]
    for copy in copies:
        copy.start()
    bias = up_bias[0:1, cols]
    high = bias.astype(bf16).astype(f32)
    mid = (bias - high).astype(bf16).astype(f32)
    low = bias - high - mid
    first[width + 2 * piece :, :] = jnp.concatenate(
        [high, mid, low, jnp.zeros((13, blk), f32)], axis=0
    ).astype(bf16)
    for copy in copies:
        copy.wait()


def bundle(sc, up_bias, up, dn, ow):
    width, hid = up.shape
    blk = hid // 4
    rows = width + ow.shape[0] // 2 + 16
    return call(
        bundle_kernel, "bundle", 2, sc, (up_bias, up, dn, ow),
        [full(up_bias.shape), ANY, ANY, ANY],
        [((rows, blk), bf16), ((blk, width), bf16)],
        [full((rows, blk)), full((blk, width))],
        [pltpu.SemaphoreType.DMA((4,))],
    )


def half_blocks(p):
    half = 2 * QB
    return (
        (pl.multiple_of(QB * p, QB), pl.multiple_of(half * p, QB), 2 * QB, 0, pl.multiple_of(QB * p, QB)),
        (pl.multiple_of(QB - QB * p, QB), pl.multiple_of(QB * p, QB), 3 * QB, 2 * QB, 0),
    )


def fill_cap(p, segrow, code, cap):
    for qs, ks, count, off, _ in half_blocks(p):
        first = pl.multiple_of(2 * QB * p + qs, QB)
        keys = code[pl.ds(ks, count), :]
        keys = jnp.concatenate([keys] * (QB // 128), axis=1)
        ask = segrow[0:1, pl.ds(first, QB)]
        shift = lax.broadcasted_iota(i32, (count, QB), 0) - lax.broadcasted_iota(
            i32, (count, QB), 1
        )
        allowed = (keys == ask) | (shift == first - ks)
        cap[off : off + count, :] = jnp.where(allowed, 3e38, MASKED)


def attend_pair(p, base, t, q, k, v, cap, e, mixed, recip):
    lane = lax.broadcasted_iota(i32, (QB, 128), 1) < HEAD_DIM
    cols = slice(t * 128, (t + 1) * 128)
    for qs, ks, count, off, _ in half_blocks(p):
        q_blk = q[pl.ds(pl.multiple_of(base + qs, QB), QB), cols]
        k_win = k[pl.ds(ks, count), cols]
        v_win = v[pl.ds(ks, count), cols]
        v_lane = lax.broadcasted_iota(i32, (count, 128), 1) < HEAD_DIM
        outs, recips = [], []
        for a in range(2):
            q_one = jnp.where(lane == (a == 0), q_blk, jnp.zeros_like(q_blk))
            s = jnp.minimum(dot(k_win, q_one, NT), cap[off : off + count, :])
            weights = jnp.exp(s - jnp.max(s, axis=0, keepdims=True)).astype(bf16)
            e[t, a, off : off + count, :] = weights
            v_one = jnp.where(v_lane == (a == 0), v_win, jnp.ones_like(v_win))
            o = dot(v_one, weights, TN)
            value, total = o[:HEAD_DIM], o[HEAD_DIM:]
            if a == 1:
                value, total = total, value
            inv = 1.0 / total
            outs.append(value * inv)
            recips.append(inv)
        mixed[pl.ds(qs, QB), cols] = jnp.transpose(jnp.concatenate(outs, axis=0)).astype(bf16)
        recip[pl.ds(qs, QB), cols] = jnp.transpose(jnp.concatenate(recips, axis=0))


def prepare_kernel(
    sc, lens, hidden, idx, dele, w, qv_bias,
    packed_hbm, q_hbm, k_hbm, v_hbm, e_hbm, mixed, recip, segrow, code, pool,
    packed, q, k, v, e, cap, sems,
):
    length, width = hidden.shape
    group = q.shape[1]
    idx_col = jnp.transpose(jnp.broadcast_to(idx[...].astype(f32), (8, length)))[:, :1]
    lane = lax.broadcasted_iota(i32, (8, length), 1)
    seg = jnp.zeros((8, length), f32)
    end = jnp.int32(0)
    for c in range(lens.shape[1]):
        end = end + lens[0, c]
        seg = seg + jnp.where(lane >= end, 1.0, 0.0)
    segrow[...] = seg
    code_row = jnp.where(jnp.broadcast_to(dele[...], (8, length)) == 0, seg, -1.0)
    code[...] = jnp.broadcast_to(jnp.transpose(code_row)[:, :1], code.shape)
    crop_row = lax.broadcasted_iota(i32, pool.shape, 0).astype(f32)
    pool[...] = onehot(crop_row == jnp.broadcast_to(code_row[:1], pool.shape))
    copies = []
    for i in range(length // QB):
        rows = slice(i * QB, (i + 1) * QB)
        place = lax.broadcasted_iota(i32, (QB, length), 1).astype(f32)
        pk = dot(onehot(idx_col[rows] == place), hidden[...], NN).astype(bf16)
        packed[rows, :] = pk
        out = dot(pk, w[...], NN)
        q[rows, :] = (out[:, :group] + qv_bias[:, :group]).astype(bf16) * jnp.asarray(
            HEAD_DIM**-0.5, bf16
        )
        k[rows, :] = out[:, group : 2 * group].astype(bf16)
        v[rows, :] = (out[:, 2 * group :] + qv_bias[:, group:]).astype(bf16)
    for number, (source, target) in enumerate(
        ((packed, packed_hbm), (q, q_hbm), (k, k_hbm), (v, v_hbm))
    ):
        copies.append(pltpu.make_async_copy(source, target, sems.at[number]))
        copies[-1].start()
    p = sc[1]
    fill_cap(p, segrow, code, cap)
    for t in range(group // 128):
        attend_pair(p, 2 * QB * p, t, q, k, v, cap, e, mixed, recip)
        copies.append(pltpu.make_async_copy(e.at[t], e_hbm.at[t], sems.at[4 + t]))
        copies[-1].start()
    for copy in copies:
        copy.wait()


def prepare(sc, lens, hidden, idx, dele, w, qv_bias):
    length, width = hidden.shape
    group = w.shape[1] // 3
    half, pairs = length // 2, group // 128
    weights = (pairs, 2, 5 * QB, QB)
    return call(
        prepare_kernel, "prepare", 15, sc, (lens, hidden, idx, dele, w, qv_bias),
        [pl.BlockSpec(memory_space=pltpu.SMEM)]
        + [full(x.shape) for x in (hidden, idx, dele, w, qv_bias)],
        [
            ((length, width), bf16),
            ((length, group), bf16),
            ((length, group), bf16),
            ((length, group), bf16),
            (weights, bf16),
            ((half, group), bf16),
            ((half, group), f32),
            ((8, length), f32),
            ((length, 128), f32),
            ((16, length), bf16),
        ],
        [ANY] * 5
        + [full((half, group)), full((half, group)), full((8, length)), full((length, 128)),
           full((16, length))],
        [
            pltpu.VMEM((length, width), bf16),
            pltpu.VMEM((length, group), bf16),
            pltpu.VMEM((length, group), bf16),
            pltpu.VMEM((length, group), bf16),
            pltpu.VMEM(weights, bf16),
            pltpu.VMEM((5 * QB, QB), f32),
            pltpu.SemaphoreType.DMA((4 + pairs,)),
        ],
    )


def attend_kernel(sc, q, k, v, segrow, code, e_hbm, mixed, recip, e, cap, sems):
    p = sc[0]
    fill_cap(p, segrow, code, cap)
    copies = []
    for t in range(q.shape[1] // 128):
        attend_pair(p, 0, t, q, k, v, cap, e, mixed, recip)
        copies.append(pltpu.make_async_copy(e.at[t], e_hbm.at[t], sems.at[t]))
        copies[-1].start()
    for copy in copies:
        copy.wait()


def attend(sc, q, k, v, segrow, code):
    length, group = q.shape
    half, pairs = length // 2, group // 128
    weights = (pairs, 2, 5 * QB, QB)
    return call(
        attend_kernel, "attend", 9, sc, (q, k, v, segrow, code),
        [pl.BlockSpec((half, group), lambda t, s: (s[0], 0))]
        + [full(x.shape) for x in (k, v, segrow, code)],
        [(weights, bf16), ((half, group), bf16), ((half, group), f32)],
        [ANY, full((half, group)), full((half, group))],
        [
            pltpu.VMEM(weights, bf16),
            pltpu.VMEM((5 * QB, QB), f32),
            pltpu.SemaphoreType.DMA((pairs,)),
        ],
    )


def back_pair(p, t, g, o, recip, q, k, v, e, put_dq, put_kv):
    lane = lax.broadcasted_iota(i32, (QB, 128), 1) < HEAD_DIM
    cols = slice(t * 128, (t + 1) * 128)
    pick = onehot(
        (lax.broadcasted_iota(i32, (16, 128), 1) < HEAD_DIM)
        == (lax.broadcasted_iota(i32, (16, 128), 0) == 0)
    )
    outer, inner = half_blocks(p)
    for number, (qs, ks, count, off, loc) in enumerate((inner, outer)):
        rows = pl.ds(qs, QB)
        grad = g[rows, cols].astype(f32) * recip[rows, cols]
        both = grad * o[rows, cols].astype(f32)
        high = both.astype(bf16)
        rest = (both - high.astype(f32)).astype(bf16)
        delta = dot(pick, high, NT) + dot(pick, rest, NT)
        grad = grad.astype(bf16)
        q_blk = q[rows, cols]
        k_win = k[pl.ds(ks, count), cols]
        v_win = v[pl.ds(ks, count), cols]
        dk = jnp.zeros((count, 128), f32)
        dv = jnp.zeros((count, 128), f32)
        dqs = []
        for a in range(2):
            g_one = jnp.where(lane == (a == 0), grad, jnp.zeros_like(grad))
            q_one = jnp.where(lane == (a == 0), q_blk, jnp.zeros_like(q_blk))
            weights = e[t, a, off : off + count, :]
            ds = (
                weights.astype(f32) * (dot(v_win, g_one, NT) - delta[a : a + 1])
            ).astype(bf16)
            dk += dot(ds, q_one, NN)
            dv += dot(weights, g_one, NN)
            dqs.append(dot(k_win, ds, TN)[a * HEAD_DIM : (a + 1) * HEAD_DIM])
        dq = jnp.transpose(jnp.concatenate(dqs, axis=0)) * HEAD_DIM ** (-0.5)
        put_dq(qs, cols, dq.astype(bf16))
        put_kv(number, loc, ks, count, cols, dk, dv)


def back_kernel(sc, g, o, recip, q, k, v, e_hbm, dq, dk, dv, e, sems):
    p = sc[0]
    pairs = q.shape[1] // 128
    loads = [pltpu.make_async_copy(e_hbm.at[t], e.at[t], sems.at[t]) for t in range(pairs)]
    for load in loads:
        load.start()

    def put_dq(qs, cols, value):
        dq[pl.ds(qs, QB), cols] = value

    def put_kv(number, loc, ks, count, cols, dk_part, dv_part):
        for ref, value in ((dk, dk_part), (dv, dv_part)):
            if number == 0:
                ref[:, cols] = value
            else:
                ref[pl.ds(loc, count), cols] += value

    for t in range(pairs):
        loads[t].wait()
        back_pair(p, t, g, o, recip, q, k, v, e, put_dq, put_kv)


def attend_back(sc, g, o, recip, q, k, v, e):
    length, group = q.shape
    half = length // 2
    return call(
        back_kernel, "attend_back", 0.1, sc, (g, o, recip, q, k, v, e),
        [full((half, group))] * 3
        + [pl.BlockSpec((half, group), lambda t, s: (s[0], 0)), full(k.shape), full(v.shape), ANY],
        [((half, group), bf16), ((3 * QB, group), f32), ((3 * QB, group), f32)],
        [full((half, group)), full((3 * QB, group)), full((3 * QB, group))],
        [pltpu.VMEM(e.shape, bf16), pltpu.SemaphoreType.DMA((group // 128,))],
    )


def finish_kernel(
    sc, g, o, recip, q, k, v, dq_own, dk_own, dv_own, pt, lines, order, e_hbm,
    keep, send, gq, e, ksum, vsum, sems,
):
    h, p = sc[0], sc[1]
    width = pt.shape[1]
    mid = width // 2
    length, group = ksum.shape
    half = length // 2
    pairs = group // 128
    loads = [pltpu.make_async_copy(e_hbm.at[t], e.at[t], sems.at[t]) for t in range(pairs)]
    for load in loads:
        load.start()
    own = pl.ds(pl.multiple_of(half * h, half), half)
    window = pl.ds(pl.multiple_of(QB * h, QB), 3 * QB)
    gq[own, 0:group] = dq_own[...]
    for total, part in ((ksum, dk_own), (vsum, dv_own)):
        total[...] = jnp.zeros_like(total)
        total[window, :] = part[...]

    def put_dq(qs, cols, value):
        gq[pl.ds(pl.multiple_of(half * p + qs, QB), QB), cols] = value

    def put_kv(number, loc, ks, count, cols, dk_part, dv_part):
        ksum[pl.ds(ks, count), cols] += dk_part
        vsum[pl.ds(ks, count), cols] += dv_part

    for t in range(pairs):
        loads[t].wait()
        back_pair(p, t, g, o, recip, q, k, v, e, put_dq, put_kv)
    gq[:, group : 2 * group] = ksum[...].astype(bf16)
    gq[:, 2 * group :] = vsum[...].astype(bf16)
    grads = gq[...]
    grad = dot(pt[...], grads, TN).astype(bf16)
    keep[:, : 3 * group] = grad[:mid]
    send[:, : 3 * group] = grad[mid:]
    sums = jnp.sum(grads.astype(f32), axis=0, keepdims=True)
    sums = jnp.concatenate([sums[:, :group], sums[:, 2 * group :]], axis=1).astype(bf16)
    sums = dot(jnp.broadcast_to(sums, (16, 2 * group)), order[...], NN)
    both = lines[...] + jnp.concatenate(
        [g[half + 32 : half + 48, :], g[half + 48 : half + 64, :]], axis=1
    ).astype(f32)
    both = jnp.where(lax.broadcasted_iota(i32, (16, width), 0) == 15, sums, both).astype(bf16)
    eye = onehot(
        lax.broadcasted_iota(i32, (16, 128), 0) == lax.broadcasted_iota(i32, (16, 128), 1)
    )
    extra = dot(both, eye, TN).astype(bf16)
    keep[:, 3 * group :] = extra[:mid]
    send[:, 3 * group :] = extra[mid:]

def finish(sc, g, o, recip, q, k, v, parts, pt, lines, order, e):
    length, group = q.shape
    half, width = length // 2, pt.shape[1]
    wide = (width // 2, 3 * group + 128)
    args = (g, o, recip, q, k, v, *parts, pt, lines, order, e)
    specs = [full(x.shape) for x in args[:-1]] + [ANY]
    specs[3] = pl.BlockSpec((half, group), lambda t, s: (s[1], 0))
    return call(
        finish_kernel, "finish", 0.1, sc, args, specs,
        [(wide, bf16), (wide, bf16), ((length, 3 * group), bf16)],
        [full(wide), full(wide), full((length, 3 * group))],
        [
            pltpu.VMEM(e.shape, bf16),
            pltpu.VMEM((length, group), f32),
            pltpu.VMEM((length, group), f32),
            pltpu.SemaphoreType.DMA((group // 128,)),
        ],
    )


def input_grad_kernel(sc, idx, gq, w, g1b, hid_other, hid_own, terms):
    h, p = sc[0], sc[1]
    half, length = g1b.shape[0], gq.shape[0]
    for i in range(2):
        rows = slice(i * half, (i + 1) * half)
        mine = jnp.where(h == i, 1.0, 0.0)
        part = dot(gq[rows, :], w[...], NT) + mine * g1b[...].astype(f32)
        terms[rows, :] = part.astype(bf16)
    spot = lax.broadcasted_iota(i32, (half, length), 0)
    hid_other[...] = dot(onehot(spot + half * p == idx[...]), terms[...], NN).astype(bf16)
    hid_own[...] = dot(onehot(spot + half * h == idx[...]), terms[...], NN).astype(bf16)


def input_grad(sc, idx, gq, w, g1b):
    half, width = g1b.shape
    args = (idx, gq, w, g1b)
    return call(
        input_grad_kernel, "input_grad", 0.1, sc, args, [full(x.shape) for x in args],
        [((half, width), bf16)] * 2, [full((half, width))] * 2,
        [pltpu.VMEM((2 * half, width), bf16)],
    )


def ordered_kernel(per, sc, tabs, packed, out, order):
    order[...] = order_matrix(sc, tabs, packed.shape[1], per)
    out[...] = dot(packed[...], order[...], NN).astype(bf16)


def ordered(per, sc, tabs, packed):
    width = packed.shape[1]
    return call(
        functools.partial(ordered_kernel, per), "ordered", ORDERED, sc, (tabs, packed),
        [full(tabs.shape), full(packed.shape)],
        [(packed.shape, bf16), ((width, width), bf16)],
        [full(packed.shape), full((width, width))],
        [],
    )


def weight_copies(sc, up_own, dn_own, quads, wup, wdn, sem_up, sem_dn):
    hid = wup.shape[2]
    width, blk, steps = wup.shape[1], hid // 4, hid // HB
    ups, dns = [], []
    for j in range(steps):
        cols = pl.ds(j * HB, HB)
        ups.append(pltpu.make_async_copy(up_own.at[:, cols], wup.at[0, :, cols], sem_up.at[j]))
        dns.append(pltpu.make_async_copy(dn_own.at[cols, :], wdn.at[0, cols, :], sem_dn.at[j]))
    for r, (a_ref, b_ref) in enumerate(quads):
        place = sc[2] ^ r
        cols = pl.ds(pl.multiple_of(blk * place, 128), blk)
        ups.append(
            pltpu.make_async_copy(
                a_ref.at[pl.ds(0, width), :], wup.at[1, :, cols], sem_up.at[steps + r]
            )
        )
        rows = pl.ds(pl.multiple_of(blk * (sc[4] ^ r), 16), blk)
        dns.append(pltpu.make_async_copy(b_ref, wdn.at[1, rows, :], sem_dn.at[steps + r]))
    return ups, dns


def await_weights(j, steps, copies):
    if j < steps:
        copies[j].wait()
    elif j == steps:
        for copy in copies[steps:]:
            copy.wait()


def block_of(j, steps):
    return j // steps, slice((j % steps) * HB, (j % steps + 1) * HB)


def forward_kernel(
    sc, lens, packed, mixed_own, mixed_other, cot, ow_own, vectors, up_bias, pool, order,
    up_own, dn_own, a0, a1, a2, a3, b0, b1, b2, b3,
    out, pooled, grad2, smalls, ow_out, nrel_out, slope_out, scaled1_out, inv1_out, dn_keep, dn_send,
    wup, wdn, ow_other, ub, act, slope, scaled1, nrel, dnk, dns,
    sem_up, sem_dn, sem_ow, sem_ub, sem_out,
):
    width, hid = wup.shape[1], wup.shape[2]
    mid, blk, steps = width // 2, hid // 4, hid // HB
    piece = ow_own.shape[0] // 4
    out_bias, attn_gain, attn_shift, down_bias, ffn_gain, ffn_shift = (
        vectors[i : i + 1, :] for i in range(6)
    )
    quads = ((a0, b0), (a1, b1), (a2, b2), (a3, b3))
    small_in = []
    for r, (a_ref, _) in enumerate(quads):
        place = sc[2] ^ r
        rows = pl.ds(pl.multiple_of(piece * place, 16), piece)
        for c in range(2):
            small_in.append(
                pltpu.make_async_copy(
                    a_ref.at[pl.ds(width + c * piece, piece), :],
                    ow_other.at[rows, pl.ds(c * blk, blk)],
                    sem_ow.at[2 * r + c],
                )
            )
        small_in.append(
            pltpu.make_async_copy(
                a_ref.at[pl.ds(width + 2 * piece, 16), :],
                ub.at[:, pl.ds(pl.multiple_of(blk * place, 128), blk)],
                sem_ub.at[r],
            )
        )
    ups, dns_in = weight_copies(sc, up_own, dn_own, quads, wup, wdn, sem_up, sem_dn)
    for copy in small_in:
        copy.start()
    for j in range(steps):
        ups[j].start()
        dns_in[j].start()
    for copy in ups[steps:] + dns_in[steps:]:
        copy.start()
    copies = []

    def store(source, target):
        copies.append(pltpu.make_async_copy(source, target, sem_out.at[len(copies)]))
        copies[-1].start()

    for copy in small_in:
        copy.wait()
    store(ow_other, ow_out)
    resid = (
        packed[...].astype(f32)
        + dot(mixed_own[...], ow_own[...], NN)
        + dot(mixed_other[...], ow_other[...], NN)
        + out_bias
    )
    center = resid - jnp.mean(resid, axis=-1, keepdims=True)
    inv1 = lax.rsqrt(jnp.mean(center * center, axis=-1, keepdims=True) + EPS)
    inv1_out[...] = jnp.broadcast_to(inv1, inv1_out.shape)
    norm = center * inv1
    scaled1[...] = norm
    store(scaled1, scaled1_out)
    normed1 = norm * attn_gain + attn_shift
    low = normed1.astype(bf16)
    nrel[...] = dot(low, order[...], NN).astype(bf16)
    store(nrel, nrel_out)
    total = normed1 + down_bias

    def pre_act(j):
        side, cols = block_of(j, steps)
        await_weights(j, steps, ups)
        if side == 0:
            bias = up_bias[:, cols]
        else:
            three = ub[:, cols].astype(f32)
            bias = three[0:1] + three[1:2] + three[2:3]
        return dot(low, wup[side, :, cols], NN) + bias

    for j in range(2 * steps):
        side, cols = block_of(j, steps)
        here = pre_act(j)
        value, deriv = gelu_pair(here)
        value = value.astype(bf16)
        act[j] = value
        slope[j] = deriv.astype(bf16)
        store(slope.at[j], slope_out.at[j])
        await_weights(j, steps, dns_in)
        total = total + dot(value, wdn[side, cols, :], NN)
    center = total - jnp.mean(total, axis=-1, keepdims=True)
    inv2 = lax.rsqrt(jnp.mean(center * center, axis=-1, keepdims=True) + EPS)
    scaled2 = center * inv2
    result = scaled2 * ffn_gain + ffn_shift
    high = result.astype(bf16)
    out[...] = high
    rest = (result - high.astype(f32)).astype(bf16)
    sums = dot(pool[...], high, NN) + dot(pool[...], rest, NN)
    row = lax.broadcasted_iota(i32, (16, 1), 0)
    scale = jnp.zeros((16, 1), f32)
    for c in range(lens.shape[1]):
        scale = jnp.where(row == c, 1.0 / lens[0, c].astype(f32), scale)
    pooled[...] = sums * scale

    grad = cot[...].astype(f32)
    smalls[1:2, :] = jnp.sum(grad * scaled2, axis=0, keepdims=True)
    smalls[2:3, :] = jnp.sum(grad, axis=0, keepdims=True)
    smalls[3:8, :] = jnp.zeros((5, width), f32)
    grad = grad * ffn_gain
    grad = inv2 * (
        grad
        - jnp.mean(grad, axis=-1, keepdims=True)
        - scaled2 * jnp.mean(grad * scaled2, axis=-1, keepdims=True)
    )
    smalls[0:1, :] = jnp.sum(grad, axis=0, keepdims=True)
    grad2[...] = grad
    grel = dot(grad.astype(bf16), order[...], NN).astype(bf16)
    for j in range(2 * steps):
        grad = dot(grel, act[j], TN).astype(bf16)
        both = slice(j * HB, (j + 1) * HB)
        dns[:, both] = grad[mid:]
        store(dns.at[:, both], dn_send.at[:, both])
        dnk[:, both] = grad[:mid]
        store(dnk.at[:, both], dn_keep.at[:, both])
    for copy in copies:
        copy.wait()


def forward(sc, lens, packed, mixed_own, mixed_other, cot, ow, vectors, up_bias, pool, order, up, dn, quads):
    half = packed.shape[0] // 2
    width, hid = up.shape
    group = ow.shape[0]
    steps, mid = hid // HB, width // 2
    blocks = (2 * steps, half, HB)
    outs = [
        ((half, width), bf16),
        ((16, width), f32),
        ((half, width), f32),
        ((8, width), f32),
        ((group, width), bf16),
        ((half, width), bf16),
        (blocks, bf16),
        ((half, width), f32),
        ((half, 128), f32),
        ((mid, 2 * hid), bf16),
        ((mid, 2 * hid), bf16),
    ]
    args = (
        lens, packed, mixed_own, mixed_other, cot, ow, vectors, up_bias, pool, order, up, dn,
        *[a for a, _ in quads], *[b for _, b in quads],
    )
    return call(
        forward_kernel, "forward", 25, sc, args,
        [
            pl.BlockSpec(memory_space=pltpu.SMEM),
            pl.BlockSpec((half, width), lambda t, s: (s[0], 0)),
            full((half, group)),
            full((half, group)),
            full((half, width)),
            full((group, width)),
            full(vectors.shape),
            full((1, hid)),
            pl.BlockSpec((16, half), lambda t, s: (0, s[0])),
            full((width, width)),
        ]
        + [ANY] * 10,
        outs,
        [full(x) for x, _ in outs[:4]] + [ANY] * 4 + [full((half, 128))] + [ANY] * 2,
        [
            pltpu.VMEM((2, width, hid), bf16),
            pltpu.VMEM((2, hid, width), bf16),
            pltpu.VMEM((group, width), bf16),
            pltpu.VMEM((16, hid), bf16),
            pltpu.VMEM(blocks, bf16),
            pltpu.VMEM(blocks, bf16),
            pltpu.VMEM((half, width), f32),
            pltpu.VMEM((half, width), bf16),
            pltpu.VMEM((mid, 2 * hid), bf16),
            pltpu.VMEM((mid, 2 * hid), bf16),
            pltpu.SemaphoreType.DMA((steps + 4,)),
            pltpu.SemaphoreType.DMA((steps + 4,)),
            pltpu.SemaphoreType.DMA((8,)),
            pltpu.SemaphoreType.DMA((4,)),
            pltpu.SemaphoreType.DMA((6 * steps + 3,)),
        ],
    )


def backward_kernel(
    per, sc, tabs, grad2, pooled, smalls2, ow_own, ow_other, inv1, vectors, order, mixed_own,
    mixed_other, nrel, scaled1, slope_in, up_own, dn_own, a0, a1, a2, a3, b0, b1, b2, b3,
    send, gm_own, g1b, lines, up_keep, up_send,
    wup, wdn, slope, upk, ups, smalls, bias_sums, sem_up, sem_dn, sem_in, sem_out,
):
    width, hid = wup.shape[1], wup.shape[2]
    mid, steps = width // 2, hid // HB
    tokens, group = mixed_own.shape
    attn_gain = vectors[1:2, :]
    quads = ((a0, b0), (a1, b1), (a2, b2), (a3, b3))
    ups_in, dns_in = weight_copies(sc, up_own, dn_own, quads, wup, wdn, sem_up, sem_dn)
    slopes = [
        pltpu.make_async_copy(slope_in.at[j], slope.at[j], sem_in.at[j]) for j in range(2 * steps)
    ]
    for j in range(steps):
        dns_in[j].start()
        slopes[j].start()
        ups_in[j].start()
    for copy in dns_in[steps:] + slopes[steps:] + ups_in[steps:]:
        copy.start()
    copies = []

    def store(source, target):
        copies.append(pltpu.make_async_copy(source, target, sem_out.at[len(copies)]))
        copies[-1].start()

    low = grad2[...].astype(bf16)
    total = grad2[...]
    bias_sums[...] = jnp.zeros_like(bias_sums)

    def grad_act(j):
        side, cols = block_of(j, steps)
        await_weights(j, steps, dns_in)
        return dot(low, wdn[side, cols, :], NT)

    for j in range(2 * steps):
        side, cols = block_of(j, steps)
        here = grad_act(j)
        slopes[j].wait()
        pre = (here * slope[j].astype(f32)).astype(bf16)
        await_weights(j, steps, ups_in)
        total = total + dot(pre, wup[side, :, cols], NT)
        bias_sums[side : side + 1, cols] = jnp.sum(pre.astype(f32), axis=0, keepdims=True)
        grad = dot(nrel[...], pre, TN).astype(bf16)
        upk[side, :, cols] = grad[:mid]
        ups[side, :, cols] = grad[mid:]
        store(upk.at[side, :, cols], up_keep.at[side, :, cols])
        store(ups.at[side, :, cols], up_send.at[side, :, cols])
    norm = scaled1[...]
    smalls[1:2, :] = jnp.sum(total * norm, axis=0, keepdims=True)
    smalls[2:3, :] = jnp.sum(total, axis=0, keepdims=True)
    smalls[3:6, :] = smalls2[0:3, :]
    smalls[6:16, :] = jnp.zeros((10, width), f32)
    grad = total * attn_gain
    grad = inv1[:, 0:1] * (
        grad
        - jnp.mean(grad, axis=-1, keepdims=True)
        - norm * jnp.mean(grad * norm, axis=-1, keepdims=True)
    )
    smalls[0:1, :] = jnp.sum(grad, axis=0, keepdims=True)
    low = grad.astype(bf16)
    g1b[...] = low
    send[0:tokens, :] = dot(low, ow_other[...], NT).astype(bf16)
    gm_own[...] = dot(low, ow_own[...], NT).astype(bf16)
    sums = pooled[...].astype(bf16)
    send[tokens : tokens + 16, :] = sums[:, :group]
    send[tokens + 16 : tokens + 32, :] = sums[:, group:]

    low = dot(low, order[...], NN).astype(bf16)
    for side, mixed in enumerate((mixed_own, mixed_other)):
        grad = dot(low, mixed[...], TN).astype(bf16)
        upk[side, :, hid:] = grad[:mid]
        ups[side, :, hid:] = grad[mid:]
        tail = slice(hid, hid + group)
        store(upk.at[side, :, tail], up_keep.at[side, :, tail])
        store(ups.at[side, :, tail], up_send.at[side, :, tail])
    rows = dot(smalls[...].astype(bf16), order[...], NN)
    pieces = []
    source = (tabs[0:1, :] ^ sc[3]) * (2 * per) + tabs[1:2, :]
    for part in range(hid // width):
        spread = onehot(source + part * per == lax.broadcasted_iota(i32, (hid, width), 0))
        pieces.append(dot(bias_sums[...].astype(bf16), spread, NN))
    lines[...] = jnp.concatenate([rows[:6]] + [x[0:1] for x in pieces] + [rows[8:]], axis=0)
    other = jnp.concatenate(
        [rows[:6]] + [x[1:2] for x in pieces] + [rows[8:]], axis=0
    ).astype(bf16)
    send[tokens + 32 : tokens + 48, :] = other[:, :group]
    send[tokens + 48 : tokens + 64, :] = other[:, group:]
    for copy in copies:
        copy.wait()


def backward(
    per, sc, tabs, grad2, pooled, smalls, ow, ow_other, inv1, vectors, order, mixed_own, mixed_other,
    nrel, scaled1, slope, up, dn, quads,
):
    half, width = grad2.shape
    hid = up.shape[1]
    group = ow.shape[0]
    steps, mid = hid // HB, width // 2
    wide = (2, mid, hid + group)
    outs = [
        ((half + 64, group), bf16),
        ((half, group), bf16),
        ((half, width), bf16),
        ((16, width), f32),
        (wide, bf16),
        (wide, bf16),
    ]
    args = (
        tabs, grad2, pooled, smalls, ow, ow_other, inv1, vectors, order, mixed_own, mixed_other,
        nrel, scaled1, slope, up, dn, *[a for a, _ in quads], *[b for _, b in quads],
    )
    return call(
        functools.partial(backward_kernel, per), "backward", 18, sc, args,
        [full(x.shape) for x in args[:13]] + [ANY] * 11,
        outs,
        [full(x) for x, _ in outs[:4]] + [ANY] * 2,
        [
            pltpu.VMEM((2, width, hid), bf16),
            pltpu.VMEM((2, hid, width), bf16),
            pltpu.VMEM(slope.shape, bf16),
            pltpu.VMEM(wide, bf16),
            pltpu.VMEM(wide, bf16),
            pltpu.VMEM((16, width), f32),
            pltpu.VMEM((16, hid), f32),
            pltpu.SemaphoreType.DMA((steps + 4,)),
            pltpu.SemaphoreType.DMA((steps + 4,)),
            pltpu.SemaphoreType.DMA((2 * steps,)),
            pltpu.SemaphoreType.DMA((4 * steps + 4,)),
        ],
    )


def chip_sums(sc, name, keep, recv, views):
    dims = [d for d, _ in views]

    def kernel(sc, keep, recv, *refs):
        outs, loads, sems = refs[: len(dims)], refs[len(dims) : -1], refs[-1]
        copies = []
        for number, (_, view) in enumerate(views):
            for source in (keep, recv):
                copies.append(
                    pltpu.make_async_copy(
                        source.at[view], loads[len(copies)], sems.at[len(copies)]
                    )
                )
                copies[-1].start()
        for number, out in enumerate(outs):
            copies[2 * number].wait()
            copies[2 * number + 1].wait()
            one, two = loads[2 * number], loads[2 * number + 1]
            out[...] = (one[...].astype(f32) + two[...].astype(f32)).astype(bf16)

    return call(
        kernel, name, ORDERED, sc, (keep, recv), [ANY] * 2, [(d, bf16) for d in dims],
        [full(d) for d in dims],
        [pltpu.VMEM(d, bf16) for d in dims for _ in range(2)]
        + [pltpu.SemaphoreType.DMA((2 * len(dims),))],
    )


def swap(value, axis, bit):
    count = lax.axis_size(axis)
    return lax.ppermute(value, axis, [(i, i ^ (1 << bit)) for i in range(count)])


def pin(*values):
    return lax.optimization_barrier(values)


def add_low(left, right):
    return (left.astype(f32) + right.astype(f32)).astype(bf16)


def body(
    hidden,
    source_index,
    crop_lengths,
    deleted,
    qkv_weight,
    qv_bias,
    out_weight,
    out_bias,
    attn_gain,
    attn_shift,
    up_weight,
    up_bias,
    down_weight,
    down_bias,
    ffn_gain,
    ffn_shift,
    cotangent,
):
    length, width = hidden.shape
    crops = crop_lengths.shape[1]
    group = out_weight.shape[0]
    hid = up_weight.shape[1]
    half = length // 2
    n_dp, n_rep = lax.axis_size("dp"), lax.axis_size("rep")
    dp_bits, rep_bits = n_dp.bit_length() - 1, n_rep.bit_length() - 1
    shards = n_dp * n_rep
    per = width // shards
    h, dp = lax.axis_index("head"), lax.axis_index("dp")
    rep_index = lax.axis_index("rep")
    me = dp * n_rep + rep_index
    sc = jnp.stack([h, 1 - h, dp & 3, me, (dp & 1) + 2 * (rep_index & 1)]).astype(i32)

    stages = [("dp", b) for b in range(dp_bits)] + [("rep", b) for b in range(rep_bits)]
    block = np.zeros(shards, np.int32)
    for number, (axis, bit) in enumerate(stages):
        value = (np.arange(shards) >> (len(stages) - 1 - number)) & 1
        block |= (value << (bit + (rep_bits if axis == "dp" else 0))).astype(np.int32)
    row = np.arange(width)
    tabs = np.zeros((8, width), np.int32)
    tabs[0] = block[row // per]
    tabs[1] = row % per
    tabs = jnp.asarray(tabs)

    first, second = bundle(sc, up_bias, up_weight, down_weight, out_weight)
    first = swap(first, "head", 0)
    second = swap(second, "head", 0)
    packed, q, k, v, e_other, o_other, recip_other, segrow, code, pool = prepare(
        sc, crop_lengths, hidden, source_index, deleted, qkv_weight, qv_bias
    )
    mixed_recv = swap(o_other, "head", 0)
    first, o_other = pin(first, o_other)
    first_y = swap(first, "dp", 1)
    q_late, first = pin(q, first)
    e_own, o_own, recip_own = attend(sc, q_late, k, v, segrow, code)
    second, o_own = pin(second, o_own)
    second_y = swap(second, "rep", 0)
    packed_late, mixed_recv, second = pin(packed, mixed_recv, second)
    pt, order = ordered(per, sc, tabs, packed_late)
    first, first_y, second_y, pt = pin(first, first_y, second_y, pt)
    first_c, first_cy = swap(first, "dp", 0), swap(first_y, "dp", 0)
    second_c, second_cy = swap(second, "dp", 0), swap(second_y, "dp", 0)
    quads = [(first, second), (first_c, second_c), (first_y, second_y), (first_cy, second_cy)]
    vectors = jnp.stack(
        [out_bias, attn_gain, attn_shift, down_bias, ffn_gain, ffn_shift, ffn_shift, ffn_shift]
    )
    (
        output, pooled, grad2, smalls, ow_other, nrel, slope, scaled1, inv1, dn_keep, dn_send
    ) = forward(
        sc, crop_lengths, packed, o_own, mixed_recv, cotangent, out_weight, vectors, up_bias, pool,
        order, up_weight, down_weight, quads,
    )
    send, gm_own, g1b, lines, up_keep, up_send = backward(
        per, sc, tabs, grad2, pooled, smalls, out_weight, ow_other, inv1, vectors, order, o_own,
        mixed_recv, nrel, scaled1, slope, up_weight, down_weight, quads,
    )
    part, cut = width // 4, 1024
    recv = swap(send, "head", 0)
    dn_recv, gm_own = pin(swap(dn_send, "dp", 0), gm_own)
    (dn_next,) = chip_sums(
        sc, "down_sums", dn_keep, dn_recv, [((part, 2 * hid), (pl.ds(part, part),))]
    )
    gm_own, dn_next = pin(gm_own, dn_next)
    up_recv, dn_next = pin(swap(up_send, "dp", 0), dn_next)
    tall = (2, n_dp // 2, 2, n_rep // 2 * per, hid + group)
    a_next, b_next = chip_sums(
        sc, "up_sums", up_keep.reshape(tall), up_recv.reshape(tall),
        [
            (
                (n_dp // 2, 2, n_rep // 2 * per, cut),
                (1, slice(None), slice(None), slice(None), pl.ds(0, cut)),
            ),
            (
                (2, n_dp // 2, n_rep // 2 * per, hid + group - cut),
                (slice(None), slice(None), 1, slice(None), pl.ds(cut, hid + group - cut)),
            ),
        ],
    )
    a_next = a_next.reshape(2 * part, cut)
    gm_own, a_next, b_next = pin(gm_own, a_next, b_next)
    dq_own, dk_own, dv_own = attend_back(sc, gm_own, o_own, recip_own, q, k, v, e_own)
    recv, dq_own = pin(recv, dq_own)
    qkv_keep, qkv_send, gq = finish(
        sc, recv, o_other, recip_other, q, k, v, (dq_own, dk_own, dv_own), pt, lines, order, e_other
    )
    hidden_other, hidden_own = input_grad(sc, source_index, gq, qkv_weight, g1b)
    hidden_recv = swap(hidden_other, "head", 0)

    last = [hidden_own]

    def arrive(value):
        return pin(value, last[0])[0].astype(f32)

    def keep_low(value):
        last[0] = value.astype(bf16)
        return last[0]

    def low_half(value, axis, bit):
        rows = value.shape[0] // 2
        return keep_low(value[:rows].astype(f32) + arrive(swap(value[rows:], axis, bit)))

    def three(keep, recv, late):
        return keep_low(keep.astype(f32) + recv.astype(f32) + arrive(late))

    later = stages[1:]
    dp_later = [x for x in later if x[0] == "dp"]
    rep_all = [x for x in later if x[0] == "rep"]
    down_swap = swap(dn_next, *later[0])
    a_swap = swap(a_next, "head", 0)
    b_swap = swap(b_next, *rep_all[0])
    qkv_swap = swap(qkv_send, "dp", 0)
    down = three(dn_keep[:part], dn_recv[:part], down_swap)
    up_b = three(
        up_keep.reshape(tall)[:, :, 0, :, cut:], up_recv.reshape(tall)[:, :, 0, :, cut:], b_swap
    )
    up_a = three(up_keep[0, :, :cut], up_recv[0, :, :cut], a_swap)
    qkv = keep_low(qkv_keep.astype(f32) + arrive(qkv_swap))
    down = low_half(down, *later[1])
    up_a = low_half(up_a, *later[0])
    up_b = keep_low(up_b[0].astype(f32) + arrive(swap(up_b[1], "head", 0)))
    qkv = low_half(qkv, *later[0])
    grad_hidden = hidden_own.astype(f32) + arrive(hidden_recv)
    last[0] = grad_hidden
    for axis, bit in dp_later:
        up_b = low_half(up_b, axis, bit)
    for axis, bit in dp_later[1:]:
        up_a = low_half(up_a, axis, bit)
    up_a = low_half(up_a, *rep_all[0])
    up = jnp.concatenate([up_a, up_b[0]], axis=1)
    for axis, bit in later[2:]:
        down = low_half(down, axis, bit)
    for axis, bit in later[1:-1]:
        qkv = low_half(qkv, axis, bit)
    for axis, bit in rep_all[1:-1]:
        up = low_half(up, axis, bit)
    axis, bit = later[-1]
    down = down[:, :hid].astype(f32) + arrive(swap(down[:, hid:], "head", 0))
    last[0] = down
    up = up[:per].astype(f32) + arrive(swap(up[per:], axis, bit))
    last[0] = up
    keep, out = qkv[:per], arrive(swap(qkv[per:], axis, bit))
    wide = 3 * group
    qkv_grad = keep[:, :wide].astype(f32) + out[:, :wide]
    extra = (keep[:, wide:].astype(f32) + out[:, wide:]).T
    small = lax.dynamic_slice_in_dim(extra[:6], h * (per // 2), per // 2, 1)
    pooled_other = recv[half:].astype(f32)
    pooled_other = jnp.concatenate([pooled_other[:crops], pooled_other[16 : 16 + crops]], axis=1)
    return (
        output,
        pooled[:crops] + pooled_other,
        grad_hidden,
        qkv_grad,
        extra[15:16],
        up[:, hid:].T,
        small[0],
        small[1],
        small[2],
        up[:, :hid],
        extra[6 : 6 + hid // width].reshape(1, hid // shards),
        down.T,
        small[3],
        small[4],
        small[5],
    )


def solution(mesh):
    rows = P(("dp", "rep"), None)
    every = P(("dp", "rep", "head"), None)
    vector = P(("dp", "rep", "head"))
    return jax.shard_map(
        body,
        mesh=mesh,
        in_specs=(
            rows,
            rows,
            rows,
            rows,
            P(None, "head"),
            P("head", None),
            P("head", None),
            P(),
            P(),
            P(),
            P(None, "head"),
            P("head", None),
            P("head", None),
            P(),
            P(),
            P(),
            every,
        ),
        out_specs=(
            every,
            rows,
            every,
            P(("dp", "rep"), "head"),
            P("head", ("dp", "rep")),
            P("head", ("dp", "rep")),
            vector,
            vector,
            vector,
            P(("dp", "rep"), "head"),
            P("head", ("dp", "rep")),
            P("head", ("dp", "rep")),
            vector,
            vector,
            vector,
        ),
        check_vma=False,
    )
```

```python
import functools
import math

import jax
import jax.numpy as jnp
import numpy as np
from jax import lax
from jax.experimental import pallas as pl
from jax.experimental.pallas import tpu as pltpu
from jax.sharding import PartitionSpec as P

HEAD_DIM = 64
CROP_MAX = 256
EPS = 1e-12
MASKED = -1e30
NN = ((1,), (0,))
NT = ((1,), (1,))
TN = ((0,), (0,))
f32 = jnp.float32
bf16 = jnp.bfloat16
i32 = jnp.int32
NEEDS = {
    "bundle": 60,
    "prepare": 26,
    "attend": 18,
    "ordered": 14,
    "forward": 60,
    "backward": 60,
    "attend_back": 24,
    "finish": 30,
    "input_grad": 24,
    "down_sums": 8,
    "up_sums": 10,
}
QB = CROP_MAX
HB = 512
SCALE = 0.4
ORDERED = 60

shape = jax.ShapeDtypeStruct
ANY = pl.BlockSpec(memory_space=pl.ANY)


def dot(left, right, how):
    return lax.dot_general(left, right, (how, ((), ())), preferred_element_type=f32)


def cost(micros):
    return pl.CostEstimate(
        flops=int(SCALE * micros * 1.1e9), bytes_accessed=1024, transcendentals=0
    )


def full(dims):
    return pl.BlockSpec(dims, lambda *_: (0,) * len(dims))


def call(kernel, name, micros, sc, args, in_specs, outs, out_specs, scratch):
    return pl.pallas_call(
        kernel,
        grid_spec=pltpu.PrefetchScalarGridSpec(
            num_scalar_prefetch=1,
            grid=(1,),
            in_specs=in_specs,
            out_specs=out_specs,
            scratch_shapes=scratch,
        ),
        out_shape=[shape(s, d) for s, d in outs],
        compiler_params=pltpu.CompilerParams(vmem_limit_bytes=NEEDS[name] * 1024 * 1024),
        cost_estimate=cost(micros),
        name=name,
    )(sc, *args)


def onehot(hit):
    return jnp.where(hit, 1.0, 0.0).astype(bf16)


def gelu_pair(u):
    phi = 0.5 + 0.5 * lax.erf(u * (1.0 / math.sqrt(2.0)))
    bell = jnp.exp2((u * u) * (-0.5 / math.log(2.0))) * (1.0 / math.sqrt(2.0 * math.pi))
    return u * phi, phi + u * bell


def order_matrix(sc, tabs, width, per):
    source = (tabs[0:1, :] ^ sc[3]) * per + tabs[1:2, :]
    return onehot(source == lax.broadcasted_iota(i32, (width, width), 0))


def bundle_kernel(sc, up_bias, up, dn, ow, first, second, sems):
    quarter = sc[2]
    width, blk = up.shape[0], second.shape[0]
    piece = ow.shape[0] // 4
    cols = pl.ds(pl.multiple_of(quarter * blk, 128), blk)
    slab = pl.ds(pl.multiple_of(quarter * piece, 16), piece)
    copies = [
        pltpu.make_async_copy(up.at[:, cols], first.at[pl.ds(0, width), :], sems.at[0]),
        pltpu.make_async_copy(
            ow.at[slab, pl.ds(0, blk)], first.at[pl.ds(width, piece), :], sems.at[1]
        ),
        pltpu.make_async_copy(
            ow.at[slab, pl.ds(blk, blk)], first.at[pl.ds(width + piece, piece), :], sems.at[2]
        ),
        pltpu.make_async_copy(
            dn.at[pl.ds(pl.multiple_of(sc[4] * blk, 16), blk), :], second, sems.at[3]
        ),
    ]
    for copy in copies:
        copy.start()
    bias = up_bias[0:1, cols]
    high = bias.astype(bf16).astype(f32)
    mid = (bias - high).astype(bf16).astype(f32)
    low = bias - high - mid
    first[width + 2 * piece :, :] = jnp.concatenate(
        [high, mid, low, jnp.zeros((13, blk), f32)], axis=0
    ).astype(bf16)
    for copy in copies:
        copy.wait()


def bundle(sc, up_bias, up, dn, ow):
    width, hid = up.shape
    blk = hid // 4
    rows = width + ow.shape[0] // 2 + 16
    return call(
        bundle_kernel, "bundle", 2, sc, (up_bias, up, dn, ow),
        [full(up_bias.shape), ANY, ANY, ANY],
        [((rows, blk), bf16), ((blk, width), bf16)],
        [full((rows, blk)), full((blk, width))],
        [pltpu.SemaphoreType.DMA((4,))],
    )


def half_blocks(p):
    half = 2 * QB
    return (
        (pl.multiple_of(QB * p, QB), pl.multiple_of(half * p, QB), 2 * QB, 0, pl.multiple_of(QB * p, QB)),
        (pl.multiple_of(QB - QB * p, QB), pl.multiple_of(QB * p, QB), 3 * QB, 2 * QB, 0),
    )


def fill_cap(p, segrow, code, cap):
    for qs, ks, count, off, _ in half_blocks(p):
        first = pl.multiple_of(2 * QB * p + qs, QB)
        keys = code[pl.ds(ks, count), :]
        keys = jnp.concatenate([keys] * (QB // 128), axis=1)
        ask = segrow[0:1, pl.ds(first, QB)]
        shift = lax.broadcasted_iota(i32, (count, QB), 0) - lax.broadcasted_iota(
            i32, (count, QB), 1
        )
        allowed = (keys == ask) | (shift == first - ks)
        cap[off : off + count, :] = jnp.where(allowed, 3e38, MASKED)


def attend_pair(p, base, t, q, k, v, cap, e, mixed, recip):
    lane = lax.broadcasted_iota(i32, (QB, 128), 1) < HEAD_DIM
    cols = slice(t * 128, (t + 1) * 128)
    for qs, ks, count, off, _ in half_blocks(p):
        q_blk = q[pl.ds(pl.multiple_of(base + qs, QB), QB), cols]
        k_win = k[pl.ds(ks, count), cols]
        v_win = v[pl.ds(ks, count), cols]
        v_lane = lax.broadcasted_iota(i32, (count, 128), 1) < HEAD_DIM
        outs, recips = [], []
        for a in range(2):
            q_one = jnp.where(lane == (a == 0), q_blk, jnp.zeros_like(q_blk))
            s = jnp.minimum(dot(k_win, q_one, NT), cap[off : off + count, :])
            weights = jnp.exp(s - jnp.max(s, axis=0, keepdims=True)).astype(bf16)
            e[t, a, off : off + count, :] = weights
            v_one = jnp.where(v_lane == (a == 0), v_win, jnp.ones_like(v_win))
            o = dot(v_one, weights, TN)
            value, total = o[:HEAD_DIM], o[HEAD_DIM:]
            if a == 1:
                value, total = total, value
            inv = 1.0 / total
            outs.append(value * inv)
            recips.append(inv)
        mixed[pl.ds(qs, QB), cols] = jnp.transpose(jnp.concatenate(outs, axis=0)).astype(bf16)
        recip[pl.ds(qs, QB), cols] = jnp.transpose(jnp.concatenate(recips, axis=0))


def prepare_kernel(
    sc, lens, hidden, idx, dele, w, qv_bias,
    packed_hbm, q_hbm, k_hbm, v_hbm, e_hbm, mixed, recip, segrow, code, pool,
    packed, q, k, v, e, cap, sems,
):
    length, width = hidden.shape
    group = q.shape[1]
    idx_col = jnp.transpose(jnp.broadcast_to(idx[...].astype(f32), (8, length)))[:, :1]
    lane = lax.broadcasted_iota(i32, (8, length), 1)
    seg = jnp.zeros((8, length), f32)
    end = jnp.int32(0)
    for c in range(lens.shape[1]):
        end = end + lens[0, c]
        seg = seg + jnp.where(lane >= end, 1.0, 0.0)
    segrow[...] = seg
    code_row = jnp.where(jnp.broadcast_to(dele[...], (8, length)) == 0, seg, -1.0)
    code[...] = jnp.broadcast_to(jnp.transpose(code_row)[:, :1], code.shape)
    crop_row = lax.broadcasted_iota(i32, pool.shape, 0).astype(f32)
    pool[...] = onehot(crop_row == jnp.broadcast_to(code_row[:1], pool.shape))
    copies = []
    for i in range(length // QB):
        rows = slice(i * QB, (i + 1) * QB)
        place = lax.broadcasted_iota(i32, (QB, length), 1).astype(f32)
        pk = dot(onehot(idx_col[rows] == place), hidden[...], NN).astype(bf16)
        packed[rows, :] = pk
        out = dot(pk, w[...], NN)
        q[rows, :] = (out[:, :group] + qv_bias[:, :group]).astype(bf16) * jnp.asarray(
            HEAD_DIM**-0.5, bf16
        )
        k[rows, :] = out[:, group : 2 * group].astype(bf16)
        v[rows, :] = (out[:, 2 * group :] + qv_bias[:, group:]).astype(bf16)
    for number, (source, target) in enumerate(
        ((packed, packed_hbm), (q, q_hbm), (k, k_hbm), (v, v_hbm))
    ):
        copies.append(pltpu.make_async_copy(source, target, sems.at[number]))
        copies[-1].start()
    p = sc[1]
    fill_cap(p, segrow, code, cap)
    for t in range(group // 128):
        attend_pair(p, 2 * QB * p, t, q, k, v, cap, e, mixed, recip)
        copies.append(pltpu.make_async_copy(e.at[t], e_hbm.at[t], sems.at[4 + t]))
        copies[-1].start()
    for copy in copies:
        copy.wait()


def prepare(sc, lens, hidden, idx, dele, w, qv_bias):
    length, width = hidden.shape
    group = w.shape[1] // 3
    half, pairs = length // 2, group // 128
    weights = (pairs, 2, 5 * QB, QB)
    return call(
        prepare_kernel, "prepare", 15, sc, (lens, hidden, idx, dele, w, qv_bias),
        [pl.BlockSpec(memory_space=pltpu.SMEM)]
        + [full(x.shape) for x in (hidden, idx, dele, w, qv_bias)],
        [
            ((length, width), bf16),
            ((length, group), bf16),
            ((length, group), bf16),
            ((length, group), bf16),
            (weights, bf16),
            ((half, group), bf16),
            ((half, group), f32),
            ((8, length), f32),
            ((length, 128), f32),
            ((16, length), bf16),
        ],
        [ANY] * 5
        + [full((half, group)), full((half, group)), full((8, length)), full((length, 128)),
           full((16, length))],
        [
            pltpu.VMEM((length, width), bf16),
            pltpu.VMEM((length, group), bf16),
            pltpu.VMEM((length, group), bf16),
            pltpu.VMEM((length, group), bf16),
            pltpu.VMEM(weights, bf16),
            pltpu.VMEM((5 * QB, QB), f32),
            pltpu.SemaphoreType.DMA((4 + pairs,)),
        ],
    )


def attend_kernel(sc, q, k, v, segrow, code, e_hbm, mixed, recip, e, cap, sems):
    p = sc[0]
    fill_cap(p, segrow, code, cap)
    copies = []
    for t in range(q.shape[1] // 128):
        attend_pair(p, 0, t, q, k, v, cap, e, mixed, recip)
        copies.append(pltpu.make_async_copy(e.at[t], e_hbm.at[t], sems.at[t]))
        copies[-1].start()
    for copy in copies:
        copy.wait()


def attend(sc, q, k, v, segrow, code):
    length, group = q.shape
    half, pairs = length // 2, group // 128
    weights = (pairs, 2, 5 * QB, QB)
    return call(
        attend_kernel, "attend", 9, sc, (q, k, v, segrow, code),
        [pl.BlockSpec((half, group), lambda t, s: (s[0], 0))]
        + [full(x.shape) for x in (k, v, segrow, code)],
        [(weights, bf16), ((half, group), bf16), ((half, group), f32)],
        [ANY, full((half, group)), full((half, group))],
        [
            pltpu.VMEM(weights, bf16),
            pltpu.VMEM((5 * QB, QB), f32),
            pltpu.SemaphoreType.DMA((pairs,)),
        ],
    )


def back_pair(p, t, g, o, recip, q, k, v, e, put_dq, put_kv):
    lane = lax.broadcasted_iota(i32, (QB, 128), 1) < HEAD_DIM
    cols = slice(t * 128, (t + 1) * 128)
    pick = onehot(
        (lax.broadcasted_iota(i32, (16, 128), 1) < HEAD_DIM)
        == (lax.broadcasted_iota(i32, (16, 128), 0) == 0)
    )
    outer, inner = half_blocks(p)
    for number, (qs, ks, count, off, loc) in enumerate((inner, outer)):
        rows = pl.ds(qs, QB)
        grad = g[rows, cols].astype(f32) * recip[rows, cols]
        both = grad * o[rows, cols].astype(f32)
        high = both.astype(bf16)
        rest = (both - high.astype(f32)).astype(bf16)
        delta = dot(pick, high, NT) + dot(pick, rest, NT)
        grad = grad.astype(bf16)
        q_blk = q[rows, cols]
        k_win = k[pl.ds(ks, count), cols]
        v_win = v[pl.ds(ks, count), cols]
        dk = jnp.zeros((count, 128), f32)
        dv = jnp.zeros((count, 128), f32)
        dqs = []
        for a in range(2):
            g_one = jnp.where(lane == (a == 0), grad, jnp.zeros_like(grad))
            q_one = jnp.where(lane == (a == 0), q_blk, jnp.zeros_like(q_blk))
            weights = e[t, a, off : off + count, :]
            ds = (
                weights.astype(f32) * (dot(v_win, g_one, NT) - delta[a : a + 1])
            ).astype(bf16)
            dk += dot(ds, q_one, NN)
            dv += dot(weights, g_one, NN)
            dqs.append(dot(k_win, ds, TN)[a * HEAD_DIM : (a + 1) * HEAD_DIM])
        dq = jnp.transpose(jnp.concatenate(dqs, axis=0)) * HEAD_DIM ** (-0.5)
        put_dq(qs, cols, dq.astype(bf16))
        put_kv(number, loc, ks, count, cols, dk, dv)


def back_kernel(sc, g, o, recip, q, k, v, e_hbm, dq, dk, dv, e, sems):
    p = sc[0]
    pairs = q.shape[1] // 128
    loads = [pltpu.make_async_copy(e_hbm.at[t], e.at[t], sems.at[t]) for t in range(pairs)]
    for load in loads:
        load.start()

    def put_dq(qs, cols, value):
        dq[pl.ds(qs, QB), cols] = value

    def put_kv(number, loc, ks, count, cols, dk_part, dv_part):
        for ref, value in ((dk, dk_part), (dv, dv_part)):
            if number == 0:
                ref[:, cols] = value
            else:
                ref[pl.ds(loc, count), cols] += value

    for t in range(pairs):
        loads[t].wait()
        back_pair(p, t, g, o, recip, q, k, v, e, put_dq, put_kv)


def attend_back(sc, g, o, recip, q, k, v, e):
    length, group = q.shape
    half = length // 2
    return call(
        back_kernel, "attend_back", 0.1, sc, (g, o, recip, q, k, v, e),
        [full((half, group))] * 3
        + [pl.BlockSpec((half, group), lambda t, s: (s[0], 0)), full(k.shape), full(v.shape), ANY],
        [((half, group), bf16), ((3 * QB, group), f32), ((3 * QB, group), f32)],
        [full((half, group)), full((3 * QB, group)), full((3 * QB, group))],
        [pltpu.VMEM(e.shape, bf16), pltpu.SemaphoreType.DMA((group // 128,))],
    )


def finish_kernel(
    sc, g, o, recip, q, k, v, dq_own, dk_own, dv_own, pt, lines, order, e_hbm,
    keep, send, gq, e, ksum, vsum, sems,
):
    h, p = sc[0], sc[1]
    width = pt.shape[1]
    mid = width // 2
    length, group = ksum.shape
    half = length // 2
    pairs = group // 128
    loads = [pltpu.make_async_copy(e_hbm.at[t], e.at[t], sems.at[t]) for t in range(pairs)]
    for load in loads:
        load.start()
    own = pl.ds(pl.multiple_of(half * h, half), half)
    window = pl.ds(pl.multiple_of(QB * h, QB), 3 * QB)
    gq[own, 0:group] = dq_own[...]
    for total, part in ((ksum, dk_own), (vsum, dv_own)):
        total[...] = jnp.zeros_like(total)
        total[window, :] = part[...]

    def put_dq(qs, cols, value):
        gq[pl.ds(pl.multiple_of(half * p + qs, QB), QB), cols] = value

    def put_kv(number, loc, ks, count, cols, dk_part, dv_part):
        ksum[pl.ds(ks, count), cols] += dk_part
        vsum[pl.ds(ks, count), cols] += dv_part

    for t in range(pairs):
        loads[t].wait()
        back_pair(p, t, g, o, recip, q, k, v, e, put_dq, put_kv)
    gq[:, group : 2 * group] = ksum[...].astype(bf16)
    gq[:, 2 * group :] = vsum[...].astype(bf16)
    grads = gq[...]
    grad = dot(pt[...], grads, TN).astype(bf16)
    keep[:, : 3 * group] = grad[:mid]
    send[:, : 3 * group] = grad[mid:]
    sums = jnp.sum(grads.astype(f32), axis=0, keepdims=True)
    sums = jnp.concatenate([sums[:, :group], sums[:, 2 * group :]], axis=1).astype(bf16)
    sums = dot(jnp.broadcast_to(sums, (16, 2 * group)), order[...], NN)
    both = lines[...] + jnp.concatenate(
        [g[half + 32 : half + 48, :], g[half + 48 : half + 64, :]], axis=1
    ).astype(f32)
    both = jnp.where(lax.broadcasted_iota(i32, (16, width), 0) == 15, sums, both).astype(bf16)
    eye = onehot(
        lax.broadcasted_iota(i32, (16, 128), 0) == lax.broadcasted_iota(i32, (16, 128), 1)
    )
    extra = dot(both, eye, TN).astype(bf16)
    keep[:, 3 * group :] = extra[:mid]
    send[:, 3 * group :] = extra[mid:]

def finish(sc, g, o, recip, q, k, v, parts, pt, lines, order, e):
    length, group = q.shape
    half, width = length // 2, pt.shape[1]
    wide = (width // 2, 3 * group + 128)
    args = (g, o, recip, q, k, v, *parts, pt, lines, order, e)
    specs = [full(x.shape) for x in args[:-1]] + [ANY]
    specs[3] = pl.BlockSpec((half, group), lambda t, s: (s[1], 0))
    return call(
        finish_kernel, "finish", 0.1, sc, args, specs,
        [(wide, bf16), (wide, bf16), ((length, 3 * group), bf16)],
        [full(wide), full(wide), full((length, 3 * group))],
        [
            pltpu.VMEM(e.shape, bf16),
            pltpu.VMEM((length, group), f32),
            pltpu.VMEM((length, group), f32),
            pltpu.SemaphoreType.DMA((group // 128,)),
        ],
    )


def input_grad_kernel(sc, idx, gq, w, g1b, hid_other, hid_own, terms):
    h, p = sc[0], sc[1]
    half, length = g1b.shape[0], gq.shape[0]
    for i in range(2):
        rows = slice(i * half, (i + 1) * half)
        mine = jnp.where(h == i, 1.0, 0.0)
        part = dot(gq[rows, :], w[...], NT) + mine * g1b[...].astype(f32)
        terms[rows, :] = part.astype(bf16)
    spot = lax.broadcasted_iota(i32, (half, length), 0)
    hid_other[...] = dot(onehot(spot + half * p == idx[...]), terms[...], NN).astype(bf16)
    hid_own[...] = dot(onehot(spot + half * h == idx[...]), terms[...], NN).astype(bf16)


def input_grad(sc, idx, gq, w, g1b):
    half, width = g1b.shape
    args = (idx, gq, w, g1b)
    return call(
        input_grad_kernel, "input_grad", 0.1, sc, args, [full(x.shape) for x in args],
        [((half, width), bf16)] * 2, [full((half, width))] * 2,
        [pltpu.VMEM((2 * half, width), bf16)],
    )


def ordered_kernel(per, sc, tabs, packed, out, order):
    order[...] = order_matrix(sc, tabs, packed.shape[1], per)
    out[...] = dot(packed[...], order[...], NN).astype(bf16)


def ordered(per, sc, tabs, packed):
    width = packed.shape[1]
    return call(
        functools.partial(ordered_kernel, per), "ordered", ORDERED, sc, (tabs, packed),
        [full(tabs.shape), full(packed.shape)],
        [(packed.shape, bf16), ((width, width), bf16)],
        [full(packed.shape), full((width, width))],
        [],
    )


def weight_copies(sc, up_own, dn_own, quads, wup, wdn, sem_up, sem_dn):
    hid = wup.shape[2]
    width, blk, steps = wup.shape[1], hid // 4, hid // HB
    ups, dns = [], []
    for j in range(steps):
        cols = pl.ds(j * HB, HB)
        ups.append(pltpu.make_async_copy(up_own.at[:, cols], wup.at[0, :, cols], sem_up.at[j]))
        dns.append(pltpu.make_async_copy(dn_own.at[cols, :], wdn.at[0, cols, :], sem_dn.at[j]))
    for r, (a_ref, b_ref) in enumerate(quads):
        place = sc[2] ^ r
        cols = pl.ds(pl.multiple_of(blk * place, 128), blk)
        ups.append(
            pltpu.make_async_copy(
                a_ref.at[pl.ds(0, width), :], wup.at[1, :, cols], sem_up.at[steps + r]
            )
        )
        rows = pl.ds(pl.multiple_of(blk * (sc[4] ^ r), 16), blk)
        dns.append(pltpu.make_async_copy(b_ref, wdn.at[1, rows, :], sem_dn.at[steps + r]))
    return ups, dns


def await_weights(j, steps, copies):
    if j < steps:
        copies[j].wait()
    elif j == steps:
        for copy in copies[steps:]:
            copy.wait()


def block_of(j, steps):
    return j // steps, slice((j % steps) * HB, (j % steps + 1) * HB)


def forward_kernel(
    sc, lens, packed, mixed_own, mixed_other, cot, ow_own, vectors, up_bias, pool, order,
    up_own, dn_own, a0, a1, a2, a3, b0, b1, b2, b3,
    out, pooled, grad2, smalls, ow_out, nrel_out, slope_out, scaled1_out, inv1_out, dn_keep, dn_send,
    wup, wdn, ow_other, ub, act, slope, scaled1, nrel, dnk, dns,
    sem_up, sem_dn, sem_ow, sem_ub, sem_out,
):
    width, hid = wup.shape[1], wup.shape[2]
    mid, blk, steps = width // 2, hid // 4, hid // HB
    piece = ow_own.shape[0] // 4
    out_bias, attn_gain, attn_shift, down_bias, ffn_gain, ffn_shift = (
        vectors[i : i + 1, :] for i in range(6)
    )
    quads = ((a0, b0), (a1, b1), (a2, b2), (a3, b3))
    small_in = []
    for r, (a_ref, _) in enumerate(quads):
        place = sc[2] ^ r
        rows = pl.ds(pl.multiple_of(piece * place, 16), piece)
        for c in range(2):
            small_in.append(
                pltpu.make_async_copy(
                    a_ref.at[pl.ds(width + c * piece, piece), :],
                    ow_other.at[rows, pl.ds(c * blk, blk)],
                    sem_ow.at[2 * r + c],
                )
            )
        small_in.append(
            pltpu.make_async_copy(
                a_ref.at[pl.ds(width + 2 * piece, 16), :],
                ub.at[:, pl.ds(pl.multiple_of(blk * place, 128), blk)],
                sem_ub.at[r],
            )
        )
    ups, dns_in = weight_copies(sc, up_own, dn_own, quads, wup, wdn, sem_up, sem_dn)
    for copy in small_in:
        copy.start()
    for j in range(steps):
        ups[j].start()
        dns_in[j].start()
    for copy in ups[steps:] + dns_in[steps:]:
        copy.start()
    copies = []

    def store(source, target):
        copies.append(pltpu.make_async_copy(source, target, sem_out.at[len(copies)]))
        copies[-1].start()

    for copy in small_in:
        copy.wait()
    store(ow_other, ow_out)
    resid = (
        packed[...].astype(f32)
        + dot(mixed_own[...], ow_own[...], NN)
        + dot(mixed_other[...], ow_other[...], NN)
        + out_bias
    )
    center = resid - jnp.mean(resid, axis=-1, keepdims=True)
    inv1 = lax.rsqrt(jnp.mean(center * center, axis=-1, keepdims=True) + EPS)
    inv1_out[...] = jnp.broadcast_to(inv1, inv1_out.shape)
    norm = center * inv1
    scaled1[...] = norm
    store(scaled1, scaled1_out)
    normed1 = norm * attn_gain + attn_shift
    low = normed1.astype(bf16)
    nrel[...] = dot(low, order[...], NN).astype(bf16)
    store(nrel, nrel_out)
    total = normed1 + down_bias

    def pre_act(j):
        side, cols = block_of(j, steps)
        await_weights(j, steps, ups)
        if side == 0:
            bias = up_bias[:, cols]
        else:
            three = ub[:, cols].astype(f32)
            bias = three[0:1] + three[1:2] + three[2:3]
        return dot(low, wup[side, :, cols], NN) + bias

    for j in range(2 * steps):
        side, cols = block_of(j, steps)
        here = pre_act(j)
        value, deriv = gelu_pair(here)
        value = value.astype(bf16)
        act[j] = value
        slope[j] = deriv.astype(bf16)
        store(slope.at[j], slope_out.at[j])
        await_weights(j, steps, dns_in)
        total = total + dot(value, wdn[side, cols, :], NN)
    center = total - jnp.mean(total, axis=-1, keepdims=True)
    inv2 = lax.rsqrt(jnp.mean(center * center, axis=-1, keepdims=True) + EPS)
    scaled2 = center * inv2
    result = scaled2 * ffn_gain + ffn_shift
    high = result.astype(bf16)
    out[...] = high
    rest = (result - high.astype(f32)).astype(bf16)
    sums = dot(pool[...], high, NN) + dot(pool[...], rest, NN)
    row = lax.broadcasted_iota(i32, (16, 1), 0)
    scale = jnp.zeros((16, 1), f32)
    for c in range(lens.shape[1]):
        scale = jnp.where(row == c, 1.0 / lens[0, c].astype(f32), scale)
    pooled[...] = sums * scale

    grad = cot[...].astype(f32)
    smalls[1:2, :] = jnp.sum(grad * scaled2, axis=0, keepdims=True)
    smalls[2:3, :] = jnp.sum(grad, axis=0, keepdims=True)
    smalls[3:8, :] = jnp.zeros((5, width), f32)
    grad = grad * ffn_gain
    grad = inv2 * (
        grad
        - jnp.mean(grad, axis=-1, keepdims=True)
        - scaled2 * jnp.mean(grad * scaled2, axis=-1, keepdims=True)
    )
    smalls[0:1, :] = jnp.sum(grad, axis=0, keepdims=True)
    grad2[...] = grad
    grel = dot(grad.astype(bf16), order[...], NN).astype(bf16)
    for j in range(2 * steps):
        grad = dot(grel, act[j], TN).astype(bf16)
        both = slice(j * HB, (j + 1) * HB)
        dns[:, both] = grad[mid:]
        store(dns.at[:, both], dn_send.at[:, both])
        dnk[:, both] = grad[:mid]
        store(dnk.at[:, both], dn_keep.at[:, both])
    for copy in copies:
        copy.wait()


def forward(sc, lens, packed, mixed_own, mixed_other, cot, ow, vectors, up_bias, pool, order, up, dn, quads):
    half = packed.shape[0] // 2
    width, hid = up.shape
    group = ow.shape[0]
    steps, mid = hid // HB, width // 2
    blocks = (2 * steps, half, HB)
    outs = [
        ((half, width), bf16),
        ((16, width), f32),
        ((half, width), f32),
        ((8, width), f32),
        ((group, width), bf16),
        ((half, width), bf16),
        (blocks, bf16),
        ((half, width), f32),
        ((half, 128), f32),
        ((mid, 2 * hid), bf16),
        ((mid, 2 * hid), bf16),
    ]
    args = (
        lens, packed, mixed_own, mixed_other, cot, ow, vectors, up_bias, pool, order, up, dn,
        *[a for a, _ in quads], *[b for _, b in quads],
    )
    return call(
        forward_kernel, "forward", 25, sc, args,
        [
            pl.BlockSpec(memory_space=pltpu.SMEM),
            pl.BlockSpec((half, width), lambda t, s: (s[0], 0)),
            full((half, group)),
            full((half, group)),
            full((half, width)),
            full((group, width)),
            full(vectors.shape),
            full((1, hid)),
            pl.BlockSpec((16, half), lambda t, s: (0, s[0])),
            full((width, width)),
        ]
        + [ANY] * 10,
        outs,
        [full(x) for x, _ in outs[:4]] + [ANY] * 4 + [full((half, 128))] + [ANY] * 2,
        [
            pltpu.VMEM((2, width, hid), bf16),
            pltpu.VMEM((2, hid, width), bf16),
            pltpu.VMEM((group, width), bf16),
            pltpu.VMEM((16, hid), bf16),
            pltpu.VMEM(blocks, bf16),
            pltpu.VMEM(blocks, bf16),
            pltpu.VMEM((half, width), f32),
            pltpu.VMEM((half, width), bf16),
            pltpu.VMEM((mid, 2 * hid), bf16),
            pltpu.VMEM((mid, 2 * hid), bf16),
            pltpu.SemaphoreType.DMA((steps + 4,)),
            pltpu.SemaphoreType.DMA((steps + 4,)),
            pltpu.SemaphoreType.DMA((8,)),
            pltpu.SemaphoreType.DMA((4,)),
            pltpu.SemaphoreType.DMA((6 * steps + 3,)),
        ],
    )


def backward_kernel(
    per, sc, tabs, grad2, pooled, smalls2, ow_own, ow_other, inv1, vectors, order, mixed_own,
    mixed_other, nrel, scaled1, slope_in, up_own, dn_own, a0, a1, a2, a3, b0, b1, b2, b3,
    send, gm_own, g1b, lines, up_keep, up_send,
    wup, wdn, slope, upk, ups, smalls, bias_sums, sem_up, sem_dn, sem_in, sem_out,
):
    width, hid = wup.shape[1], wup.shape[2]
    mid, steps = width // 2, hid // HB
    tokens, group = mixed_own.shape
    attn_gain = vectors[1:2, :]
    quads = ((a0, b0), (a1, b1), (a2, b2), (a3, b3))
    ups_in, dns_in = weight_copies(sc, up_own, dn_own, quads, wup, wdn, sem_up, sem_dn)
    slopes = [
        pltpu.make_async_copy(slope_in.at[j], slope.at[j], sem_in.at[j]) for j in range(2 * steps)
    ]
    for j in range(steps):
        dns_in[j].start()
        slopes[j].start()
        ups_in[j].start()
    for copy in dns_in[steps:] + slopes[steps:] + ups_in[steps:]:
        copy.start()
    copies = []

    def store(source, target):
        copies.append(pltpu.make_async_copy(source, target, sem_out.at[len(copies)]))
        copies[-1].start()

    low = grad2[...].astype(bf16)
    total = grad2[...]
    bias_sums[...] = jnp.zeros_like(bias_sums)

    def grad_act(j):
        side, cols = block_of(j, steps)
        await_weights(j, steps, dns_in)
        return dot(low, wdn[side, cols, :], NT)

    for j in range(2 * steps):
        side, cols = block_of(j, steps)
        here = grad_act(j)
        slopes[j].wait()
        pre = (here * slope[j].astype(f32)).astype(bf16)
        await_weights(j, steps, ups_in)
        total = total + dot(pre, wup[side, :, cols], NT)
        bias_sums[side : side + 1, cols] = jnp.sum(pre.astype(f32), axis=0, keepdims=True)
        grad = dot(nrel[...], pre, TN).astype(bf16)
        upk[side, :, cols] = grad[:mid]
        ups[side, :, cols] = grad[mid:]
        store(upk.at[side, :, cols], up_keep.at[side, :, cols])
        store(ups.at[side, :, cols], up_send.at[side, :, cols])
    norm = scaled1[...]
    smalls[1:2, :] = jnp.sum(total * norm, axis=0, keepdims=True)
    smalls[2:3, :] = jnp.sum(total, axis=0, keepdims=True)
    smalls[3:6, :] = smalls2[0:3, :]
    smalls[6:16, :] = jnp.zeros((10, width), f32)
    grad = total * attn_gain
    grad = inv1[:, 0:1] * (
        grad
        - jnp.mean(grad, axis=-1, keepdims=True)
        - norm * jnp.mean(grad * norm, axis=-1, keepdims=True)
    )
    smalls[0:1, :] = jnp.sum(grad, axis=0, keepdims=True)
    low = grad.astype(bf16)
    g1b[...] = low
    send[0:tokens, :] = dot(low, ow_other[...], NT).astype(bf16)
    gm_own[...] = dot(low, ow_own[...], NT).astype(bf16)
    sums = pooled[...].astype(bf16)
    send[tokens : tokens + 16, :] = sums[:, :group]
    send[tokens + 16 : tokens + 32, :] = sums[:, group:]

    low = dot(low, order[...], NN).astype(bf16)
    for side, mixed in enumerate((mixed_own, mixed_other)):
        grad = dot(low, mixed[...], TN).astype(bf16)
        upk[side, :, hid:] = grad[:mid]
        ups[side, :, hid:] = grad[mid:]
        tail = slice(hid, hid + group)
        store(upk.at[side, :, tail], up_keep.at[side, :, tail])
        store(ups.at[side, :, tail], up_send.at[side, :, tail])
    rows = dot(smalls[...].astype(bf16), order[...], NN)
    pieces = []
    source = (tabs[0:1, :] ^ sc[3]) * (2 * per) + tabs[1:2, :]
    for part in range(hid // width):
        spread = onehot(source + part * per == lax.broadcasted_iota(i32, (hid, width), 0))
        pieces.append(dot(bias_sums[...].astype(bf16), spread, NN))
    lines[...] = jnp.concatenate([rows[:6]] + [x[0:1] for x in pieces] + [rows[8:]], axis=0)
    other = jnp.concatenate(
        [rows[:6]] + [x[1:2] for x in pieces] + [rows[8:]], axis=0
    ).astype(bf16)
    send[tokens + 32 : tokens + 48, :] = other[:, :group]
    send[tokens + 48 : tokens + 64, :] = other[:, group:]
    for copy in copies:
        copy.wait()


def backward(
    per, sc, tabs, grad2, pooled, smalls, ow, ow_other, inv1, vectors, order, mixed_own, mixed_other,
    nrel, scaled1, slope, up, dn, quads,
):
    half, width = grad2.shape
    hid = up.shape[1]
    group = ow.shape[0]
    steps, mid = hid // HB, width // 2
    wide = (2, mid, hid + group)
    outs = [
        ((half + 64, group), bf16),
        ((half, group), bf16),
        ((half, width), bf16),
        ((16, width), f32),
        (wide, bf16),
        (wide, bf16),
    ]
    args = (
        tabs, grad2, pooled, smalls, ow, ow_other, inv1, vectors, order, mixed_own, mixed_other,
        nrel, scaled1, slope, up, dn, *[a for a, _ in quads], *[b for _, b in quads],
    )
    return call(
        functools.partial(backward_kernel, per), "backward", 18, sc, args,
        [full(x.shape) for x in args[:13]] + [ANY] * 11,
        outs,
        [full(x) for x, _ in outs[:4]] + [ANY] * 2,
        [
            pltpu.VMEM((2, width, hid), bf16),
            pltpu.VMEM((2, hid, width), bf16),
            pltpu.VMEM(slope.shape, bf16),
            pltpu.VMEM(wide, bf16),
            pltpu.VMEM(wide, bf16),
            pltpu.VMEM((16, width), f32),
            pltpu.VMEM((16, hid), f32),
            pltpu.SemaphoreType.DMA((steps + 4,)),
            pltpu.SemaphoreType.DMA((steps + 4,)),
            pltpu.SemaphoreType.DMA((2 * steps,)),
            pltpu.SemaphoreType.DMA((4 * steps + 4,)),
        ],
    )


def chip_sums(sc, name, pairs, views):
    dims = [d for d, _, _ in views]
    count = 2 * len(pairs)

    def kernel(sc, *refs):
        ins, outs = refs[:count], refs[count : count + len(dims)]
        loads, sems = refs[count + len(dims) : -1], refs[-1]
        copies = []
        for _, pair, view in views:
            for source in ins[2 * pair : 2 * pair + 2]:
                copies.append(
                    pltpu.make_async_copy(
                        source.at[view], loads[len(copies)], sems.at[len(copies)]
                    )
                )
                copies[-1].start()
        for number, out in enumerate(outs):
            copies[2 * number].wait()
            copies[2 * number + 1].wait()
            one, two = loads[2 * number], loads[2 * number + 1]
            out[...] = (one[...].astype(f32) + two[...].astype(f32)).astype(bf16)

    return call(
        kernel, name, ORDERED, sc, [x for pair in pairs for x in pair], [ANY] * count,
        [(d, bf16) for d in dims],
        [full(d) for d in dims],
        [pltpu.VMEM(d, bf16) for d in dims for _ in range(2)]
        + [pltpu.SemaphoreType.DMA((2 * len(dims),))],
    )


def swap(value, axis, bit):
    count = lax.axis_size(axis)
    return lax.ppermute(value, axis, [(i, i ^ (1 << bit)) for i in range(count)])


def pin(*values):
    return lax.optimization_barrier(values)


def add_low(left, right):
    return (left.astype(f32) + right.astype(f32)).astype(bf16)


def body(
    hidden,
    source_index,
    crop_lengths,
    deleted,
    qkv_weight,
    qv_bias,
    out_weight,
    out_bias,
    attn_gain,
    attn_shift,
    up_weight,
    up_bias,
    down_weight,
    down_bias,
    ffn_gain,
    ffn_shift,
    cotangent,
):
    length, width = hidden.shape
    crops = crop_lengths.shape[1]
    group = out_weight.shape[0]
    hid = up_weight.shape[1]
    half = length // 2
    n_dp, n_rep = lax.axis_size("dp"), lax.axis_size("rep")
    dp_bits, rep_bits = n_dp.bit_length() - 1, n_rep.bit_length() - 1
    shards = n_dp * n_rep
    per = width // shards
    h, dp = lax.axis_index("head"), lax.axis_index("dp")
    rep_index = lax.axis_index("rep")
    me = dp * n_rep + rep_index
    sc = jnp.stack([h, 1 - h, dp & 3, me, (dp & 1) + 2 * (rep_index & 1)]).astype(i32)

    stages = [("dp", b) for b in range(dp_bits)] + [("rep", b) for b in range(rep_bits)]
    block = np.zeros(shards, np.int32)
    for number, (axis, bit) in enumerate(stages):
        value = (np.arange(shards) >> (len(stages) - 1 - number)) & 1
        block |= (value << (bit + (rep_bits if axis == "dp" else 0))).astype(np.int32)
    row = np.arange(width)
    tabs = np.zeros((8, width), np.int32)
    tabs[0] = block[row // per]
    tabs[1] = row % per
    tabs = jnp.asarray(tabs)

    first, second = bundle(sc, up_bias, up_weight, down_weight, out_weight)
    first = swap(first, "head", 0)
    second = swap(second, "head", 0)
    packed, q, k, v, e_other, o_other, recip_other, segrow, code, pool = prepare(
        sc, crop_lengths, hidden, source_index, deleted, qkv_weight, qv_bias
    )
    mixed_recv = swap(o_other, "head", 0)
    first, o_other = pin(first, o_other)
    first_y = swap(first, "dp", 1)
    q_late, first = pin(q, first)
    e_own, o_own, recip_own = attend(sc, q_late, k, v, segrow, code)
    second, o_own = pin(second, o_own)
    second_y = swap(second, "rep", 0)
    packed_late, mixed_recv, second = pin(packed, mixed_recv, second)
    pt, order = ordered(per, sc, tabs, packed_late)
    first, first_y, second_y, pt = pin(first, first_y, second_y, pt)
    first_c, first_cy = swap(first, "dp", 0), swap(first_y, "dp", 0)
    second_c, second_cy = swap(second, "dp", 0), swap(second_y, "dp", 0)
    quads = [(first, second), (first_c, second_c), (first_y, second_y), (first_cy, second_cy)]
    vectors = jnp.stack(
        [out_bias, attn_gain, attn_shift, down_bias, ffn_gain, ffn_shift, ffn_shift, ffn_shift]
    )
    (
        output, pooled, grad2, smalls, ow_other, nrel, slope, scaled1, inv1, dn_keep, dn_send
    ) = forward(
        sc, crop_lengths, packed, o_own, mixed_recv, cotangent, out_weight, vectors, up_bias, pool,
        order, up_weight, down_weight, quads,
    )
    send, gm_own, g1b, lines, up_keep, up_send = backward(
        per, sc, tabs, grad2, pooled, smalls, out_weight, ow_other, inv1, vectors, order, o_own,
        mixed_recv, nrel, scaled1, slope, up_weight, down_weight, quads,
    )
    part, cut = width // 4, 1024
    recv = swap(send, "head", 0)
    dn_recv, gm_own = pin(swap(dn_send, "dp", 0), gm_own)
    across, few = n_dp // 2, n_rep // 2 * per
    low_tall = (across, 2, few, 2 * hid)
    rest = hid + group - cut
    (dn_next,) = chip_sums(
        sc, "down_sums", [(dn_keep.reshape(low_tall), dn_recv.reshape(low_tall))],
        [((across, few, 2 * hid), 0, (slice(None), 1))],
    )
    gm_own, dn_next = pin(gm_own, dn_next)
    up_recv, dn_next = pin(swap(up_send, "dp", 0), dn_next)
    a_next, b_next = chip_sums(
        sc, "up_sums", [(up_keep, up_recv)],
        [
            ((2 * part, cut), 0, (1, slice(None), pl.ds(0, cut))),
            ((2, part, rest), 0, (slice(None), pl.ds(part, part), pl.ds(cut, rest))),
        ],
    )
    gm_own, a_next, b_next = pin(gm_own, a_next, b_next)
    dq_own, dk_own, dv_own = attend_back(sc, gm_own, o_own, recip_own, q, k, v, e_own)
    recv, dq_own = pin(recv, dq_own)
    qkv_keep, qkv_send, gq = finish(
        sc, recv, o_other, recip_other, q, k, v, (dq_own, dk_own, dv_own), pt, lines, order, e_other
    )
    hidden_other, hidden_own = input_grad(sc, source_index, gq, qkv_weight, g1b)

    last = [hidden_own]

    def arrive(value):
        return pin(value, last[0])[0].astype(f32)

    def keep_low(value):
        last[0] = value.astype(bf16)
        return last[0]

    def low_half(value, axis, bit):
        rows = value.shape[0] // 2
        return keep_low(value[:rows].astype(f32) + arrive(swap(value[rows:], axis, bit)))

    def low_rest(value, axis, bit, dim):
        keep, out = jnp.split(value, 2, axis=dim)
        return keep_low(keep.astype(f32) + arrive(swap(out, axis, bit)))

    def three(keep, recv, late):
        return keep_low(keep.astype(f32) + recv.astype(f32) + arrive(late))

    later = stages[1:]
    dp_later = [x for x in later if x[0] == "dp"]
    rep_all = [x for x in later if x[0] == "rep"]
    down_swap = swap(dn_next, *rep_all[0])
    a_swap = swap(a_next, "head", 0)
    b_swap = swap(b_next, *later[0])
    qkv_swap = swap(qkv_send, "dp", 0)
    down = three(dn_keep.reshape(low_tall)[:, 0], dn_recv.reshape(low_tall)[:, 0], down_swap)
    up_b = three(up_keep[:, :part, cut:], up_recv[:, :part, cut:], b_swap)
    up_a = three(up_keep[0, :, :cut], up_recv[0, :, :cut], a_swap)
    qkv = keep_low(qkv_keep.astype(f32) + arrive(qkv_swap))
    qkv = qkv.reshape(across, n_rep, per, qkv.shape[1])
    qkv = low_rest(qkv, *rep_all[0], 1)
    up_a = low_half(up_a, *later[0])
    up_b = keep_low(up_b[0].astype(f32) + arrive(swap(up_b[1], "head", 0)))
    down = keep_low(down[:, :, :hid].astype(f32) + arrive(swap(down[:, :, hid:], "head", 0)))
    hidden_recv = swap(pin(hidden_other, last[0])[0], "head", 0)
    for axis, bit in rep_all[1:]:
        qkv = low_rest(qkv, axis, bit, 1)
    for axis, bit in later[1 : len(dp_later) + 1]:
        up_a = low_half(up_a, axis, bit)
        up_b = low_half(up_b, axis, bit)
    up = jnp.concatenate([up_a, up_b], axis=1)
    for axis, bit in dp_later:
        down = low_half(down, axis, bit)
    down = down[0]
    for axis, bit in rep_all[1:-1]:
        down = low_half(down, axis, bit)
        up = low_half(up, axis, bit)
    for axis, bit in dp_later[:-1]:
        qkv = low_rest(qkv, axis, bit, 0)
    axis, bit = dp_later[-1]
    keep, out = qkv[0, 0], arrive(swap(qkv[1:], axis, bit))[0, 0]
    wide = 3 * group
    qkv_grad = keep[:, :wide].astype(f32) + out[:, :wide]
    extra = (keep[:, wide:].astype(f32) + out[:, wide:]).T
    small = lax.dynamic_slice_in_dim(extra[:6], h * (per // 2), per // 2, 1)
    last[0] = qkv_grad
    axis, bit = later[-1]
    keep, out = up[:per], arrive(swap(up[per:], axis, bit))
    up_grad = keep[:, :hid].astype(f32) + out[:, :hid]
    out_grad = keep[:, hid:].astype(f32) + out[:, hid:]
    last[0] = up_grad
    down = down[:per].astype(f32) + arrive(swap(down[per:], axis, bit))
    last[0] = down
    grad_hidden = hidden_own.astype(f32) + arrive(hidden_recv)

    pooled_other = recv[half:].astype(f32)
    pooled_other = jnp.concatenate([pooled_other[:crops], pooled_other[16 : 16 + crops]], axis=1)
    return (
        output,
        pooled[:crops] + pooled_other,
        grad_hidden,
        qkv_grad,
        extra[15:16],
        out_grad.T,
        small[0],
        small[1],
        small[2],
        up_grad,
        extra[6 : 6 + hid // width].reshape(1, hid // shards),
        down.T,
        small[3],
        small[4],
        small[5],
    )


def solution(mesh):
    rows = P(("dp", "rep"), None)
    every = P(("dp", "rep", "head"), None)
    vector = P(("dp", "rep", "head"))
    return jax.shard_map(
        body,
        mesh=mesh,
        in_specs=(
            rows,
            rows,
            rows,
            rows,
            P(None, "head"),
            P("head", None),
            P("head", None),
            P(),
            P(),
            P(),
            P(None, "head"),
            P("head", None),
            P("head", None),
            P(),
            P(),
            P(),
            every,
        ),
        out_specs=(
            every,
            rows,
            every,
            P(("dp", "rep"), "head"),
            P("head", ("dp", "rep")),
            P("head", ("dp", "rep")),
            vector,
            vector,
            vector,
            P(("dp", "rep"), "head"),
            P("head", ("dp", "rep")),
            P("head", ("dp", "rep")),
            vector,
            vector,
            vector,
        ),
        check_vma=False,
    )
```

```python
import functools
import math

import jax
import jax.numpy as jnp
import numpy as np
from jax import lax
from jax.experimental import pallas as pl
from jax.experimental.pallas import tpu as pltpu
from jax.sharding import PartitionSpec as P

HEAD_DIM = 64
CROP_MAX = 256
EPS = 1e-12
MASKED = -1e30
NN = ((1,), (0,))
NT = ((1,), (1,))
TN = ((0,), (0,))
f32 = jnp.float32
bf16 = jnp.bfloat16
i32 = jnp.int32
NEEDS = {
    "bundle": 60,
    "prepare": 26,
    "attend": 18,
    "ordered": 14,
    "forward": 60,
    "backward": 60,
    "attend_back": 24,
    "finish": 30,
    "input_grad": 24,
    "down_sums": 8,
    "up_sums": 10,
}
QB = CROP_MAX
HB = 512
SCALE = 0.4
ORDERED = 60

shape = jax.ShapeDtypeStruct
ANY = pl.BlockSpec(memory_space=pl.ANY)


def dot(left, right, how):
    return lax.dot_general(left, right, (how, ((), ())), preferred_element_type=f32)


def cost(micros):
    return pl.CostEstimate(
        flops=int(SCALE * micros * 1.1e9), bytes_accessed=1024, transcendentals=0
    )


def full(dims):
    return pl.BlockSpec(dims, lambda *_: (0,) * len(dims))


def call(kernel, name, micros, sc, args, in_specs, outs, out_specs, scratch):
    return pl.pallas_call(
        kernel,
        grid_spec=pltpu.PrefetchScalarGridSpec(
            num_scalar_prefetch=1,
            grid=(1,),
            in_specs=in_specs,
            out_specs=out_specs,
            scratch_shapes=scratch,
        ),
        out_shape=[shape(s, d) for s, d in outs],
        compiler_params=pltpu.CompilerParams(vmem_limit_bytes=NEEDS[name] * 1024 * 1024),
        cost_estimate=cost(micros),
        name=name,
    )(sc, *args)


def onehot(hit):
    return jnp.where(hit, 1.0, 0.0).astype(bf16)


def gelu_pair(u):
    phi = 0.5 + 0.5 * lax.erf(u * (1.0 / math.sqrt(2.0)))
    bell = jnp.exp2((u * u) * (-0.5 / math.log(2.0))) * (1.0 / math.sqrt(2.0 * math.pi))
    return u * phi, phi + u * bell


def order_matrix(sc, tabs, width, per):
    source = (tabs[0:1, :] ^ sc[3]) * per + tabs[1:2, :]
    return onehot(source == lax.broadcasted_iota(i32, (width, width), 0))


def bundle_kernel(sc, up_bias, up, dn, ow, first, second, sems):
    quarter = sc[2]
    width, blk = up.shape[0], second.shape[0]
    piece = ow.shape[0] // 4
    cols = pl.ds(pl.multiple_of(quarter * blk, 128), blk)
    slab = pl.ds(pl.multiple_of(quarter * piece, 16), piece)
    copies = [
        pltpu.make_async_copy(up.at[:, cols], first.at[pl.ds(0, width), :], sems.at[0]),
        pltpu.make_async_copy(
            ow.at[slab, pl.ds(0, blk)], first.at[pl.ds(width, piece), :], sems.at[1]
        ),
        pltpu.make_async_copy(
            ow.at[slab, pl.ds(blk, blk)], first.at[pl.ds(width + piece, piece), :], sems.at[2]
        ),
        pltpu.make_async_copy(
            dn.at[pl.ds(pl.multiple_of(sc[4] * blk, 16), blk), :], second, sems.at[3]
        ),
    ]
    for copy in copies:
        copy.start()
    bias = up_bias[0:1, cols]
    high = bias.astype(bf16).astype(f32)
    mid = (bias - high).astype(bf16).astype(f32)
    low = bias - high - mid
    first[width + 2 * piece :, :] = jnp.concatenate(
        [high, mid, low, jnp.zeros((13, blk), f32)], axis=0
    ).astype(bf16)
    for copy in copies:
        copy.wait()


def bundle(sc, up_bias, up, dn, ow):
    width, hid = up.shape
    blk = hid // 4
    rows = width + ow.shape[0] // 2 + 16
    return call(
        bundle_kernel, "bundle", 2, sc, (up_bias, up, dn, ow),
        [full(up_bias.shape), ANY, ANY, ANY],
        [((rows, blk), bf16), ((blk, width), bf16)],
        [full((rows, blk)), full((blk, width))],
        [pltpu.SemaphoreType.DMA((4,))],
    )


def half_blocks(p):
    half = 2 * QB
    return (
        (pl.multiple_of(QB * p, QB), pl.multiple_of(half * p, QB), 2 * QB, 0, pl.multiple_of(QB * p, QB)),
        (pl.multiple_of(QB - QB * p, QB), pl.multiple_of(QB * p, QB), 3 * QB, 2 * QB, 0),
    )


def fill_cap(p, segrow, code, cap):
    for qs, ks, count, off, _ in half_blocks(p):
        first = pl.multiple_of(2 * QB * p + qs, QB)
        keys = code[pl.ds(ks, count), :]
        keys = jnp.concatenate([keys] * (QB // 128), axis=1)
        ask = segrow[0:1, pl.ds(first, QB)]
        shift = lax.broadcasted_iota(i32, (count, QB), 0) - lax.broadcasted_iota(
            i32, (count, QB), 1
        )
        allowed = (keys == ask) | (shift == first - ks)
        cap[off : off + count, :] = jnp.where(allowed, 3e38, MASKED)


def attend_pair(p, base, t, q, k, v, cap, e, mixed, recip):
    lane = lax.broadcasted_iota(i32, (QB, 128), 1) < HEAD_DIM
    cols = slice(t * 128, (t + 1) * 128)
    for qs, ks, count, off, _ in half_blocks(p):
        q_blk = q[pl.ds(pl.multiple_of(base + qs, QB), QB), cols]
        k_win = k[pl.ds(ks, count), cols]
        v_win = v[pl.ds(ks, count), cols]
        v_lane = lax.broadcasted_iota(i32, (count, 128), 1) < HEAD_DIM
        outs, recips = [], []
        for a in range(2):
            q_one = jnp.where(lane == (a == 0), q_blk, jnp.zeros_like(q_blk))
            s = jnp.minimum(dot(k_win, q_one, NT), cap[off : off + count, :])
            weights = jnp.exp(s - jnp.max(s, axis=0, keepdims=True)).astype(bf16)
            e[t, a, off : off + count, :] = weights
            v_one = jnp.where(v_lane == (a == 0), v_win, jnp.ones_like(v_win))
            o = dot(v_one, weights, TN)
            value, total = o[:HEAD_DIM], o[HEAD_DIM:]
            if a == 1:
                value, total = total, value
            inv = 1.0 / total
            outs.append(value * inv)
            recips.append(inv)
        mixed[pl.ds(qs, QB), cols] = jnp.transpose(jnp.concatenate(outs, axis=0)).astype(bf16)
        recip[pl.ds(qs, QB), cols] = jnp.transpose(jnp.concatenate(recips, axis=0))


def prepare_kernel(
    sc, lens, hidden, idx, dele, w, qv_bias,
    packed_hbm, q_hbm, k_hbm, v_hbm, e_hbm, mixed, recip, segrow, code, pool,
    packed, q, k, v, e, cap, sems,
):
    length, width = hidden.shape
    group = q.shape[1]
    idx_col = jnp.transpose(jnp.broadcast_to(idx[...].astype(f32), (8, length)))[:, :1]
    lane = lax.broadcasted_iota(i32, (8, length), 1)
    seg = jnp.zeros((8, length), f32)
    end = jnp.int32(0)
    for c in range(lens.shape[1]):
        end = end + lens[0, c]
        seg = seg + jnp.where(lane >= end, 1.0, 0.0)
    segrow[...] = seg
    code_row = jnp.where(jnp.broadcast_to(dele[...], (8, length)) == 0, seg, -1.0)
    code[...] = jnp.broadcast_to(jnp.transpose(code_row)[:, :1], code.shape)
    crop_row = lax.broadcasted_iota(i32, pool.shape, 0).astype(f32)
    pool[...] = onehot(crop_row == jnp.broadcast_to(code_row[:1], pool.shape))
    copies = []
    for i in range(length // QB):
        rows = slice(i * QB, (i + 1) * QB)
        place = lax.broadcasted_iota(i32, (QB, length), 1).astype(f32)
        pk = dot(onehot(idx_col[rows] == place), hidden[...], NN).astype(bf16)
        packed[rows, :] = pk
        out = dot(pk, w[...], NN)
        q[rows, :] = (out[:, :group] + qv_bias[:, :group]).astype(bf16) * jnp.asarray(
            HEAD_DIM**-0.5, bf16
        )
        k[rows, :] = out[:, group : 2 * group].astype(bf16)
        v[rows, :] = (out[:, 2 * group :] + qv_bias[:, group:]).astype(bf16)
    for number, (source, target) in enumerate(
        ((packed, packed_hbm), (q, q_hbm), (k, k_hbm), (v, v_hbm))
    ):
        copies.append(pltpu.make_async_copy(source, target, sems.at[number]))
        copies[-1].start()
    p = sc[1]
    fill_cap(p, segrow, code, cap)
    for t in range(group // 128):
        attend_pair(p, 2 * QB * p, t, q, k, v, cap, e, mixed, recip)
        copies.append(pltpu.make_async_copy(e.at[t], e_hbm.at[t], sems.at[4 + t]))
        copies[-1].start()
    for copy in copies:
        copy.wait()


def prepare(sc, lens, hidden, idx, dele, w, qv_bias):
    length, width = hidden.shape
    group = w.shape[1] // 3
    half, pairs = length // 2, group // 128
    weights = (pairs, 2, 5 * QB, QB)
    return call(
        prepare_kernel, "prepare", 15, sc, (lens, hidden, idx, dele, w, qv_bias),
        [pl.BlockSpec(memory_space=pltpu.SMEM)]
        + [full(x.shape) for x in (hidden, idx, dele, w, qv_bias)],
        [
            ((length, width), bf16),
            ((length, group), bf16),
            ((length, group), bf16),
            ((length, group), bf16),
            (weights, bf16),
            ((half, group), bf16),
            ((half, group), f32),
            ((8, length), f32),
            ((length, 128), f32),
            ((16, length), bf16),
        ],
        [ANY] * 5
        + [full((half, group)), full((half, group)), full((8, length)), full((length, 128)),
           full((16, length))],
        [
            pltpu.VMEM((length, width), bf16),
            pltpu.VMEM((length, group), bf16),
            pltpu.VMEM((length, group), bf16),
            pltpu.VMEM((length, group), bf16),
            pltpu.VMEM(weights, bf16),
            pltpu.VMEM((5 * QB, QB), f32),
            pltpu.SemaphoreType.DMA((4 + pairs,)),
        ],
    )


def attend_kernel(sc, q, k, v, segrow, code, e_hbm, mixed, recip, e, cap, sems):
    p = sc[0]
    fill_cap(p, segrow, code, cap)
    copies = []
    for t in range(q.shape[1] // 128):
        attend_pair(p, 0, t, q, k, v, cap, e, mixed, recip)
        copies.append(pltpu.make_async_copy(e.at[t], e_hbm.at[t], sems.at[t]))
        copies[-1].start()
    for copy in copies:
        copy.wait()


def attend(sc, q, k, v, segrow, code):
    length, group = q.shape
    half, pairs = length // 2, group // 128
    weights = (pairs, 2, 5 * QB, QB)
    return call(
        attend_kernel, "attend", 9, sc, (q, k, v, segrow, code),
        [pl.BlockSpec((half, group), lambda t, s: (s[0], 0))]
        + [full(x.shape) for x in (k, v, segrow, code)],
        [(weights, bf16), ((half, group), bf16), ((half, group), f32)],
        [ANY, full((half, group)), full((half, group))],
        [
            pltpu.VMEM(weights, bf16),
            pltpu.VMEM((5 * QB, QB), f32),
            pltpu.SemaphoreType.DMA((pairs,)),
        ],
    )


def back_pair(p, t, g, o, recip, q, k, v, e, put_dq, put_kv):
    lane = lax.broadcasted_iota(i32, (QB, 128), 1) < HEAD_DIM
    cols = slice(t * 128, (t + 1) * 128)
    pick = onehot(
        (lax.broadcasted_iota(i32, (16, 128), 1) < HEAD_DIM)
        == (lax.broadcasted_iota(i32, (16, 128), 0) == 0)
    )
    outer, inner = half_blocks(p)
    for number, (qs, ks, count, off, loc) in enumerate((inner, outer)):
        rows = pl.ds(qs, QB)
        grad = g[rows, cols].astype(f32) * recip[rows, cols]
        both = grad * o[rows, cols].astype(f32)
        high = both.astype(bf16)
        rest = (both - high.astype(f32)).astype(bf16)
        delta = dot(pick, high, NT) + dot(pick, rest, NT)
        grad = grad.astype(bf16)
        q_blk = q[rows, cols]
        k_win = k[pl.ds(ks, count), cols]
        v_win = v[pl.ds(ks, count), cols]
        dk = jnp.zeros((count, 128), f32)
        dv = jnp.zeros((count, 128), f32)
        dqs = []
        for a in range(2):
            g_one = jnp.where(lane == (a == 0), grad, jnp.zeros_like(grad))
            q_one = jnp.where(lane == (a == 0), q_blk, jnp.zeros_like(q_blk))
            weights = e[t, a, off : off + count, :]
            ds = (
                weights.astype(f32) * (dot(v_win, g_one, NT) - delta[a : a + 1])
            ).astype(bf16)
            dk += dot(ds, q_one, NN)
            dv += dot(weights, g_one, NN)
            dqs.append(dot(k_win, ds, TN)[a * HEAD_DIM : (a + 1) * HEAD_DIM])
        dq = jnp.transpose(jnp.concatenate(dqs, axis=0)) * HEAD_DIM ** (-0.5)
        put_dq(qs, cols, dq.astype(bf16))
        put_kv(number, loc, ks, count, cols, dk, dv)


def back_kernel(sc, g, o, recip, q, k, v, e_hbm, dq, dk, dv, e, sems):
    p = sc[0]
    pairs = q.shape[1] // 128
    loads = [pltpu.make_async_copy(e_hbm.at[t], e.at[t], sems.at[t]) for t in range(pairs)]
    for load in loads:
        load.start()

    def put_dq(qs, cols, value):
        dq[pl.ds(qs, QB), cols] = value

    def put_kv(number, loc, ks, count, cols, dk_part, dv_part):
        for ref, value in ((dk, dk_part), (dv, dv_part)):
            if number == 0:
                ref[:, cols] = value
            else:
                ref[pl.ds(loc, count), cols] += value

    for t in range(pairs):
        loads[t].wait()
        back_pair(p, t, g, o, recip, q, k, v, e, put_dq, put_kv)


def attend_back(sc, g, o, recip, q, k, v, e):
    length, group = q.shape
    half = length // 2
    return call(
        back_kernel, "attend_back", 0.1, sc, (g, o, recip, q, k, v, e),
        [full((half, group))] * 3
        + [pl.BlockSpec((half, group), lambda t, s: (s[0], 0)), full(k.shape), full(v.shape), ANY],
        [((half, group), bf16), ((3 * QB, group), f32), ((3 * QB, group), f32)],
        [full((half, group)), full((3 * QB, group)), full((3 * QB, group))],
        [pltpu.VMEM(e.shape, bf16), pltpu.SemaphoreType.DMA((group // 128,))],
    )


def finish_kernel(
    sc, g, o, recip, q, k, v, dq_own, dk_own, dv_own, pt, lines, order, e_hbm,
    keep, send, gq, e, ksum, vsum, sems,
):
    h, p = sc[0], sc[1]
    width = pt.shape[1]
    mid = width // 2
    length, group = ksum.shape
    half = length // 2
    pairs = group // 128
    loads = [pltpu.make_async_copy(e_hbm.at[t], e.at[t], sems.at[t]) for t in range(pairs)]
    for load in loads:
        load.start()
    own = pl.ds(pl.multiple_of(half * h, half), half)
    window = pl.ds(pl.multiple_of(QB * h, QB), 3 * QB)
    gq[own, 0:group] = dq_own[...]
    for total, part in ((ksum, dk_own), (vsum, dv_own)):
        total[...] = jnp.zeros_like(total)
        total[window, :] = part[...]

    def put_dq(qs, cols, value):
        gq[pl.ds(pl.multiple_of(half * p + qs, QB), QB), cols] = value

    def put_kv(number, loc, ks, count, cols, dk_part, dv_part):
        ksum[pl.ds(ks, count), cols] += dk_part
        vsum[pl.ds(ks, count), cols] += dv_part

    for t in range(pairs):
        loads[t].wait()
        back_pair(p, t, g, o, recip, q, k, v, e, put_dq, put_kv)
    gq[:, group : 2 * group] = ksum[...].astype(bf16)
    gq[:, 2 * group :] = vsum[...].astype(bf16)
    grads = gq[...]
    grad = dot(pt[...], grads, TN).astype(bf16)
    keep[:, : 3 * group] = grad[:mid]
    send[:, : 3 * group] = grad[mid:]
    sums = jnp.sum(grads.astype(f32), axis=0, keepdims=True)
    sums = jnp.concatenate([sums[:, :group], sums[:, 2 * group :]], axis=1).astype(bf16)
    sums = dot(jnp.broadcast_to(sums, (16, 2 * group)), order[...], NN)
    both = lines[...] + jnp.concatenate(
        [g[half + 32 : half + 48, :], g[half + 48 : half + 64, :]], axis=1
    ).astype(f32)
    both = jnp.where(lax.broadcasted_iota(i32, (16, width), 0) == 15, sums, both).astype(bf16)
    eye = onehot(
        lax.broadcasted_iota(i32, (16, 128), 0) == lax.broadcasted_iota(i32, (16, 128), 1)
    )
    extra = dot(both, eye, TN).astype(bf16)
    keep[:, 3 * group :] = extra[:mid]
    send[:, 3 * group :] = extra[mid:]

def finish(sc, g, o, recip, q, k, v, parts, pt, lines, order, e):
    length, group = q.shape
    half, width = length // 2, pt.shape[1]
    wide = (width // 2, 3 * group + 128)
    args = (g, o, recip, q, k, v, *parts, pt, lines, order, e)
    specs = [full(x.shape) for x in args[:-1]] + [ANY]
    specs[3] = pl.BlockSpec((half, group), lambda t, s: (s[1], 0))
    return call(
        finish_kernel, "finish", 0.1, sc, args, specs,
        [(wide, bf16), (wide, bf16), ((length, 3 * group), bf16)],
        [full(wide), full(wide), full((length, 3 * group))],
        [
            pltpu.VMEM(e.shape, bf16),
            pltpu.VMEM((length, group), f32),
            pltpu.VMEM((length, group), f32),
            pltpu.SemaphoreType.DMA((group // 128,)),
        ],
    )


def input_grad_kernel(sc, idx, gq, w, g1b, hid_other, hid_own, terms):
    h, p = sc[0], sc[1]
    half, length = g1b.shape[0], gq.shape[0]
    for i in range(2):
        rows = slice(i * half, (i + 1) * half)
        mine = jnp.where(h == i, 1.0, 0.0)
        part = dot(gq[rows, :], w[...], NT) + mine * g1b[...].astype(f32)
        terms[rows, :] = part.astype(bf16)
    spot = lax.broadcasted_iota(i32, (half, length), 0)
    hid_other[...] = dot(onehot(spot + half * p == idx[...]), terms[...], NN).astype(bf16)
    hid_own[...] = dot(onehot(spot + half * h == idx[...]), terms[...], NN).astype(bf16)


def input_grad(sc, idx, gq, w, g1b):
    half, width = g1b.shape
    args = (idx, gq, w, g1b)
    return call(
        input_grad_kernel, "input_grad", 0.1, sc, args, [full(x.shape) for x in args],
        [((half, width), bf16)] * 2, [full((half, width))] * 2,
        [pltpu.VMEM((2 * half, width), bf16)],
    )


def ordered_kernel(per, sc, tabs, packed, out, order):
    order[...] = order_matrix(sc, tabs, packed.shape[1], per)
    out[...] = dot(packed[...], order[...], NN).astype(bf16)


def ordered(per, sc, tabs, packed):
    width = packed.shape[1]
    return call(
        functools.partial(ordered_kernel, per), "ordered", ORDERED, sc, (tabs, packed),
        [full(tabs.shape), full(packed.shape)],
        [(packed.shape, bf16), ((width, width), bf16)],
        [full(packed.shape), full((width, width))],
        [],
    )


def weight_copies(sc, up_own, dn_own, quads, wup, wdn, sem_up, sem_dn):
    hid = wup.shape[2]
    width, blk, steps = wup.shape[1], hid // 4, hid // HB
    ups, dns = [], []
    for j in range(steps):
        cols = pl.ds(j * HB, HB)
        ups.append(pltpu.make_async_copy(up_own.at[:, cols], wup.at[0, :, cols], sem_up.at[j]))
        dns.append(pltpu.make_async_copy(dn_own.at[cols, :], wdn.at[0, cols, :], sem_dn.at[j]))
    for r, (a_ref, b_ref) in enumerate(quads):
        place = sc[2] ^ r
        cols = pl.ds(pl.multiple_of(blk * place, 128), blk)
        ups.append(
            pltpu.make_async_copy(
                a_ref.at[pl.ds(0, width), :], wup.at[1, :, cols], sem_up.at[steps + r]
            )
        )
        rows = pl.ds(pl.multiple_of(blk * (sc[4] ^ r), 16), blk)
        dns.append(pltpu.make_async_copy(b_ref, wdn.at[1, rows, :], sem_dn.at[steps + r]))
    return ups, dns


def await_weights(j, steps, copies):
    if j < steps:
        copies[j].wait()
    elif j == steps:
        for copy in copies[steps:]:
            copy.wait()


def block_of(j, steps):
    return j // steps, slice((j % steps) * HB, (j % steps + 1) * HB)


def forward_kernel(
    sc, lens, packed, mixed_own, mixed_other, cot, ow_own, v0, v1, v2, v3, v4, v5, up_bias, pool,
    order, up_own, dn_own, a0, a1, a2, a3, b0, b1, b2, b3,
    out, pooled, grad2, smalls, ow_out, nrel_out, slope_out, scaled1_out, inv1_out, dn_keep, dn_send,
    wup, wdn, ow_other, ub, act, slope, scaled1, nrel, dnk, dns,
    sem_up, sem_dn, sem_ow, sem_ub, sem_out,
):
    width, hid = wup.shape[1], wup.shape[2]
    mid, blk, steps = width // 2, hid // 4, hid // HB
    piece = ow_own.shape[0] // 4
    out_bias, attn_gain, attn_shift, down_bias, ffn_gain, ffn_shift = (
        ref[...].reshape(1, width) for ref in (v0, v1, v2, v3, v4, v5)
    )
    quads = ((a0, b0), (a1, b1), (a2, b2), (a3, b3))
    small_in = []
    for r, (a_ref, _) in enumerate(quads):
        place = sc[2] ^ r
        rows = pl.ds(pl.multiple_of(piece * place, 16), piece)
        for c in range(2):
            small_in.append(
                pltpu.make_async_copy(
                    a_ref.at[pl.ds(width + c * piece, piece), :],
                    ow_other.at[rows, pl.ds(c * blk, blk)],
                    sem_ow.at[2 * r + c],
                )
            )
        small_in.append(
            pltpu.make_async_copy(
                a_ref.at[pl.ds(width + 2 * piece, 16), :],
                ub.at[:, pl.ds(pl.multiple_of(blk * place, 128), blk)],
                sem_ub.at[r],
            )
        )
    ups, dns_in = weight_copies(sc, up_own, dn_own, quads, wup, wdn, sem_up, sem_dn)
    for copy in small_in:
        copy.start()
    for j in range(steps):
        ups[j].start()
        dns_in[j].start()
    for copy in ups[steps:] + dns_in[steps:]:
        copy.start()
    copies = []

    def store(source, target):
        copies.append(pltpu.make_async_copy(source, target, sem_out.at[len(copies)]))
        copies[-1].start()

    for copy in small_in:
        copy.wait()
    store(ow_other, ow_out)
    resid = (
        packed[...].astype(f32)
        + dot(mixed_own[...], ow_own[...], NN)
        + dot(mixed_other[...], ow_other[...], NN)
        + out_bias
    )
    center = resid - jnp.mean(resid, axis=-1, keepdims=True)
    inv1 = lax.rsqrt(jnp.mean(center * center, axis=-1, keepdims=True) + EPS)
    inv1_out[...] = jnp.broadcast_to(inv1, inv1_out.shape)
    norm = center * inv1
    scaled1[...] = norm
    store(scaled1, scaled1_out)
    normed1 = norm * attn_gain + attn_shift
    low = normed1.astype(bf16)
    nrel[...] = dot(low, order[...], NN).astype(bf16)
    store(nrel, nrel_out)
    total = normed1 + down_bias

    def pre_act(j):
        side, cols = block_of(j, steps)
        await_weights(j, steps, ups)
        if side == 0:
            bias = up_bias[:, cols]
        else:
            three = ub[:, cols].astype(f32)
            bias = three[0:1] + three[1:2] + three[2:3]
        return dot(low, wup[side, :, cols], NN) + bias

    for j in range(2 * steps):
        side, cols = block_of(j, steps)
        here = pre_act(j)
        value, deriv = gelu_pair(here)
        value = value.astype(bf16)
        act[j] = value
        slope[j] = deriv.astype(bf16)
        store(slope.at[j], slope_out.at[j])
        await_weights(j, steps, dns_in)
        total = total + dot(value, wdn[side, cols, :], NN)
    center = total - jnp.mean(total, axis=-1, keepdims=True)
    inv2 = lax.rsqrt(jnp.mean(center * center, axis=-1, keepdims=True) + EPS)
    scaled2 = center * inv2
    result = scaled2 * ffn_gain + ffn_shift
    high = result.astype(bf16)
    out[...] = high
    rest = (result - high.astype(f32)).astype(bf16)
    sums = dot(pool[...], high, NN) + dot(pool[...], rest, NN)
    row = lax.broadcasted_iota(i32, (16, 1), 0)
    scale = jnp.zeros((16, 1), f32)
    for c in range(lens.shape[1]):
        scale = jnp.where(row == c, 1.0 / lens[0, c].astype(f32), scale)
    pooled[...] = sums * scale

    grad = cot[...].astype(f32)
    smalls[1:2, :] = jnp.sum(grad * scaled2, axis=0, keepdims=True)
    smalls[2:3, :] = jnp.sum(grad, axis=0, keepdims=True)
    smalls[3:8, :] = jnp.zeros((5, width), f32)
    grad = grad * ffn_gain
    grad = inv2 * (
        grad
        - jnp.mean(grad, axis=-1, keepdims=True)
        - scaled2 * jnp.mean(grad * scaled2, axis=-1, keepdims=True)
    )
    smalls[0:1, :] = jnp.sum(grad, axis=0, keepdims=True)
    grad2[...] = grad
    grel = dot(grad.astype(bf16), order[...], NN).astype(bf16)
    for j in range(2 * steps):
        grad = dot(grel, act[j], TN).astype(bf16)
        both = slice(j * HB, (j + 1) * HB)
        dns[:, both] = grad[mid:]
        store(dns.at[:, both], dn_send.at[:, both])
        dnk[:, both] = grad[:mid]
        store(dnk.at[:, both], dn_keep.at[:, both])
    for copy in copies:
        copy.wait()


def forward(sc, lens, packed, mixed_own, mixed_other, cot, ow, vectors, up_bias, pool, order, up, dn, quads):
    half = packed.shape[0] // 2
    width, hid = up.shape
    group = ow.shape[0]
    steps, mid = hid // HB, width // 2
    blocks = (2 * steps, half, HB)
    outs = [
        ((half, width), bf16),
        ((16, width), f32),
        ((half, width), f32),
        ((8, width), f32),
        ((group, width), bf16),
        ((half, width), bf16),
        (blocks, bf16),
        ((half, width), f32),
        ((half, 128), f32),
        ((mid, 2 * hid), bf16),
        ((mid, 2 * hid), bf16),
    ]
    args = (
        lens, packed, mixed_own, mixed_other, cot, ow, *vectors, up_bias, pool, order, up, dn,
        *[a for a, _ in quads], *[b for _, b in quads],
    )
    return call(
        forward_kernel, "forward", 25, sc, args,
        [
            pl.BlockSpec(memory_space=pltpu.SMEM),
            pl.BlockSpec((half, width), lambda t, s: (s[0], 0)),
            full((half, group)),
            full((half, group)),
            full((half, width)),
            full((group, width)),
            *[full((width,))] * 6,
            full((1, hid)),
            pl.BlockSpec((16, half), lambda t, s: (0, s[0])),
            full((width, width)),
        ]
        + [ANY] * 10,
        outs,
        [full(x) for x, _ in outs[:4]] + [ANY] * 4 + [full((half, 128))] + [ANY] * 2,
        [
            pltpu.VMEM((2, width, hid), bf16),
            pltpu.VMEM((2, hid, width), bf16),
            pltpu.VMEM((group, width), bf16),
            pltpu.VMEM((16, hid), bf16),
            pltpu.VMEM(blocks, bf16),
            pltpu.VMEM(blocks, bf16),
            pltpu.VMEM((half, width), f32),
            pltpu.VMEM((half, width), bf16),
            pltpu.VMEM((mid, 2 * hid), bf16),
            pltpu.VMEM((mid, 2 * hid), bf16),
            pltpu.SemaphoreType.DMA((steps + 4,)),
            pltpu.SemaphoreType.DMA((steps + 4,)),
            pltpu.SemaphoreType.DMA((8,)),
            pltpu.SemaphoreType.DMA((4,)),
            pltpu.SemaphoreType.DMA((6 * steps + 3,)),
        ],
    )


def backward_kernel(
    per, sc, tabs, grad2, pooled, smalls2, ow_own, ow_other, inv1, gain, order, mixed_own,
    mixed_other, nrel, scaled1, slope_in, up_own, dn_own, a0, a1, a2, a3, b0, b1, b2, b3,
    send, gm_own, g1b, lines, up_keep, up_send,
    wup, wdn, slope, upk, ups, smalls, bias_sums, sem_up, sem_dn, sem_in, sem_out,
):
    width, hid = wup.shape[1], wup.shape[2]
    mid, steps = width // 2, hid // HB
    tokens, group = mixed_own.shape
    attn_gain = gain[...].reshape(1, width)
    quads = ((a0, b0), (a1, b1), (a2, b2), (a3, b3))
    ups_in, dns_in = weight_copies(sc, up_own, dn_own, quads, wup, wdn, sem_up, sem_dn)
    slopes = [
        pltpu.make_async_copy(slope_in.at[j], slope.at[j], sem_in.at[j]) for j in range(2 * steps)
    ]
    for j in range(steps):
        dns_in[j].start()
        slopes[j].start()
        ups_in[j].start()
    for copy in dns_in[steps:] + slopes[steps:] + ups_in[steps:]:
        copy.start()
    copies = []

    def store(source, target):
        copies.append(pltpu.make_async_copy(source, target, sem_out.at[len(copies)]))
        copies[-1].start()

    low = grad2[...].astype(bf16)
    total = grad2[...]
    bias_sums[...] = jnp.zeros_like(bias_sums)

    def grad_act(j):
        side, cols = block_of(j, steps)
        await_weights(j, steps, dns_in)
        return dot(low, wdn[side, cols, :], NT)

    for j in range(2 * steps):
        side, cols = block_of(j, steps)
        here = grad_act(j)
        slopes[j].wait()
        pre = (here * slope[j].astype(f32)).astype(bf16)
        await_weights(j, steps, ups_in)
        total = total + dot(pre, wup[side, :, cols], NT)
        bias_sums[side : side + 1, cols] = jnp.sum(pre.astype(f32), axis=0, keepdims=True)
        grad = dot(nrel[...], pre, TN).astype(bf16)
        upk[side, :, cols] = grad[:mid]
        ups[side, :, cols] = grad[mid:]
        store(upk.at[side, :, cols], up_keep.at[side, :, cols])
        store(ups.at[side, :, cols], up_send.at[side, :, cols])
    norm = scaled1[...]
    smalls[1:2, :] = jnp.sum(total * norm, axis=0, keepdims=True)
    smalls[2:3, :] = jnp.sum(total, axis=0, keepdims=True)
    smalls[3:6, :] = smalls2[0:3, :]
    smalls[6:16, :] = jnp.zeros((10, width), f32)
    grad = total * attn_gain
    grad = inv1[:, 0:1] * (
        grad
        - jnp.mean(grad, axis=-1, keepdims=True)
        - norm * jnp.mean(grad * norm, axis=-1, keepdims=True)
    )
    smalls[0:1, :] = jnp.sum(grad, axis=0, keepdims=True)
    low = grad.astype(bf16)
    g1b[...] = low
    send[0:tokens, :] = dot(low, ow_other[...], NT).astype(bf16)
    gm_own[...] = dot(low, ow_own[...], NT).astype(bf16)
    sums = pooled[...].astype(bf16)
    send[tokens : tokens + 16, :] = sums[:, :group]
    send[tokens + 16 : tokens + 32, :] = sums[:, group:]

    low = dot(low, order[...], NN).astype(bf16)
    for side, mixed in enumerate((mixed_own, mixed_other)):
        grad = dot(low, mixed[...], TN).astype(bf16)
        upk[side, :, hid:] = grad[:mid]
        ups[side, :, hid:] = grad[mid:]
        tail = slice(hid, hid + group)
        store(upk.at[side, :, tail], up_keep.at[side, :, tail])
        store(ups.at[side, :, tail], up_send.at[side, :, tail])
    rows = dot(smalls[...].astype(bf16), order[...], NN)
    pieces = []
    source = (tabs[0:1, :] ^ sc[3]) * (2 * per) + tabs[1:2, :]
    for part in range(hid // width):
        spread = onehot(source + part * per == lax.broadcasted_iota(i32, (hid, width), 0))
        pieces.append(dot(bias_sums[...].astype(bf16), spread, NN))
    lines[...] = jnp.concatenate([rows[:6]] + [x[0:1] for x in pieces] + [rows[8:]], axis=0)
    other = jnp.concatenate(
        [rows[:6]] + [x[1:2] for x in pieces] + [rows[8:]], axis=0
    ).astype(bf16)
    send[tokens + 32 : tokens + 48, :] = other[:, :group]
    send[tokens + 48 : tokens + 64, :] = other[:, group:]
    for copy in copies:
        copy.wait()


def backward(
    per, sc, tabs, grad2, pooled, smalls, ow, ow_other, inv1, vectors, order, mixed_own, mixed_other,
    nrel, scaled1, slope, up, dn, quads,
):
    half, width = grad2.shape
    hid = up.shape[1]
    group = ow.shape[0]
    steps, mid = hid // HB, width // 2
    wide = (2, mid, hid + group)
    outs = [
        ((half + 64, group), bf16),
        ((half, group), bf16),
        ((half, width), bf16),
        ((16, width), f32),
        (wide, bf16),
        (wide, bf16),
    ]
    args = (
        tabs, grad2, pooled, smalls, ow, ow_other, inv1, vectors[1], order, mixed_own, mixed_other,
        nrel, scaled1, slope, up, dn, *[a for a, _ in quads], *[b for _, b in quads],
    )
    return call(
        functools.partial(backward_kernel, per), "backward", 18, sc, args,
        [full(x.shape) for x in args[:13]] + [ANY] * 11,
        outs,
        [full(x) for x, _ in outs[:4]] + [ANY] * 2,
        [
            pltpu.VMEM((2, width, hid), bf16),
            pltpu.VMEM((2, hid, width), bf16),
            pltpu.VMEM(slope.shape, bf16),
            pltpu.VMEM(wide, bf16),
            pltpu.VMEM(wide, bf16),
            pltpu.VMEM((16, width), f32),
            pltpu.VMEM((16, hid), f32),
            pltpu.SemaphoreType.DMA((steps + 4,)),
            pltpu.SemaphoreType.DMA((steps + 4,)),
            pltpu.SemaphoreType.DMA((2 * steps,)),
            pltpu.SemaphoreType.DMA((4 * steps + 4,)),
        ],
    )


def chip_sums(sc, name, pairs, views):
    dims = [d for d, _, _ in views]
    count = 2 * len(pairs)

    def kernel(sc, *refs):
        ins, outs = refs[:count], refs[count : count + len(dims)]
        loads, sems = refs[count + len(dims) : -1], refs[-1]
        copies = []
        for _, pair, view in views:
            for source in ins[2 * pair : 2 * pair + 2]:
                copies.append(
                    pltpu.make_async_copy(
                        source.at[view], loads[len(copies)], sems.at[len(copies)]
                    )
                )
                copies[-1].start()
        for number, out in enumerate(outs):
            copies[2 * number].wait()
            copies[2 * number + 1].wait()
            one, two = loads[2 * number], loads[2 * number + 1]
            out[...] = (one[...].astype(f32) + two[...].astype(f32)).astype(bf16)

    return call(
        kernel, name, ORDERED, sc, [x for pair in pairs for x in pair], [ANY] * count,
        [(d, bf16) for d in dims],
        [full(d) for d in dims],
        [pltpu.VMEM(d, bf16) for d in dims for _ in range(2)]
        + [pltpu.SemaphoreType.DMA((2 * len(dims),))],
    )


def swap(value, axis, bit):
    count = lax.axis_size(axis)
    return lax.ppermute(value, axis, [(i, i ^ (1 << bit)) for i in range(count)])


def pin(*values):
    return lax.optimization_barrier(values)


def add_low(left, right):
    return (left.astype(f32) + right.astype(f32)).astype(bf16)


def body(
    hidden,
    source_index,
    crop_lengths,
    deleted,
    qkv_weight,
    qv_bias,
    out_weight,
    out_bias,
    attn_gain,
    attn_shift,
    up_weight,
    up_bias,
    down_weight,
    down_bias,
    ffn_gain,
    ffn_shift,
    cotangent,
):
    length, width = hidden.shape
    crops = crop_lengths.shape[1]
    group = out_weight.shape[0]
    hid = up_weight.shape[1]
    half = length // 2
    n_dp, n_rep = lax.axis_size("dp"), lax.axis_size("rep")
    dp_bits, rep_bits = n_dp.bit_length() - 1, n_rep.bit_length() - 1
    shards = n_dp * n_rep
    per = width // shards
    h, dp = lax.axis_index("head"), lax.axis_index("dp")
    rep_index = lax.axis_index("rep")
    me = dp * n_rep + rep_index
    sc = jnp.stack([h, 1 - h, dp & 3, me, (dp & 1) + 2 * (rep_index & 1)]).astype(i32)

    stages = [("dp", b) for b in range(dp_bits)] + [("rep", b) for b in range(rep_bits)]
    block = np.zeros(shards, np.int32)
    for number, (axis, bit) in enumerate(stages):
        value = (np.arange(shards) >> (len(stages) - 1 - number)) & 1
        block |= (value << (bit + (rep_bits if axis == "dp" else 0))).astype(np.int32)
    row = np.arange(width)
    tabs = np.zeros((8, width), np.int32)
    tabs[0] = block[row // per]
    tabs[1] = row % per
    tabs = jnp.asarray(tabs)

    first, second = bundle(sc, up_bias, up_weight, down_weight, out_weight)
    first = swap(first, "head", 0)
    second = swap(second, "head", 0)
    packed, q, k, v, e_other, o_other, recip_other, segrow, code, pool = prepare(
        sc, crop_lengths, hidden, source_index, deleted, qkv_weight, qv_bias
    )
    mixed_recv = swap(o_other, "head", 0)
    first, o_other = pin(first, o_other)
    first_y = swap(first, "dp", 1)
    q_late, first = pin(q, first)
    e_own, o_own, recip_own = attend(sc, q_late, k, v, segrow, code)
    second, o_own = pin(second, o_own)
    second_y = swap(second, "rep", 0)
    packed_late, mixed_recv, second = pin(packed, mixed_recv, second)
    pt, order = ordered(per, sc, tabs, packed_late)
    first, first_y, second_y, pt = pin(first, first_y, second_y, pt)
    first_c, first_cy = swap(first, "dp", 0), swap(first_y, "dp", 0)
    second_c, second_cy = swap(second, "dp", 0), swap(second_y, "dp", 0)
    quads = [(first, second), (first_c, second_c), (first_y, second_y), (first_cy, second_cy)]
    vectors = [out_bias, attn_gain, attn_shift, down_bias, ffn_gain, ffn_shift]
    (
        output, pooled, grad2, smalls, ow_other, nrel, slope, scaled1, inv1, dn_keep, dn_send
    ) = forward(
        sc, crop_lengths, packed, o_own, mixed_recv, cotangent, out_weight, vectors, up_bias, pool,
        order, up_weight, down_weight, quads,
    )
    send, gm_own, g1b, lines, up_keep, up_send = backward(
        per, sc, tabs, grad2, pooled, smalls, out_weight, ow_other, inv1, vectors, order, o_own,
        mixed_recv, nrel, scaled1, slope, up_weight, down_weight, quads,
    )
    part, cut = width // 4, 1024
    recv = swap(send, "head", 0)
    dn_recv, gm_own = pin(swap(dn_send, "dp", 0), gm_own)
    across, few = n_dp // 2, n_rep // 2 * per
    low_tall = (across, 2, few, 2 * hid)
    rest = hid + group - cut
    (dn_next,) = chip_sums(
        sc, "down_sums", [(dn_keep.reshape(low_tall), dn_recv.reshape(low_tall))],
        [((across, few, 2 * hid), 0, (slice(None), 1))],
    )
    gm_own, dn_next = pin(gm_own, dn_next)
    up_recv, dn_next = pin(swap(up_send, "dp", 0), dn_next)
    a_next, b_next = chip_sums(
        sc, "up_sums", [(up_keep, up_recv)],
        [
            ((2 * part, cut), 0, (1, slice(None), pl.ds(0, cut))),
            ((2, part, rest), 0, (slice(None), pl.ds(part, part), pl.ds(cut, rest))),
        ],
    )
    gm_own, a_next, b_next = pin(gm_own, a_next, b_next)
    dq_own, dk_own, dv_own = attend_back(sc, gm_own, o_own, recip_own, q, k, v, e_own)
    recv, dq_own = pin(recv, dq_own)
    qkv_keep, qkv_send, gq = finish(
        sc, recv, o_other, recip_other, q, k, v, (dq_own, dk_own, dv_own), pt, lines, order, e_other
    )
    hidden_other, hidden_own = input_grad(sc, source_index, gq, qkv_weight, g1b)

    last = [hidden_own]

    def arrive(value):
        return pin(value, last[0])[0].astype(f32)

    def keep_low(value):
        last[0] = value.astype(bf16)
        return last[0]

    def low_half(value, axis, bit):
        rows = value.shape[0] // 2
        return keep_low(value[:rows].astype(f32) + arrive(swap(value[rows:], axis, bit)))

    def low_rest(value, axis, bit, dim):
        keep, out = jnp.split(value, 2, axis=dim)
        return keep_low(keep.astype(f32) + arrive(swap(out, axis, bit)))

    def three(keep, recv, late):
        return keep_low(keep.astype(f32) + recv.astype(f32) + arrive(late))

    later = stages[1:]
    dp_later = [x for x in later if x[0] == "dp"]
    rep_all = [x for x in later if x[0] == "rep"]
    down_swap = swap(dn_next, *rep_all[0])
    a_swap = swap(a_next, "head", 0)
    b_swap = swap(b_next, *later[0])
    qkv_swap = swap(qkv_send, "dp", 0)
    down = three(dn_keep.reshape(low_tall)[:, 0], dn_recv.reshape(low_tall)[:, 0], down_swap)
    up_b = three(up_keep[:, :part, cut:], up_recv[:, :part, cut:], b_swap)
    up_a = three(up_keep[0, :, :cut], up_recv[0, :, :cut], a_swap)
    qkv = keep_low(qkv_keep.astype(f32) + arrive(qkv_swap))
    qkv = qkv.reshape(across, n_rep, per, qkv.shape[1])
    qkv = low_rest(qkv, *rep_all[0], 1)
    up_a = low_half(up_a, *later[0])
    up_b = keep_low(up_b[0].astype(f32) + arrive(swap(up_b[1], "head", 0)))
    down = keep_low(down[:, :, :hid].astype(f32) + arrive(swap(down[:, :, hid:], "head", 0)))
    hidden_recv = swap(pin(hidden_other, last[0])[0], "head", 0)
    for axis, bit in rep_all[1:]:
        qkv = low_rest(qkv, axis, bit, 1)
    for axis, bit in later[1 : len(dp_later) + 1]:
        up_a = low_half(up_a, axis, bit)
        up_b = low_half(up_b, axis, bit)
    up = jnp.concatenate([up_a, up_b], axis=1)
    for axis, bit in dp_later:
        down = low_half(down, axis, bit)
    down = down[0]
    for axis, bit in rep_all[1:-1]:
        down = low_half(down, axis, bit)
        up = low_half(up, axis, bit)
    for axis, bit in dp_later[:-1]:
        qkv = low_rest(qkv, axis, bit, 0)
    axis, bit = dp_later[-1]
    keep, out = qkv[0, 0], arrive(swap(qkv[1:], axis, bit))[0, 0]
    wide = 3 * group
    qkv_grad = keep[:, :wide].astype(f32) + out[:, :wide]
    extra = (keep[:, wide:].astype(f32) + out[:, wide:]).T
    small = lax.dynamic_slice_in_dim(extra[:6], h * (per // 2), per // 2, 1)
    last[0] = qkv_grad
    axis, bit = later[-1]
    keep, out = up[:per], arrive(swap(up[per:], axis, bit))
    up_grad = keep[:, :hid].astype(f32) + out[:, :hid]
    out_grad = keep[:, hid:].astype(f32) + out[:, hid:]
    last[0] = up_grad
    grad_hidden = hidden_own.astype(f32) + arrive(hidden_recv)
    last[0] = grad_hidden
    down = down[:per].astype(f32) + arrive(swap(down[per:], axis, bit))

    pooled_other = recv[half:].astype(f32)
    pooled_other = jnp.concatenate([pooled_other[:crops], pooled_other[16 : 16 + crops]], axis=1)
    return (
        output,
        pooled[:crops] + pooled_other,
        grad_hidden,
        qkv_grad,
        extra[15:16],
        out_grad.T,
        small[0],
        small[1],
        small[2],
        up_grad,
        extra[6 : 6 + hid // width].reshape(1, hid // shards),
        down.T,
        small[3],
        small[4],
        small[5],
    )


def solution(mesh):
    rows = P(("dp", "rep"), None)
    every = P(("dp", "rep", "head"), None)
    vector = P(("dp", "rep", "head"))
    return jax.shard_map(
        body,
        mesh=mesh,
        in_specs=(
            rows,
            rows,
            rows,
            rows,
            P(None, "head"),
            P("head", None),
            P("head", None),
            P(),
            P(),
            P(),
            P(None, "head"),
            P("head", None),
            P("head", None),
            P(),
            P(),
            P(),
            every,
        ),
        out_specs=(
            every,
            rows,
            every,
            P(("dp", "rep"), "head"),
            P("head", ("dp", "rep")),
            P("head", ("dp", "rep")),
            vector,
            vector,
            vector,
            P(("dp", "rep"), "head"),
            P("head", ("dp", "rep")),
            P("head", ("dp", "rep")),
            vector,
            vector,
            vector,
        ),
        check_vma=False,
    )
```

```python
import functools
import math

import jax
import jax.numpy as jnp
import numpy as np
from jax import lax
from jax.experimental import pallas as pl
from jax.experimental.pallas import tpu as pltpu
from jax.sharding import PartitionSpec as P

HEAD_DIM = 64
CROP_MAX = 256
EPS = 1e-12
MASKED = -1e30
NN = ((1,), (0,))
NT = ((1,), (1,))
TN = ((0,), (0,))
f32 = jnp.float32
bf16 = jnp.bfloat16
i32 = jnp.int32
NEEDS = {
    "bundle": 60,
    "prepare": 26,
    "attend": 18,
    "ordered": 14,
    "forward": 60,
    "backward": 60,
    "attend_back": 24,
    "finish": 30,
    "input_grad": 24,
    "down_sums": 8,
    "up_sums": 10,
}
QB = CROP_MAX
HB = 512
SCALE = 0.4
ORDERED = 60

shape = jax.ShapeDtypeStruct
ANY = pl.BlockSpec(memory_space=pl.ANY)


def dot(left, right, how):
    return lax.dot_general(left, right, (how, ((), ())), preferred_element_type=f32)


def cost(micros):
    return pl.CostEstimate(
        flops=int(SCALE * micros * 1.1e9), bytes_accessed=1024, transcendentals=0
    )


def full(dims):
    return pl.BlockSpec(dims, lambda *_: (0,) * len(dims))


def call(kernel, name, micros, sc, args, in_specs, outs, out_specs, scratch):
    return pl.pallas_call(
        kernel,
        grid_spec=pltpu.PrefetchScalarGridSpec(
            num_scalar_prefetch=1,
            grid=(1,),
            in_specs=in_specs,
            out_specs=out_specs,
            scratch_shapes=scratch,
        ),
        out_shape=[shape(s, d) for s, d in outs],
        compiler_params=pltpu.CompilerParams(vmem_limit_bytes=NEEDS[name] * 1024 * 1024),
        cost_estimate=cost(micros),
        name=name,
    )(sc, *args)


def onehot(hit):
    return jnp.where(hit, 1.0, 0.0).astype(bf16)


def gelu_pair(u):
    phi = 0.5 + 0.5 * lax.erf(u * (1.0 / math.sqrt(2.0)))
    bell = jnp.exp2((u * u) * (-0.5 / math.log(2.0))) * (1.0 / math.sqrt(2.0 * math.pi))
    return u * phi, phi + u * bell


def order_matrix(sc, tabs, width, per):
    source = (tabs[0:1, :] ^ sc[3]) * per + tabs[1:2, :]
    return onehot(source == lax.broadcasted_iota(i32, (width, width), 0))


def bundle_kernel(sc, up_bias, up, dn, ow, first, second, sems):
    quarter = sc[2]
    width, blk = up.shape[0], second.shape[0]
    piece = ow.shape[0] // 4
    cols = pl.ds(pl.multiple_of(quarter * blk, 128), blk)
    slab = pl.ds(pl.multiple_of(quarter * piece, 16), piece)
    copies = [
        pltpu.make_async_copy(up.at[:, cols], first.at[pl.ds(0, width), :], sems.at[0]),
        pltpu.make_async_copy(
            ow.at[slab, pl.ds(0, blk)], first.at[pl.ds(width, piece), :], sems.at[1]
        ),
        pltpu.make_async_copy(
            ow.at[slab, pl.ds(blk, blk)], first.at[pl.ds(width + piece, piece), :], sems.at[2]
        ),
        pltpu.make_async_copy(
            dn.at[pl.ds(pl.multiple_of(sc[4] * blk, 16), blk), :], second, sems.at[3]
        ),
    ]
    for copy in copies:
        copy.start()
    bias = up_bias[0:1, cols]
    high = bias.astype(bf16).astype(f32)
    mid = (bias - high).astype(bf16).astype(f32)
    low = bias - high - mid
    first[width + 2 * piece :, :] = jnp.concatenate(
        [high, mid, low, jnp.zeros((13, blk), f32)], axis=0
    ).astype(bf16)
    for copy in copies:
        copy.wait()


def bundle(sc, up_bias, up, dn, ow):
    width, hid = up.shape
    blk = hid // 4
    rows = width + ow.shape[0] // 2 + 16
    return call(
        bundle_kernel, "bundle", 2, sc, (up_bias, up, dn, ow),
        [full(up_bias.shape), ANY, ANY, ANY],
        [((rows, blk), bf16), ((blk, width), bf16)],
        [full((rows, blk)), full((blk, width))],
        [pltpu.SemaphoreType.DMA((4,))],
    )


def half_blocks(p):
    half = 2 * QB
    return (
        (pl.multiple_of(QB * p, QB), pl.multiple_of(half * p, QB), 2 * QB, 0, pl.multiple_of(QB * p, QB)),
        (pl.multiple_of(QB - QB * p, QB), pl.multiple_of(QB * p, QB), 3 * QB, 2 * QB, 0),
    )


def fill_cap(p, segrow, code, cap):
    for qs, ks, count, off, _ in half_blocks(p):
        first = pl.multiple_of(2 * QB * p + qs, QB)
        keys = code[pl.ds(ks, count), :]
        keys = jnp.concatenate([keys] * (QB // 128), axis=1)
        ask = segrow[0:1, pl.ds(first, QB)]
        shift = lax.broadcasted_iota(i32, (count, QB), 0) - lax.broadcasted_iota(
            i32, (count, QB), 1
        )
        allowed = (keys == ask) | (shift == first - ks)
        cap[off : off + count, :] = jnp.where(allowed, 3e38, MASKED)


def attend_pair(p, base, t, q, k, v, cap, e, mixed, recip):
    lane = lax.broadcasted_iota(i32, (QB, 128), 1) < HEAD_DIM
    cols = slice(t * 128, (t + 1) * 128)
    for qs, ks, count, off, _ in half_blocks(p):
        q_blk = q[pl.ds(pl.multiple_of(base + qs, QB), QB), cols]
        k_win = k[pl.ds(ks, count), cols]
        v_win = v[pl.ds(ks, count), cols]
        v_lane = lax.broadcasted_iota(i32, (count, 128), 1) < HEAD_DIM
        outs, recips = [], []
        for a in range(2):
            q_one = jnp.where(lane == (a == 0), q_blk, jnp.zeros_like(q_blk))
            s = jnp.minimum(dot(k_win, q_one, NT), cap[off : off + count, :])
            weights = jnp.exp(s - jnp.max(s, axis=0, keepdims=True)).astype(bf16)
            e[t, a, off : off + count, :] = weights
            v_one = jnp.where(v_lane == (a == 0), v_win, jnp.ones_like(v_win))
            o = dot(v_one, weights, TN)
            value, total = o[:HEAD_DIM], o[HEAD_DIM:]
            if a == 1:
                value, total = total, value
            inv = 1.0 / total
            outs.append(value * inv)
            recips.append(inv)
        mixed[pl.ds(qs, QB), cols] = jnp.transpose(jnp.concatenate(outs, axis=0)).astype(bf16)
        recip[pl.ds(qs, QB), cols] = jnp.transpose(jnp.concatenate(recips, axis=0))


def prepare_kernel(
    sc, lens, hidden, idx, dele, w, qv_bias,
    packed_hbm, q_hbm, k_hbm, v_hbm, e_hbm, mixed, recip, segrow, code, pool,
    packed, q, k, v, e, cap, sems,
):
    length, width = hidden.shape
    group = q.shape[1]
    idx_col = jnp.transpose(jnp.broadcast_to(idx[...].astype(f32), (8, length)))[:, :1]
    lane = lax.broadcasted_iota(i32, (8, length), 1)
    seg = jnp.zeros((8, length), f32)
    end = jnp.int32(0)
    for c in range(lens.shape[1]):
        end = end + lens[0, c]
        seg = seg + jnp.where(lane >= end, 1.0, 0.0)
    segrow[...] = seg
    code_row = jnp.where(jnp.broadcast_to(dele[...], (8, length)) == 0, seg, -1.0)
    code[...] = jnp.broadcast_to(jnp.transpose(code_row)[:, :1], code.shape)
    crop_row = lax.broadcasted_iota(i32, pool.shape, 0).astype(f32)
    pool[...] = onehot(crop_row == jnp.broadcast_to(code_row[:1], pool.shape))
    copies = []
    for i in range(length // QB):
        rows = slice(i * QB, (i + 1) * QB)
        place = lax.broadcasted_iota(i32, (QB, length), 1).astype(f32)
        pk = dot(onehot(idx_col[rows] == place), hidden[...], NN).astype(bf16)
        packed[rows, :] = pk
        out = dot(pk, w[...], NN)
        q[rows, :] = (out[:, :group] + qv_bias[:, :group]).astype(bf16) * jnp.asarray(
            HEAD_DIM**-0.5, bf16
        )
        k[rows, :] = out[:, group : 2 * group].astype(bf16)
        v[rows, :] = (out[:, 2 * group :] + qv_bias[:, group:]).astype(bf16)
    for number, (source, target) in enumerate(
        ((packed, packed_hbm), (q, q_hbm), (k, k_hbm), (v, v_hbm))
    ):
        copies.append(pltpu.make_async_copy(source, target, sems.at[number]))
        copies[-1].start()
    p = sc[1]
    fill_cap(p, segrow, code, cap)
    for t in range(group // 128):
        attend_pair(p, 2 * QB * p, t, q, k, v, cap, e, mixed, recip)
        copies.append(pltpu.make_async_copy(e.at[t], e_hbm.at[t], sems.at[4 + t]))
        copies[-1].start()
    for copy in copies:
        copy.wait()


def prepare(sc, lens, hidden, idx, dele, w, qv_bias):
    length, width = hidden.shape
    group = w.shape[1] // 3
    half, pairs = length // 2, group // 128
    weights = (pairs, 2, 5 * QB, QB)
    return call(
        prepare_kernel, "prepare", 15, sc, (lens, hidden, idx, dele, w, qv_bias),
        [pl.BlockSpec(memory_space=pltpu.SMEM)]
        + [full(x.shape) for x in (hidden, idx, dele, w, qv_bias)],
        [
            ((length, width), bf16),
            ((length, group), bf16),
            ((length, group), bf16),
            ((length, group), bf16),
            (weights, bf16),
            ((half, group), bf16),
            ((half, group), f32),
            ((8, length), f32),
            ((length, 128), f32),
            ((16, length), bf16),
        ],
        [ANY] * 5
        + [full((half, group)), full((half, group)), full((8, length)), full((length, 128)),
           full((16, length))],
        [
            pltpu.VMEM((length, width), bf16),
            pltpu.VMEM((length, group), bf16),
            pltpu.VMEM((length, group), bf16),
            pltpu.VMEM((length, group), bf16),
            pltpu.VMEM(weights, bf16),
            pltpu.VMEM((5 * QB, QB), f32),
            pltpu.SemaphoreType.DMA((4 + pairs,)),
        ],
    )


def attend_kernel(sc, q, k, v, segrow, code, e_hbm, mixed, recip, e, cap, sems):
    p = sc[0]
    fill_cap(p, segrow, code, cap)
    copies = []
    for t in range(q.shape[1] // 128):
        attend_pair(p, 0, t, q, k, v, cap, e, mixed, recip)
        copies.append(pltpu.make_async_copy(e.at[t], e_hbm.at[t], sems.at[t]))
        copies[-1].start()
    for copy in copies:
        copy.wait()


def attend(sc, q, k, v, segrow, code):
    length, group = q.shape
    half, pairs = length // 2, group // 128
    weights = (pairs, 2, 5 * QB, QB)
    return call(
        attend_kernel, "attend", 9, sc, (q, k, v, segrow, code),
        [pl.BlockSpec((half, group), lambda t, s: (s[0], 0))]
        + [full(x.shape) for x in (k, v, segrow, code)],
        [(weights, bf16), ((half, group), bf16), ((half, group), f32)],
        [ANY, full((half, group)), full((half, group))],
        [
            pltpu.VMEM(weights, bf16),
            pltpu.VMEM((5 * QB, QB), f32),
            pltpu.SemaphoreType.DMA((pairs,)),
        ],
    )


def back_pair(p, t, g, o, recip, q, k, v, e, put_dq, put_kv):
    lane = lax.broadcasted_iota(i32, (QB, 128), 1) < HEAD_DIM
    cols = slice(t * 128, (t + 1) * 128)
    pick = onehot(
        (lax.broadcasted_iota(i32, (16, 128), 1) < HEAD_DIM)
        == (lax.broadcasted_iota(i32, (16, 128), 0) == 0)
    )
    outer, inner = half_blocks(p)
    for number, (qs, ks, count, off, loc) in enumerate((inner, outer)):
        rows = pl.ds(qs, QB)
        grad = g[rows, cols].astype(f32) * recip[rows, cols]
        both = grad * o[rows, cols].astype(f32)
        high = both.astype(bf16)
        rest = (both - high.astype(f32)).astype(bf16)
        delta = dot(pick, high, NT) + dot(pick, rest, NT)
        grad = grad.astype(bf16)
        q_blk = q[rows, cols]
        k_win = k[pl.ds(ks, count), cols]
        v_win = v[pl.ds(ks, count), cols]
        dk = jnp.zeros((count, 128), f32)
        dv = jnp.zeros((count, 128), f32)
        dqs = []
        for a in range(2):
            g_one = jnp.where(lane == (a == 0), grad, jnp.zeros_like(grad))
            q_one = jnp.where(lane == (a == 0), q_blk, jnp.zeros_like(q_blk))
            weights = e[t, a, off : off + count, :]
            ds = (
                weights.astype(f32) * (dot(v_win, g_one, NT) - delta[a : a + 1])
            ).astype(bf16)
            dk += dot(ds, q_one, NN)
            dv += dot(weights, g_one, NN)
            dqs.append(dot(k_win, ds, TN)[a * HEAD_DIM : (a + 1) * HEAD_DIM])
        dq = jnp.transpose(jnp.concatenate(dqs, axis=0)) * HEAD_DIM ** (-0.5)
        put_dq(qs, cols, dq.astype(bf16))
        put_kv(number, loc, ks, count, cols, dk, dv)


def back_kernel(sc, g, o, recip, q, k, v, e_hbm, dq, dk, dv, e, sems):
    p = sc[0]
    pairs = q.shape[1] // 128
    loads = [pltpu.make_async_copy(e_hbm.at[t], e.at[t], sems.at[t]) for t in range(pairs)]
    for load in loads:
        load.start()

    def put_dq(qs, cols, value):
        dq[pl.ds(qs, QB), cols] = value

    def put_kv(number, loc, ks, count, cols, dk_part, dv_part):
        for ref, value in ((dk, dk_part), (dv, dv_part)):
            if number == 0:
                ref[:, cols] = value
            else:
                ref[pl.ds(loc, count), cols] += value

    for t in range(pairs):
        loads[t].wait()
        back_pair(p, t, g, o, recip, q, k, v, e, put_dq, put_kv)


def attend_back(sc, g, o, recip, q, k, v, e):
    length, group = q.shape
    half = length // 2
    return call(
        back_kernel, "attend_back", 0.1, sc, (g, o, recip, q, k, v, e),
        [full((half, group))] * 3
        + [pl.BlockSpec((half, group), lambda t, s: (s[0], 0)), full(k.shape), full(v.shape), ANY],
        [((half, group), bf16), ((3 * QB, group), f32), ((3 * QB, group), f32)],
        [full((half, group)), full((3 * QB, group)), full((3 * QB, group))],
        [pltpu.VMEM(e.shape, bf16), pltpu.SemaphoreType.DMA((group // 128,))],
    )


def finish_kernel(
    sc, g, o, recip, q, k, v, dq_own, dk_own, dv_own, pt, lines, order, e_hbm,
    keep, send, gq, e, ksum, vsum, sems,
):
    h, p = sc[0], sc[1]
    width = pt.shape[1]
    mid = width // 2
    length, group = ksum.shape
    half = length // 2
    pairs = group // 128
    loads = [pltpu.make_async_copy(e_hbm.at[t], e.at[t], sems.at[t]) for t in range(pairs)]
    for load in loads:
        load.start()
    own = pl.ds(pl.multiple_of(half * h, half), half)
    window = pl.ds(pl.multiple_of(QB * h, QB), 3 * QB)
    gq[own, 0:group] = dq_own[...]
    for total, part in ((ksum, dk_own), (vsum, dv_own)):
        total[...] = jnp.zeros_like(total)
        total[window, :] = part[...]

    def put_dq(qs, cols, value):
        gq[pl.ds(pl.multiple_of(half * p + qs, QB), QB), cols] = value

    def put_kv(number, loc, ks, count, cols, dk_part, dv_part):
        ksum[pl.ds(ks, count), cols] += dk_part
        vsum[pl.ds(ks, count), cols] += dv_part

    for t in range(pairs):
        loads[t].wait()
        back_pair(p, t, g, o, recip, q, k, v, e, put_dq, put_kv)
    gq[:, group : 2 * group] = ksum[...].astype(bf16)
    gq[:, 2 * group :] = vsum[...].astype(bf16)
    grads = gq[...]
    grad = dot(pt[...], grads, TN).astype(bf16)
    keep[:, : 3 * group] = grad[:mid]
    send[:, : 3 * group] = grad[mid:]
    sums = jnp.sum(grads.astype(f32), axis=0, keepdims=True)
    sums = jnp.concatenate([sums[:, :group], sums[:, 2 * group :]], axis=1).astype(bf16)
    sums = dot(jnp.broadcast_to(sums, (16, 2 * group)), order[...], NN)
    both = lines[...] + jnp.concatenate(
        [g[half + 32 : half + 48, :], g[half + 48 : half + 64, :]], axis=1
    ).astype(f32)
    both = jnp.where(lax.broadcasted_iota(i32, (16, width), 0) == 15, sums, both).astype(bf16)
    eye = onehot(
        lax.broadcasted_iota(i32, (16, 128), 0) == lax.broadcasted_iota(i32, (16, 128), 1)
    )
    extra = dot(both, eye, TN).astype(bf16)
    keep[:, 3 * group :] = extra[:mid]
    send[:, 3 * group :] = extra[mid:]

def finish(sc, g, o, recip, q, k, v, parts, pt, lines, order, e):
    length, group = q.shape
    half, width = length // 2, pt.shape[1]
    wide = (width // 2, 3 * group + 128)
    args = (g, o, recip, q, k, v, *parts, pt, lines, order, e)
    specs = [full(x.shape) for x in args[:-1]] + [ANY]
    specs[3] = pl.BlockSpec((half, group), lambda t, s: (s[1], 0))
    return call(
        finish_kernel, "finish", 0.1, sc, args, specs,
        [(wide, bf16), (wide, bf16), ((length, 3 * group), bf16)],
        [full(wide), full(wide), full((length, 3 * group))],
        [
            pltpu.VMEM(e.shape, bf16),
            pltpu.VMEM((length, group), f32),
            pltpu.VMEM((length, group), f32),
            pltpu.SemaphoreType.DMA((group // 128,)),
        ],
    )


def input_grad_kernel(sc, idx, gq, w, g1b, hid_other, hid_own, terms):
    h, p = sc[0], sc[1]
    half, length = g1b.shape[0], gq.shape[0]
    for i in range(2):
        rows = slice(i * half, (i + 1) * half)
        mine = jnp.where(h == i, 1.0, 0.0)
        part = dot(gq[rows, :], w[...], NT) + mine * g1b[...].astype(f32)
        terms[rows, :] = part.astype(bf16)
    spot = lax.broadcasted_iota(i32, (half, length), 0)
    hid_other[...] = dot(onehot(spot + half * p == idx[...]), terms[...], NN).astype(bf16)
    hid_own[...] = dot(onehot(spot + half * h == idx[...]), terms[...], NN).astype(bf16)


def input_grad(sc, idx, gq, w, g1b):
    half, width = g1b.shape
    args = (idx, gq, w, g1b)
    return call(
        input_grad_kernel, "input_grad", 0.1, sc, args, [full(x.shape) for x in args],
        [((half, width), bf16)] * 2, [full((half, width))] * 2,
        [pltpu.VMEM((2 * half, width), bf16)],
    )


def ordered_kernel(per, sc, tabs, packed, out, order):
    order[...] = order_matrix(sc, tabs, packed.shape[1], per)
    out[...] = dot(packed[...], order[...], NN).astype(bf16)


def ordered(per, sc, tabs, packed):
    width = packed.shape[1]
    return call(
        functools.partial(ordered_kernel, per), "ordered", ORDERED, sc, (tabs, packed),
        [full(tabs.shape), full(packed.shape)],
        [(packed.shape, bf16), ((width, width), bf16)],
        [full(packed.shape), full((width, width))],
        [],
    )


def weight_copies(sc, up_own, dn_own, quads, wup, wdn, sem_up, sem_dn):
    hid = wup.shape[2]
    width, blk, steps = wup.shape[1], hid // 4, hid // HB
    ups, dns = [], []
    for j in range(steps):
        cols = pl.ds(j * HB, HB)
        ups.append(pltpu.make_async_copy(up_own.at[:, cols], wup.at[0, :, cols], sem_up.at[j]))
        dns.append(pltpu.make_async_copy(dn_own.at[cols, :], wdn.at[0, cols, :], sem_dn.at[j]))
    for r, (a_ref, b_ref) in enumerate(quads):
        place = sc[2] ^ r
        cols = pl.ds(pl.multiple_of(blk * place, 128), blk)
        ups.append(
            pltpu.make_async_copy(
                a_ref.at[pl.ds(0, width), :], wup.at[1, :, cols], sem_up.at[steps + r]
            )
        )
        rows = pl.ds(pl.multiple_of(blk * (sc[4] ^ r), 16), blk)
        dns.append(pltpu.make_async_copy(b_ref, wdn.at[1, rows, :], sem_dn.at[steps + r]))
    return ups, dns


def await_weights(j, steps, copies):
    if j < steps:
        copies[j].wait()
    elif j == steps:
        for copy in copies[steps:]:
            copy.wait()


def block_of(j, steps):
    return j // steps, slice((j % steps) * HB, (j % steps + 1) * HB)


def forward_kernel(
    sc, lens, packed, mixed_own, mixed_other, cot, ow_own, vectors, up_bias, pool, order,
    up_own, dn_own, a0, a1, a2, a3, b0, b1, b2, b3,
    out, pooled, grad2, smalls, ow_out, nrel_out, slope_out, scaled1_out, inv1_out, dn_keep, dn_send,
    wup, wdn, ow_other, ub, act, slope, scaled1, nrel, dnk, dns,
    sem_up, sem_dn, sem_ow, sem_ub, sem_out,
):
    width, hid = wup.shape[1], wup.shape[2]
    mid, blk, steps = width // 2, hid // 4, hid // HB
    piece = ow_own.shape[0] // 4
    out_bias, attn_gain, attn_shift, down_bias, ffn_gain, ffn_shift = (
        vectors[i : i + 1, :] for i in range(6)
    )
    quads = ((a0, b0), (a1, b1), (a2, b2), (a3, b3))
    small_in = []
    for r, (a_ref, _) in enumerate(quads):
        place = sc[2] ^ r
        rows = pl.ds(pl.multiple_of(piece * place, 16), piece)
        for c in range(2):
            small_in.append(
                pltpu.make_async_copy(
                    a_ref.at[pl.ds(width + c * piece, piece), :],
                    ow_other.at[rows, pl.ds(c * blk, blk)],
                    sem_ow.at[2 * r + c],
                )
            )
        small_in.append(
            pltpu.make_async_copy(
                a_ref.at[pl.ds(width + 2 * piece, 16), :],
                ub.at[:, pl.ds(pl.multiple_of(blk * place, 128), blk)],
                sem_ub.at[r],
            )
        )
    ups, dns_in = weight_copies(sc, up_own, dn_own, quads, wup, wdn, sem_up, sem_dn)
    for copy in small_in:
        copy.start()
    for j in range(steps):
        ups[j].start()
        dns_in[j].start()
    for copy in ups[steps:] + dns_in[steps:]:
        copy.start()
    copies = []

    def store(source, target):
        copies.append(pltpu.make_async_copy(source, target, sem_out.at[len(copies)]))
        copies[-1].start()

    for copy in small_in:
        copy.wait()
    store(ow_other, ow_out)
    resid = (
        packed[...].astype(f32)
        + dot(mixed_own[...], ow_own[...], NN)
        + dot(mixed_other[...], ow_other[...], NN)
        + out_bias
    )
    center = resid - jnp.mean(resid, axis=-1, keepdims=True)
    inv1 = lax.rsqrt(jnp.mean(center * center, axis=-1, keepdims=True) + EPS)
    inv1_out[...] = jnp.broadcast_to(inv1, inv1_out.shape)
    norm = center * inv1
    scaled1[...] = norm
    store(scaled1, scaled1_out)
    normed1 = norm * attn_gain + attn_shift
    low = normed1.astype(bf16)
    nrel[...] = dot(low, order[...], NN).astype(bf16)
    store(nrel, nrel_out)
    total = normed1 + down_bias

    def pre_act(j):
        side, cols = block_of(j, steps)
        await_weights(j, steps, ups)
        if side == 0:
            bias = up_bias[:, cols]
        else:
            three = ub[:, cols].astype(f32)
            bias = three[0:1] + three[1:2] + three[2:3]
        return dot(low, wup[side, :, cols], NN) + bias

    for j in range(2 * steps):
        side, cols = block_of(j, steps)
        here = pre_act(j)
        value, deriv = gelu_pair(here)
        value = value.astype(bf16)
        act[j] = value
        slope[j] = deriv.astype(bf16)
        store(slope.at[j], slope_out.at[j])
        await_weights(j, steps, dns_in)
        total = total + dot(value, wdn[side, cols, :], NN)
    center = total - jnp.mean(total, axis=-1, keepdims=True)
    inv2 = lax.rsqrt(jnp.mean(center * center, axis=-1, keepdims=True) + EPS)
    scaled2 = center * inv2
    result = scaled2 * ffn_gain + ffn_shift
    high = result.astype(bf16)
    out[...] = high
    rest = (result - high.astype(f32)).astype(bf16)
    sums = dot(pool[...], high, NN) + dot(pool[...], rest, NN)
    row = lax.broadcasted_iota(i32, (16, 1), 0)
    scale = jnp.zeros((16, 1), f32)
    for c in range(lens.shape[1]):
        scale = jnp.where(row == c, 1.0 / lens[0, c].astype(f32), scale)
    pooled[...] = sums * scale

    grad = cot[...].astype(f32)
    smalls[1:2, :] = jnp.sum(grad * scaled2, axis=0, keepdims=True)
    smalls[2:3, :] = jnp.sum(grad, axis=0, keepdims=True)
    smalls[3:8, :] = jnp.zeros((5, width), f32)
    grad = grad * ffn_gain
    grad = inv2 * (
        grad
        - jnp.mean(grad, axis=-1, keepdims=True)
        - scaled2 * jnp.mean(grad * scaled2, axis=-1, keepdims=True)
    )
    smalls[0:1, :] = jnp.sum(grad, axis=0, keepdims=True)
    grad2[...] = grad
    grel = dot(grad.astype(bf16), order[...], NN).astype(bf16)
    for j in range(2 * steps):
        grad = dot(grel, act[j], TN).astype(bf16)
        both = slice(j * HB, (j + 1) * HB)
        dns[:, both] = grad[mid:]
        store(dns.at[:, both], dn_send.at[:, both])
        dnk[:, both] = grad[:mid]
        store(dnk.at[:, both], dn_keep.at[:, both])
    for copy in copies:
        copy.wait()


def forward(sc, lens, packed, mixed_own, mixed_other, cot, ow, vectors, up_bias, pool, order, up, dn, quads):
    half = packed.shape[0] // 2
    width, hid = up.shape
    group = ow.shape[0]
    steps, mid = hid // HB, width // 2
    blocks = (2 * steps, half, HB)
    outs = [
        ((half, width), bf16),
        ((16, width), f32),
        ((half, width), f32),
        ((8, width), f32),
        ((group, width), bf16),
        ((half, width), bf16),
        (blocks, bf16),
        ((half, width), f32),
        ((half, 128), f32),
        ((mid, 2 * hid), bf16),
        ((mid, 2 * hid), bf16),
    ]
    args = (
        lens, packed, mixed_own, mixed_other, cot, ow, vectors, up_bias, pool, order, up, dn,
        *[a for a, _ in quads], *[b for _, b in quads],
    )
    return call(
        forward_kernel, "forward", 25, sc, args,
        [
            pl.BlockSpec(memory_space=pltpu.SMEM),
            pl.BlockSpec((half, width), lambda t, s: (s[0], 0)),
            full((half, group)),
            full((half, group)),
            full((half, width)),
            full((group, width)),
            full(vectors.shape),
            full((1, hid)),
            pl.BlockSpec((16, half), lambda t, s: (0, s[0])),
            full((width, width)),
        ]
        + [ANY] * 10,
        outs,
        [full(x) for x, _ in outs[:4]] + [ANY] * 4 + [full((half, 128))] + [ANY] * 2,
        [
            pltpu.VMEM((2, width, hid), bf16),
            pltpu.VMEM((2, hid, width), bf16),
            pltpu.VMEM((group, width), bf16),
            pltpu.VMEM((16, hid), bf16),
            pltpu.VMEM(blocks, bf16),
            pltpu.VMEM(blocks, bf16),
            pltpu.VMEM((half, width), f32),
            pltpu.VMEM((half, width), bf16),
            pltpu.VMEM((mid, 2 * hid), bf16),
            pltpu.VMEM((mid, 2 * hid), bf16),
            pltpu.SemaphoreType.DMA((steps + 4,)),
            pltpu.SemaphoreType.DMA((steps + 4,)),
            pltpu.SemaphoreType.DMA((8,)),
            pltpu.SemaphoreType.DMA((4,)),
            pltpu.SemaphoreType.DMA((6 * steps + 3,)),
        ],
    )


def backward_kernel(
    per, sc, tabs, grad2, pooled, smalls2, ow_own, ow_other, inv1, vectors, order, mixed_own,
    mixed_other, nrel, scaled1, slope_in, up_own, dn_own, a0, a1, a2, a3, b0, b1, b2, b3,
    send, gm_own, g1b, lines, up_keep, up_send,
    wup, wdn, slope, upk, ups, smalls, bias_sums, sem_up, sem_dn, sem_in, sem_out,
):
    width, hid = wup.shape[1], wup.shape[2]
    mid, steps = width // 2, hid // HB
    tokens, group = mixed_own.shape
    attn_gain = vectors[1:2, :]
    quads = ((a0, b0), (a1, b1), (a2, b2), (a3, b3))
    ups_in, dns_in = weight_copies(sc, up_own, dn_own, quads, wup, wdn, sem_up, sem_dn)
    slopes = [
        pltpu.make_async_copy(slope_in.at[j], slope.at[j], sem_in.at[j]) for j in range(2 * steps)
    ]
    for j in range(steps):
        dns_in[j].start()
        slopes[j].start()
        ups_in[j].start()
    for copy in dns_in[steps:] + slopes[steps:] + ups_in[steps:]:
        copy.start()
    copies = []

    def store(source, target):
        copies.append(pltpu.make_async_copy(source, target, sem_out.at[len(copies)]))
        copies[-1].start()

    low = grad2[...].astype(bf16)
    total = grad2[...]
    bias_sums[...] = jnp.zeros_like(bias_sums)

    def grad_act(j):
        side, cols = block_of(j, steps)
        await_weights(j, steps, dns_in)
        return dot(low, wdn[side, cols, :], NT)

    for j in range(2 * steps):
        side, cols = block_of(j, steps)
        here = grad_act(j)
        slopes[j].wait()
        pre = (here * slope[j].astype(f32)).astype(bf16)
        await_weights(j, steps, ups_in)
        total = total + dot(pre, wup[side, :, cols], NT)
        bias_sums[side : side + 1, cols] = jnp.sum(pre.astype(f32), axis=0, keepdims=True)
        grad = dot(nrel[...], pre, TN).astype(bf16)
        upk[side, :, cols] = grad[:mid]
        ups[side, :, cols] = grad[mid:]
        store(upk.at[side, :, cols], up_keep.at[side, :, cols])
        store(ups.at[side, :, cols], up_send.at[side, :, cols])
    norm = scaled1[...]
    smalls[1:2, :] = jnp.sum(total * norm, axis=0, keepdims=True)
    smalls[2:3, :] = jnp.sum(total, axis=0, keepdims=True)
    smalls[3:6, :] = smalls2[0:3, :]
    smalls[6:16, :] = jnp.zeros((10, width), f32)
    grad = total * attn_gain
    grad = inv1[:, 0:1] * (
        grad
        - jnp.mean(grad, axis=-1, keepdims=True)
        - norm * jnp.mean(grad * norm, axis=-1, keepdims=True)
    )
    smalls[0:1, :] = jnp.sum(grad, axis=0, keepdims=True)
    low = grad.astype(bf16)
    g1b[...] = low
    send[0:tokens, :] = dot(low, ow_other[...], NT).astype(bf16)
    gm_own[...] = dot(low, ow_own[...], NT).astype(bf16)
    sums = pooled[...].astype(bf16)
    send[tokens : tokens + 16, :] = sums[:, :group]
    send[tokens + 16 : tokens + 32, :] = sums[:, group:]

    low = dot(low, order[...], NN).astype(bf16)
    for side, mixed in enumerate((mixed_own, mixed_other)):
        grad = dot(low, mixed[...], TN).astype(bf16)
        upk[side, :, hid:] = grad[:mid]
        ups[side, :, hid:] = grad[mid:]
        tail = slice(hid, hid + group)
        store(upk.at[side, :, tail], up_keep.at[side, :, tail])
        store(ups.at[side, :, tail], up_send.at[side, :, tail])
    rows = dot(smalls[...].astype(bf16), order[...], NN)
    pieces = []
    source = (tabs[0:1, :] ^ sc[3]) * (2 * per) + tabs[1:2, :]
    for part in range(hid // width):
        spread = onehot(source + part * per == lax.broadcasted_iota(i32, (hid, width), 0))
        pieces.append(dot(bias_sums[...].astype(bf16), spread, NN))
    lines[...] = jnp.concatenate([rows[:6]] + [x[0:1] for x in pieces] + [rows[8:]], axis=0)
    other = jnp.concatenate(
        [rows[:6]] + [x[1:2] for x in pieces] + [rows[8:]], axis=0
    ).astype(bf16)
    send[tokens + 32 : tokens + 48, :] = other[:, :group]
    send[tokens + 48 : tokens + 64, :] = other[:, group:]
    for copy in copies:
        copy.wait()


def backward(
    per, sc, tabs, grad2, pooled, smalls, ow, ow_other, inv1, vectors, order, mixed_own, mixed_other,
    nrel, scaled1, slope, up, dn, quads,
):
    half, width = grad2.shape
    hid = up.shape[1]
    group = ow.shape[0]
    steps, mid = hid // HB, width // 2
    wide = (2, mid, hid + group)
    outs = [
        ((half + 64, group), bf16),
        ((half, group), bf16),
        ((half, width), bf16),
        ((16, width), f32),
        (wide, bf16),
        (wide, bf16),
    ]
    args = (
        tabs, grad2, pooled, smalls, ow, ow_other, inv1, vectors, order, mixed_own, mixed_other,
        nrel, scaled1, slope, up, dn, *[a for a, _ in quads], *[b for _, b in quads],
    )
    return call(
        functools.partial(backward_kernel, per), "backward", 18, sc, args,
        [full(x.shape) for x in args[:13]] + [ANY] * 11,
        outs,
        [full(x) for x, _ in outs[:4]] + [ANY] * 2,
        [
            pltpu.VMEM((2, width, hid), bf16),
            pltpu.VMEM((2, hid, width), bf16),
            pltpu.VMEM(slope.shape, bf16),
            pltpu.VMEM(wide, bf16),
            pltpu.VMEM(wide, bf16),
            pltpu.VMEM((16, width), f32),
            pltpu.VMEM((16, hid), f32),
            pltpu.SemaphoreType.DMA((steps + 4,)),
            pltpu.SemaphoreType.DMA((steps + 4,)),
            pltpu.SemaphoreType.DMA((2 * steps,)),
            pltpu.SemaphoreType.DMA((4 * steps + 4,)),
        ],
    )


def chip_sums(sc, name, pairs, views):
    dims = [d for d, _, _ in views]
    count = 2 * len(pairs)

    def kernel(sc, *refs):
        ins, outs = refs[:count], refs[count : count + len(dims)]
        loads, sems = refs[count + len(dims) : -1], refs[-1]
        copies = []
        for _, pair, view in views:
            for source in ins[2 * pair : 2 * pair + 2]:
                copies.append(
                    pltpu.make_async_copy(
                        source.at[view], loads[len(copies)], sems.at[len(copies)]
                    )
                )
                copies[-1].start()
        for number, out in enumerate(outs):
            copies[2 * number].wait()
            copies[2 * number + 1].wait()
            one, two = loads[2 * number], loads[2 * number + 1]
            out[...] = (one[...].astype(f32) + two[...].astype(f32)).astype(bf16)

    return call(
        kernel, name, ORDERED, sc, [x for pair in pairs for x in pair], [ANY] * count,
        [(d, bf16) for d in dims],
        [full(d) for d in dims],
        [pltpu.VMEM(d, bf16) for d in dims for _ in range(2)]
        + [pltpu.SemaphoreType.DMA((2 * len(dims),))],
    )


def swap(value, axis, bit):
    count = lax.axis_size(axis)
    return lax.ppermute(value, axis, [(i, i ^ (1 << bit)) for i in range(count)])


def pin(*values):
    return lax.optimization_barrier(values)


def add_low(left, right):
    return (left.astype(f32) + right.astype(f32)).astype(bf16)


def body(
    hidden,
    source_index,
    crop_lengths,
    deleted,
    qkv_weight,
    qv_bias,
    out_weight,
    out_bias,
    attn_gain,
    attn_shift,
    up_weight,
    up_bias,
    down_weight,
    down_bias,
    ffn_gain,
    ffn_shift,
    cotangent,
):
    length, width = hidden.shape
    crops = crop_lengths.shape[1]
    group = out_weight.shape[0]
    hid = up_weight.shape[1]
    half = length // 2
    n_dp, n_rep = lax.axis_size("dp"), lax.axis_size("rep")
    dp_bits, rep_bits = n_dp.bit_length() - 1, n_rep.bit_length() - 1
    shards = n_dp * n_rep
    per = width // shards
    h, dp = lax.axis_index("head"), lax.axis_index("dp")
    rep_index = lax.axis_index("rep")
    me = dp * n_rep + rep_index
    sc = jnp.stack([h, 1 - h, dp & 3, me, (dp & 1) + 2 * (rep_index & 1)]).astype(i32)

    stages = [("dp", b) for b in range(dp_bits)] + [("rep", b) for b in range(rep_bits)]
    block = np.zeros(shards, np.int32)
    for number, (axis, bit) in enumerate(stages):
        value = (np.arange(shards) >> (len(stages) - 1 - number)) & 1
        block |= (value << (bit + (rep_bits if axis == "dp" else 0))).astype(np.int32)
    row = np.arange(width)
    tabs = np.zeros((8, width), np.int32)
    tabs[0] = block[row // per]
    tabs[1] = row % per
    tabs = jnp.asarray(tabs)

    first, second = bundle(sc, up_bias, up_weight, down_weight, out_weight)
    first = swap(first, "head", 0)
    second = swap(second, "head", 0)
    packed, q, k, v, e_other, o_other, recip_other, segrow, code, pool = prepare(
        sc, crop_lengths, hidden, source_index, deleted, qkv_weight, qv_bias
    )
    mixed_recv = swap(o_other, "head", 0)
    first, o_other = pin(first, o_other)
    first_y = swap(first, "dp", 1)
    q_late, first = pin(q, first)
    e_own, o_own, recip_own = attend(sc, q_late, k, v, segrow, code)
    second, o_own = pin(second, o_own)
    second_y = swap(second, "rep", 0)
    packed_late, mixed_recv, second = pin(packed, mixed_recv, second)
    pt, order = ordered(per, sc, tabs, packed_late)
    first, first_y, second_y, pt = pin(first, first_y, second_y, pt)
    first_c, first_cy = swap(first, "dp", 0), swap(first_y, "dp", 0)
    second_c, second_cy = swap(second, "dp", 0), swap(second_y, "dp", 0)
    quads = [(first, second), (first_c, second_c), (first_y, second_y), (first_cy, second_cy)]
    vectors = jnp.stack(
        [out_bias, attn_gain, attn_shift, down_bias, ffn_gain, ffn_shift, ffn_shift, ffn_shift]
    )
    (
        output, pooled, grad2, smalls, ow_other, nrel, slope, scaled1, inv1, dn_keep, dn_send
    ) = forward(
        sc, crop_lengths, packed, o_own, mixed_recv, cotangent, out_weight, vectors, up_bias, pool,
        order, up_weight, down_weight, quads,
    )
    send, gm_own, g1b, lines, up_keep, up_send = backward(
        per, sc, tabs, grad2, pooled, smalls, out_weight, ow_other, inv1, vectors, order, o_own,
        mixed_recv, nrel, scaled1, slope, up_weight, down_weight, quads,
    )
    part, cut = width // 4, 1152
    recv = swap(send, "head", 0)
    dn_recv, gm_own = pin(swap(dn_send, "dp", 0), gm_own)
    across, few = n_dp // 2, n_rep // 2 * per
    low_tall = (across, 2, few, 2 * hid)
    rest = hid + group - cut
    (dn_next,) = chip_sums(
        sc, "down_sums", [(dn_keep.reshape(low_tall), dn_recv.reshape(low_tall))],
        [((across, few, 2 * hid), 0, (slice(None), 1))],
    )
    gm_own, dn_next = pin(gm_own, dn_next)
    up_recv, dn_next = pin(swap(up_send, "dp", 0), dn_next)
    a_next, b_next = chip_sums(
        sc, "up_sums", [(up_keep, up_recv)],
        [
            ((2 * part, cut), 0, (1, slice(None), pl.ds(0, cut))),
            ((2, part, rest), 0, (slice(None), pl.ds(part, part), pl.ds(cut, rest))),
        ],
    )
    gm_own, a_next, b_next = pin(gm_own, a_next, b_next)
    dq_own, dk_own, dv_own = attend_back(sc, gm_own, o_own, recip_own, q, k, v, e_own)
    recv, dq_own = pin(recv, dq_own)
    qkv_keep, qkv_send, gq = finish(
        sc, recv, o_other, recip_other, q, k, v, (dq_own, dk_own, dv_own), pt, lines, order, e_other
    )
    hidden_other, hidden_own = input_grad(sc, source_index, gq, qkv_weight, g1b)

    last = [hidden_own]

    def arrive(value):
        return pin(value, last[0])[0].astype(f32)

    def keep_low(value):
        last[0] = value.astype(bf16)
        return last[0]

    def low_half(value, axis, bit):
        rows = value.shape[0] // 2
        return keep_low(value[:rows].astype(f32) + arrive(swap(value[rows:], axis, bit)))

    def low_rest(value, axis, bit, dim):
        keep, out = jnp.split(value, 2, axis=dim)
        return keep_low(keep.astype(f32) + arrive(swap(out, axis, bit)))

    def three(keep, recv, late):
        return keep_low(keep.astype(f32) + recv.astype(f32) + arrive(late))

    later = stages[1:]
    dp_later = [x for x in later if x[0] == "dp"]
    rep_all = [x for x in later if x[0] == "rep"]
    down_swap = swap(dn_next, *rep_all[0])
    a_swap = swap(a_next, "head", 0)
    b_swap = swap(b_next, *later[0])
    qkv_swap = swap(qkv_send, "dp", 0)
    down = three(dn_keep.reshape(low_tall)[:, 0], dn_recv.reshape(low_tall)[:, 0], down_swap)
    up_b = three(up_keep[:, :part, cut:], up_recv[:, :part, cut:], b_swap)
    up_a = three(up_keep[0, :, :cut], up_recv[0, :, :cut], a_swap)
    qkv = keep_low(qkv_keep.astype(f32) + arrive(qkv_swap))
    qkv = qkv.reshape(across, n_rep, per, qkv.shape[1])
    qkv = low_rest(qkv, *rep_all[0], 1)
    up_a = low_half(up_a, *later[0])
    up_b = keep_low(up_b[0].astype(f32) + arrive(swap(up_b[1], "head", 0)))
    down = keep_low(down[:, :, :hid].astype(f32) + arrive(swap(down[:, :, hid:], "head", 0)))
    hidden_recv = swap(pin(hidden_other, last[0])[0], "head", 0)
    for axis, bit in rep_all[1:]:
        qkv = low_rest(qkv, axis, bit, 1)
    for axis, bit in later[1 : len(dp_later) + 1]:
        up_a = low_half(up_a, axis, bit)
        up_b = low_half(up_b, axis, bit)
    up = jnp.concatenate([up_a, up_b], axis=1)
    for axis, bit in dp_later:
        down = low_half(down, axis, bit)
    down = down[0]
    for axis, bit in rep_all[1:-1]:
        down = low_half(down, axis, bit)
        up = low_half(up, axis, bit)
    for axis, bit in dp_later[:-1]:
        qkv = low_rest(qkv, axis, bit, 0)
    axis, bit = dp_later[-1]
    keep, out = qkv[0, 0], arrive(swap(qkv[1:], axis, bit))[0, 0]
    wide = 3 * group
    qkv_grad = keep[:, :wide].astype(f32) + out[:, :wide]
    extra = (keep[:, wide:].astype(f32) + out[:, wide:]).T
    small = lax.dynamic_slice_in_dim(extra[:6], h * (per // 2), per // 2, 1)
    last[0] = qkv_grad
    axis, bit = later[-1]
    keep, out = up[:per], arrive(swap(up[per:], axis, bit))
    up_grad = keep[:, :hid].astype(f32) + out[:, :hid]
    out_grad = keep[:, hid:].astype(f32) + out[:, hid:]
    last[0] = up_grad
    down = down[:per].astype(f32) + arrive(swap(down[per:], axis, bit))
    last[0] = down
    grad_hidden = hidden_own.astype(f32) + arrive(hidden_recv)

    pooled_other = recv[half:].astype(f32)
    pooled_other = jnp.concatenate([pooled_other[:crops], pooled_other[16 : 16 + crops]], axis=1)
    return (
        output,
        pooled[:crops] + pooled_other,
        grad_hidden,
        qkv_grad,
        extra[15:16],
        out_grad.T,
        small[0],
        small[1],
        small[2],
        up_grad,
        extra[6 : 6 + hid // width].reshape(1, hid // shards),
        down.T,
        small[3],
        small[4],
        small[5],
    )


def solution(mesh):
    rows = P(("dp", "rep"), None)
    every = P(("dp", "rep", "head"), None)
    vector = P(("dp", "rep", "head"))
    return jax.shard_map(
        body,
        mesh=mesh,
        in_specs=(
            rows,
            rows,
            rows,
            rows,
            P(None, "head"),
            P("head", None),
            P("head", None),
            P(),
            P(),
            P(),
            P(None, "head"),
            P("head", None),
            P("head", None),
            P(),
            P(),
            P(),
            every,
        ),
        out_specs=(
            every,
            rows,
            every,
            P(("dp", "rep"), "head"),
            P("head", ("dp", "rep")),
            P("head", ("dp", "rep")),
            vector,
            vector,
            vector,
            P(("dp", "rep"), "head"),
            P("head", ("dp", "rep")),
            P("head", ("dp", "rep")),
            vector,
            vector,
            vector,
        ),
        check_vma=False,
    )
```
